32 devices in a mesh: dp: 4 (over z), seq: 2 (over core), head: 4 (over y, x).
Axes of the slice: x: 2, y: 2, z: 4, core: 2. Of those that a mesh axis runs over, the one named last changes fastest.
Arguments:
- tokens: bfloat16 [2, 8192, 768], P(None, ('dp', 'seq', 'head')), may hold values from -6 to 6
- lengths: int32 [2, 4, 4], P(None, 'dp'), may hold values from 64 to 1792, as said below
- ln_gain: float32 [768], replicated, may hold values from 0.5 to 1.5
- w_up: bfloat16 [768, 3072], replicated, may hold values from -0.21875 to 0.21875
- conv_w: float32 [4, 1536], replicated, may hold values from -3 to 3
- conv_b: float32 [1536], replicated, may hold values from -3 to 3
- w_q: bfloat16 [384, 4, 4], replicated, may hold values from -3 to 3
- w_k: bfloat16 [384, 4, 4], replicated, may hold values from -3 to 3
- w_v: bfloat16 [384, 4, 4], replicated, may hold values from -3 to 3
- gate_w: bfloat16 [4608, 8], replicated, may hold values from -0.09375 to 0.09375
- i_bias: float32 [4], replicated, may hold values from -9 to -6
- f_bias: float32 [4], replicated, may hold values from 2.5 to 9
- gn_gain: float32 [1536], replicated, may hold values from 0.5 to 1.5
- skip: float32 [1536], replicated, may hold values from 0.1 to 1.9
- w_down: bfloat16 [1536, 768], replicated, may hold values from -0.3125 to 0.3125
- cotangent: bfloat16 [2, 8192, 768], P(None, ('dp', 'seq', 'head')), may hold values from -6 to 6
Outputs:
- block_out: bfloat16 [2, 8192, 768], P(None, ('dp', 'seq', 'head'))
- d_tokens: bfloat16 [2, 8192, 768], P(None, ('dp', 'seq', 'head'))
- g_ln_gain: float32 [768], replicated
- g_w_up: float32 [768, 3072], P(None, ('dp', 'seq', 'head'))
- g_conv_w: float32 [4, 1536], replicated
- g_conv_b: float32 [1536], replicated
- g_w_q: float32 [384, 4, 4], replicated
- g_w_k: float32 [384, 4, 4], replicated
- g_w_v: float32 [384, 4, 4], replicated
- g_gate_w: float32 [4608, 8], replicated
- g_i_bias: float32 [4], replicated
- g_f_bias: float32 [4], replicated
- g_gn_gain: float32 [1536], replicated
- g_skip: float32 [1536], replicated
- g_w_down: float32 [1536, 768], P(('dp', 'seq', 'head'))
The draws below stay inside these ranges and needn't reach their ends.
Inputs may be any that keep to these rules, and one draw needn't show every extreme that they name: lengths[m, g] are the lengths of the 4 sequences packed in this order from the start of stream g of micro-batch m; they sum to at most 2048, and the stream's remaining tokens are padding.
All inputs are finite; a program needn't handle non-finite values.
Results may differ from the reference program's by a relative error of at most 0.005.
The reference program's roundings to bfloat16 on the way count: a program that leaves them out, or rounds other values in their place, can miss the bound.
Values may be sent and summed in bfloat16 or wider, within the bound.
No kernel may reach another device: no remote copies, remote signals or barrier semaphores. Data moves between devices by JAX's collectives and lax.ppermute only.
A program may use at most 256 MiB of HBM per device.

```python
import jax
import jax.numpy as jnp
from jax import lax

D = 768
INNER = 1536
NH = 4
DH = 384
KCONV = 4
QKVB = 4
NBLK = 384
TOK_DEV = 256
MICRO = 2
NSEQ = 4
MINLEN = 64
GROUP = 2048
TOKENS = 8192
N_DP = 4
N_SEQ = 2


def draw_lengths(key, part):
    key = jax.random.fold_in(key, 11)
    subkeys = jax.random.split(key, 8)
    grid_shape = (MICRO, N_DP)
    first_len = jax.random.randint(subkeys[0], grid_shape, MINLEN, TOK_DEV - 2 * MINLEN + 1)
    rest_len = TOK_DEV - first_len
    third_len = jax.random.randint(subkeys[1], grid_shape, MINLEN, rest_len - MINLEN + 1)
    spare_room = rest_len - third_len - MINLEN
    pad_len = jax.random.randint(subkeys[2], grid_shape, 0, spare_room + 1)
    fourth_len = rest_len - third_len - pad_len
    long_len = jnp.full(grid_shape, GROUP - TOK_DEV, jnp.int32)
    spanning = jnp.stack([first_len, long_len, third_len, fourth_len], axis=-1)
    lead_len = min(GROUP // N_SEQ, GROUP - 2 * TOK_DEV)
    room_blocks = (GROUP - lead_len) // TOK_DEV
    step_count = jax.random.randint(subkeys[3], grid_shape, 1, room_blocks)
    back_off = jax.random.randint(subkeys[4], grid_shape, 0, 4)
    second_len = step_count * TOK_DEV - back_off
    remain = GROUP - lead_len - second_len
    third_cut = jax.random.randint(subkeys[5], grid_shape, MINLEN, remain - MINLEN + 1)
    pad_cut = jax.random.randint(subkeys[6], grid_shape, 0, remain - third_cut - MINLEN + 1)
    fourth_cut = remain - third_cut - pad_cut
    aligned = jnp.stack([jnp.full(grid_shape, lead_len, jnp.int32), second_len, third_cut, fourth_cut], axis=-1)
    coin_flip = jax.random.randint(subkeys[7], (), 0, 2)
    parity = (jnp.arange(MICRO)[:, None] + jnp.arange(N_DP)[None, :] + coin_flip) % 2
    return jnp.where((parity == 0)[:, :, None], spanning, aligned).astype(jnp.int32)


def draw_f_bias(key, part):
    key = jax.random.fold_in(key, 23)
    order_key, slow_key, fast_key = jax.random.split(key, 3)
    ranking = jax.random.permutation(order_key, NH)
    slow_bias = jax.random.uniform(slow_key, (NH,), jnp.float32, 7.0, 9.0)
    fast_bias = jax.random.uniform(fast_key, (NH,), jnp.float32, 2.5, 3.5)
    kept_heads = NH // 2
    return jnp.where(ranking < kept_heads, slow_bias, fast_bias)


def shard_levels(rng, extent, cuts, low, high):
    factor_of, own = 1.0, jax.random.fold_in(rng, 6)
    for dim, blocks in cuts:
        draws = jnp.exp(jax.random.uniform(jax.random.fold_in(own, dim), (blocks,), jnp.float32, low / len(cuts), high / len(cuts)))
        factor_of = factor_of * jnp.repeat(draws, extent[dim] // blocks).reshape([-1 if axis == dim else 1 for axis in range(len(extent))])
    return factor_of


def normal_values(key, shape, scale, bound, pieces=(), held_as=jnp.bfloat16):
    entries = scale * jax.random.normal(key, shape, jnp.float32)
    if pieces:
        entries = entries * shard_levels(key, shape, pieces, -0.22, 0.18)
    return jnp.clip(entries, -bound, bound).astype(held_as)


def setup_inputs(seed: int = 0) -> dict:
    key_list = jax.random.split(jax.random.key(seed), 17)
    return {
        "tokens": normal_values(key_list[0], (MICRO, TOKENS, D), 1.0, 6.0, ((1, 32),)),
        "lengths": draw_lengths(jax.random.fold_in(key_list[16], 71), 0),
        "ln_gain": jnp.clip(1.0 + 0.1 * jax.random.normal(key_list[2], (D,), jnp.float32), 0.5, 1.5),
        "w_up": normal_values(key_list[3], (D, 2 * INNER), D ** -0.5, 0.21875),
        "conv_w": normal_values(key_list[4], (KCONV, INNER), 0.5, 3.0, (), jnp.float32),
        "conv_b": normal_values(key_list[5], (INNER,), 0.5, 3.0, (), jnp.float32),
        "w_q": normal_values(key_list[6], (NBLK, QKVB, QKVB), QKVB ** -0.5, 3.0),
        "w_k": normal_values(key_list[7], (NBLK, QKVB, QKVB), QKVB ** -0.5, 3.0),
        "w_v": normal_values(key_list[8], (NBLK, QKVB, QKVB), QKVB ** -0.5, 3.0),
        "gate_w": normal_values(key_list[9], (3 * INNER, 2 * NH), (3 * INNER) ** -0.5, 0.09375),
        "i_bias": jnp.clip(jax.random.uniform(key_list[10], (NH,), jnp.float32, -9.0, -6.0), -9.0, -6.0),
        "f_bias": draw_f_bias(jax.random.fold_in(key_list[16], 71), 0),
        "gn_gain": jnp.clip(1.0 + 0.1 * jax.random.normal(key_list[12], (INNER,), jnp.float32), 0.5, 1.5),
        "skip": jnp.clip(1.0 + 0.18 * jax.random.normal(key_list[13], (INNER,), jnp.float32), 0.1, 1.9),
        "w_down": normal_values(key_list[14], (INNER, D), (INNER // 4) ** -0.5, 0.3125),
        "cotangent": normal_values(key_list[15], (MICRO, TOKENS, D), 1.0, 6.0, ((1, 32),)),
    }


EPS = 1e-05
HIGH = lax.Precision.HIGHEST

@jax.custom_vjp
def low(v):
    return lax.optimization_barrier(v.astype(jnp.bfloat16)).astype(jnp.float32)

@jax.custom_vjp
def low_back(v):
    return v

def low_keep(v):
    return (low(v), None)

def low_pass(kept, grad):
    return (grad,)

def back_keep(v):
    return (v, None)

def back_low(kept, grad):
    return (low(grad),)
low.defvjp(low_keep, low_pass)
low_back.defvjp(back_keep, back_low)

def norm_rows(stream, ln_gain):
    average = lax.optimization_barrier(jnp.mean(stream, axis=-1, keepdims=True))
    centred = stream - average
    variance = lax.optimization_barrier(jnp.mean(centred * centred, axis=-1, keepdims=True))
    return low(centred * lax.rsqrt(variance + EPS) * ln_gain)

def block_mix(values_in, weight):
    blocks, size_in, size_out = weight.shape
    grouped = values_in.reshape(values_in.shape[0], blocks, size_in)
    mapped = jnp.einsum('tbi,bio->tbo', grouped, weight, precision=HIGH)
    return mapped.reshape(values_in.shape[0], blocks * size_out)

def mixer(queries, key_rows, values, gate_pre, seg_all, valid_rows):
    length = seg_all.shape[0]
    factor = DH ** (-0.5)
    log_keep = valid_rows[:, None] * jax.nn.log_sigmoid(gate_pre[:, :, 1])
    weight = valid_rows[:, None] * jnp.exp(gate_pre[:, :, 0])
    cumulative = jnp.cumsum(log_keep, axis=0)
    order_idx = jnp.arange(length)
    allowed = (seg_all[:, None] == seg_all[None, :]) & (order_idx[None, :] <= order_idx[:, None])
    differ = cumulative.T[:, :, None] - cumulative.T[:, None, :]
    decays = jnp.where(allowed[None], jnp.exp(jnp.minimum(differ, 0.0)) * weight.T[:, None, :], 0.0)
    scores = jnp.einsum('thd,shd->hts', queries, key_rows, precision=HIGH) * factor
    hidden = jnp.einsum('hts,shd->thd', scores * decays, values, precision=HIGH)
    average = lax.optimization_barrier(jnp.mean(hidden, axis=-1, keepdims=True))
    centred = hidden - average
    variance = lax.optimization_barrier(jnp.mean(centred * centred, axis=-1, keepdims=True))
    return centred * lax.rsqrt(variance + EPS)

def group_forward(stream, lens_one, ln_gain, w_up, conv_w, conv_b, w_q, w_k, w_v, gate_w, i_bias, f_bias, gn_gain, skip, w_down):
    ends_at = jnp.cumsum(lens_one).astype(jnp.int32)
    positions = jnp.arange(GROUP, dtype=jnp.int32)
    seg_all = lax.optimization_barrier(jnp.sum((positions[:, None] >= ends_at[None, :]).astype(jnp.int32), axis=1)).astype(jnp.int32)
    valid_rows = (seg_all < NSEQ).astype(jnp.float32)
    normed = norm_rows(stream, ln_gain)
    up_proj = low_back(jnp.dot(normed, w_up, precision=HIGH))
    inner_rows = low(up_proj[:, :INNER])
    gate_z = up_proj[:, INNER:]
    conv_sum = jnp.zeros((GROUP, INNER), jnp.float32) + conv_b
    for lagged in range(KCONV):
        shifted = jnp.pad(inner_rows, ((lagged, 0), (0, 0)))[:GROUP]
        seg_shift = jnp.pad(seg_all, (lagged, 0), constant_values=-1)[:GROUP]
        same_seq = (seg_shift == seg_all).astype(jnp.float32)
        conv_sum = conv_sum + conv_w[KCONV - 1 - lagged] * shifted * same_seq[:, None]
    conv_act = low(jax.nn.silu(conv_sum))
    queries = low(block_mix(conv_act, w_q))
    key_rows = low(block_mix(conv_act, w_k))
    values = low(block_mix(inner_rows, w_v))
    joined = jnp.concatenate([queries, key_rows, values], axis=1)
    bias_pair = jnp.stack([i_bias, f_bias], axis=-1).reshape(2 * NH)
    gate_pre = low(jnp.dot(joined, gate_w, precision=HIGH)) + bias_pair
    normed_h = jax.checkpoint(mixer)(queries.reshape(GROUP, NH, DH), key_rows.reshape(GROUP, NH, DH), values.reshape(GROUP, NH, DH), gate_pre.reshape(GROUP, NH, 2), seg_all, valid_rows)
    normed_h = low_back(low(normed_h)).reshape(GROUP, INNER)
    branch = low((normed_h * gn_gain + skip * conv_act) * jax.nn.silu(gate_z))
    return stream + valid_rows[:, None] * jnp.dot(branch, w_down, precision=HIGH)

def reference(tokens, lengths, ln_gain, w_up, conv_w, conv_b, w_q, w_k, w_v, gate_w, i_bias, f_bias, gn_gain, skip, w_down, cotangent):
    params = (ln_gain.astype(jnp.float32), w_up.astype(jnp.float32), conv_w.astype(jnp.float32), conv_b.astype(jnp.float32), w_q.astype(jnp.float32), w_k.astype(jnp.float32), w_v.astype(jnp.float32), gate_w.astype(jnp.float32), i_bias.astype(jnp.float32), f_bias.astype(jnp.float32), gn_gain.astype(jnp.float32), skip.astype(jnp.float32), w_down.astype(jnp.float32))
    streams = tokens.astype(jnp.float32).reshape(MICRO * N_DP, GROUP, D)
    cot_all = cotangent.astype(jnp.float32).reshape(MICRO * N_DP, GROUP, D)
    lens_all = lengths.reshape(MICRO * N_DP, NSEQ).astype(jnp.int32)

    def one_group(totals, item):
        stream, lens_one, cot_one = item

        def forward_fn(stream_in, *weights):
            return group_forward(stream_in, lens_one, *weights)
        result, pull = jax.vjp(forward_fn, stream, *params)
        grads = pull(cot_one)
        totals = tuple((held + fresh for held, fresh in zip(totals, grads[1:])))
        return (totals, (result.astype(jnp.bfloat16), grads[0].astype(jnp.bfloat16)))
    zeros_init = tuple((jnp.zeros_like(member) for member in params))
    totals, (outs_all, grads_in) = lax.scan(one_group, zeros_init, (streams, lens_all, cot_all))
    block_out = outs_all.reshape(MICRO, TOKENS, D)
    d_tokens = grads_in.reshape(MICRO, TOKENS, D)
    return (block_out, d_tokens, totals[0], totals[1], totals[2], totals[3], totals[4], totals[5], totals[6], totals[7], totals[8], totals[9], totals[10], totals[11], totals[12])
```

```python
from functools import partial

import jax
import jax.numpy as jnp
from jax import lax
from jax.experimental import pallas as pl
from jax.experimental.pallas import tpu as pltpu
from jax.sharding import PartitionSpec as P

EPS = 1e-05
HIGH = lax.Precision.HIGHEST
BF = jnp.bfloat16
F32 = jnp.float32
EDGE = 16
SMALL = 56
VMEM_BYTES = 56 * 1024 * 1024


def mm(a, b):
    return lax.dot_general(a, b, (((1,), (0,)), ((), ())), preferred_element_type=F32)


def nt(a, b):
    return lax.dot_general(a, b, (((1,), (1,)), ((), ())), preferred_element_type=F32)


def tn(a, b):
    return lax.dot_general(a, b, (((0,), (0,)), ((), ())), preferred_element_type=F32)


def split(v):
    high = v.astype(BF)
    return high, (v - high.astype(F32)).astype(BF)


def iota(shape, dim):
    return lax.broadcasted_iota(jnp.int32, shape, dim)


def seg_of(pos, sc, seqs):
    total = (pos >= sc[2]).astype(jnp.int32)
    for e in range(1, seqs):
        total = total + (pos >= sc[2 + e]).astype(jnp.int32)
    return total


def pick(refs, which, dest):
    for at, ref in enumerate(refs):

        @pl.when(which == at)
        def _(ref=ref):
            dest[...] = ref[...]


def put(refs, which, value):
    for at, ref in enumerate(refs):

        @pl.when(which == at)
        def _(ref=ref):
            ref[...] = value


def running_sum(v):
    width = 256
    tri = (iota((width, width), 0) <= iota((width, width), 1)).astype(F32)
    carry = jnp.zeros((v.shape[0], 1), F32)
    parts = []
    for at in range(v.shape[1] // width):
        part = lax.dot_general(
            v[:, at * width : (at + 1) * width],
            tri,
            (((1,), (0,)), ((), ())),
            precision=HIGH,
            preferred_element_type=F32,
        )
        part = part + carry
        carry = part[:, width - 1 : width]
        parts.append(part)
    return jnp.concatenate(parts, axis=1)


def front_kernel(
    seqs, sc, x0, x1, x2, x3, xh, gain, w_in, w_gt, cw, cb, wq, wk, wv, gq, gk, gv,
    normed_o, gz_o, inner_o, halo_o, act_o, cs_o, q_o, k_o, v_o, gt_o, xs, ext,
):
    i = pl.program_id(0)
    chunk = xs.shape[0]
    span = chunk * 4
    pick((x0, x1, x2, x3), i ^ sc[0], xs)

    def norm(rows):
        stream = rows.astype(F32)
        centred = stream - jnp.mean(stream, axis=-1, keepdims=True)
        variance = jnp.mean(centred * centred, axis=-1, keepdims=True)
        return (centred * lax.rsqrt(variance + EPS) * gain[...]).astype(BF)

    @pl.when(i == 0)
    def _():
        edge = mm(norm(xh[...]), w_in[...]).astype(BF).astype(F32)
        ext[0:EDGE, :] = edge
        halo_o[...] = edge

    @pl.when(i > 0)
    def _():
        ext[0:EDGE, :] = ext[chunk : chunk + EDGE, :]

    normed = norm(xs[...])
    normed_o[...] = normed
    inner = mm(normed, w_in[...]).astype(BF)
    inner_o[...] = inner
    gz_o[...] = mm(normed, w_gt[...])
    ext[EDGE : EDGE + chunk, :] = inner.astype(F32)
    pos = sc[1] * span + i * chunk + iota((chunk, 1), 0)
    seg = seg_of(pos, sc, seqs)
    conv_sum = cb[...] + cw[3:4, :] * ext[EDGE : EDGE + chunk, :]
    for lag in range(1, 4):
        same = ((seg_of(pos - lag, sc, seqs) == seg) & (pos >= lag)).astype(F32)
        conv_sum = conv_sum + cw[3 - lag : 4 - lag, :] * ext[EDGE - lag : EDGE - lag + chunk, :] * same
    cs_o[...] = conv_sum
    act = (conv_sum / (1.0 + jnp.exp(-conv_sum))).astype(BF)
    act_o[...] = act
    q = mm(act, wq[...]).astype(BF)
    k = mm(act, wk[...]).astype(BF)
    v = mm(inner, wv[...]).astype(BF)
    q_o[...] = q
    k_o[...] = k
    v_o[...] = v
    gt_o[...] = nt(gq[...], q) + nt(gk[...], k) + nt(gv[...], v)


def gates_kernel(seqs, sc, ib, fb, g0, g1, g2, g3, k, v, rows_o, cols_o, s_o):
    h, s = sc[0], sc[1]
    span, width = k.shape
    factor = width ** (-0.5)
    lin = (g0[...] + g1[...] + g2[...] + g3[...]).astype(BF).astype(F32)
    r = iota(lin.shape, 0)
    ig = jnp.sum(jnp.where(r == 2 * h, lin, 0.0), axis=0, keepdims=True) + ib[h]
    fg = jnp.sum(jnp.where(r == 2 * h + 1, lin, 0.0), axis=0, keepdims=True) + fb[h]
    pos = s * span + iota((1, span), 1)
    seg = seg_of(pos, sc, seqs)
    valid = (seg < seqs).astype(F32)
    log_keep = valid * (jnp.minimum(fg, 0.0) - jnp.log1p(jnp.exp(-jnp.abs(fg))))
    weight = valid * jnp.exp(ig)
    cum8 = running_sum(jnp.broadcast_to(log_keep, (8, span)))
    cum = cum8[0:1, :]
    prev = jnp.where(s == 0, -1, seg_of(s * span - 1, sc, seqs))
    last = seg_of(s * span + span - 1, sc, seqs)
    carried = jnp.where(seg == prev, jnp.exp(cum), 0.0)
    tail = jnp.where(seg == last, jnp.exp(jnp.minimum(cum[:, span - 1 : span] - cum, 0.0)), 0.0)
    tail = tail * weight * factor
    slope = valid / (1.0 + jnp.exp(fg))
    rows = jnp.zeros((8, span), F32)
    for at, row in enumerate((cum, weight, seg.astype(F32), slope, carried, tail, valid)):
        rows = jnp.where(r == at, row, rows)
    rows_o[...] = rows
    cols = jnp.transpose(rows)
    cols_o[...] = cols
    high, low = split(k[...].astype(F32) * cols[:, 5:6])
    s_o[...] = tn(high, v[...]) + tn(low, v[...])


def mix_kernel(
    sc, q, k, v, cols, rows, s_in, act, gz, gn, sk, hid_o, b0, b1, b2, b3, acc
):
    i = pl.program_id(0)
    chunk, width = q.shape
    factor = width ** (-0.5)
    for row in range(4):

        @pl.when(i == row)
        def _(row=row):
            total = None
            for col in range(row + 1):
                at = slice(col * chunk, (col + 1) * chunk)
                scores = nt(q[...], k[at, :]) * factor
                decay = jnp.exp(jnp.minimum(cols[:, 0:1] - rows[0:1, at], 0.0)) * rows[1:2, at]
                allowed = cols[:, 2:3] == rows[2:3, at]
                if col == row:
                    allowed = allowed & (iota((chunk, chunk), 1) <= iota((chunk, chunk), 0))
                high, low = split(scores * jnp.where(allowed, decay, 0.0))
                term = mm(high, v[at, :]) + mm(low, v[at, :])
                total = term if total is None else total + term
            acc[...] = total

    s_high, s_low = split(s_in[...])
    hidden = acc[...] + cols[:, 4:5] * (mm(q[...], s_high) + mm(q[...], s_low))
    hid_o[...] = hidden
    centred = hidden - jnp.mean(hidden, axis=-1, keepdims=True)
    variance = jnp.mean(centred * centred, axis=-1, keepdims=True)
    normed = (centred * lax.rsqrt(variance + EPS)).astype(BF).astype(F32)
    gate = gz[...]
    branch = (normed * gn[...] + sk[...] * act[...].astype(F32)) * (gate / (1.0 + jnp.exp(-gate)))
    put((b0, b1, b2, b3), i ^ sc[0], branch.astype(BF))


def down_back_kernel(
    first, sc, c0, c1, c2, c3, b0, b1, b2, b3, w_dn, gz, act, hid, normed, q, cols, gn, sk, *rest
):
    if not first:
        gd_i, gg_i = rest[:2]
        rest = rest[2:]
    dh_o, z0, z1, z2, z3, skip_o, gd_o, gg_o, small_o, ds_o, cs, bs = rest
    i = pl.program_id(0)
    rel = i ^ sc[0]
    pick((c0, c1, c2, c3), rel, cs)
    pick((b0, b1, b2, b3), rel, bs)

    @pl.when(i == 0)
    def _():
        gd_o[...] = jnp.zeros_like(gd_o) if first else gd_i[...]
        gg_o[...] = jnp.zeros_like(gg_o) if first else gg_i[...]
        small_o[...] = jnp.zeros_like(small_o)
        ds_o[...] = jnp.zeros_like(ds_o)

    cot_mix = (cs[...].astype(F32) * cols[:, 6:7]).astype(BF)
    gd_o[...] += tn(bs[...], cot_mix)
    d_branch = nt(cot_mix, w_dn[...])
    gate = gz[...]
    sig = 1.0 / (1.0 + jnp.exp(-gate))
    d_mid = d_branch * (gate * sig)
    hidden = hid[...]
    centred = hidden - jnp.mean(hidden, axis=-1, keepdims=True)
    rstd = lax.rsqrt(jnp.mean(centred * centred, axis=-1, keepdims=True) + EPS)
    exact = centred * rstd
    normed_h = exact.astype(BF).astype(F32)
    act_f = act[...].astype(F32)
    mid = normed_h * gn[...] + sk[...] * act_f
    d_gate = (d_branch * mid * (sig * (1.0 + gate * (1.0 - sig)))).astype(BF)
    put((z0, z1, z2, z3), rel, d_gate)
    gg_o[...] += tn(d_gate, normed[...])
    small_o[0:1, :] += jnp.sum(d_mid * normed_h, axis=0, keepdims=True)
    small_o[1:2, :] += jnp.sum(d_mid * act_f, axis=0, keepdims=True)
    skip_o[...] = d_mid * sk[...]
    d_norm = (d_mid * gn[...]).astype(BF).astype(F32)
    d_cent = rstd * (d_norm - exact * jnp.mean(d_norm * exact, axis=-1, keepdims=True))
    d_hid = d_cent - jnp.mean(d_cent, axis=-1, keepdims=True)
    dh_o[...] = d_hid
    high, low = split(d_hid * cols[:, 4:5])
    ds_o[...] += tn(q[...], high) + tn(q[...], low)


def mix_back_kernel(
    sc, q, q_all, k, v, dh, cols, cols_all, rows, s_in, ds_out, dq_o, dk_o, dv_o, dg_o, rs
):
    i = pl.program_id(0)
    h, s = sc[0], sc[1]
    chunk, width = q.shape
    span = k.shape[0]
    factor = width ** (-0.5)

    @pl.when(i == 0)
    def _():
        d_high, d_low = split(ds_out[...])
        tail = cols_all[:, 5:6]
        dk_o[...] = tail * (nt(v[...], d_high) + nt(v[...], d_low))
        dv_o[...] = tail * (mm(k[...], d_high) + mm(k[...], d_low))

    dh_high, dh_low = split(dh[...])
    s_high, s_low = split(s_in[...])
    dq_o[...] = cols[:, 4:5] * (nt(dh_high, s_high) + nt(dh_low, s_high) + nt(dh_high, s_low))
    for row in range(4):

        @pl.when(i == row)
        def _(row=row):
            total = None
            for col in range(row + 1):
                at = slice(col * chunk, (col + 1) * chunk)
                scores = nt(q[...], k[at, :]) * factor
                decay = jnp.exp(jnp.minimum(cols[:, 0:1] - rows[0:1, at], 0.0)) * rows[1:2, at]
                allowed = cols[:, 2:3] == rows[2:3, at]
                if col == row:
                    allowed = allowed & (iota((chunk, chunk), 1) <= iota((chunk, chunk), 0))
                decay = jnp.where(allowed, decay, 0.0)
                d_att = nt(dh_high, v[at, :]) + nt(dh_low, v[at, :])
                a_high, a_low = split(decay * scores)
                dv_o[at, :] += tn(a_high, dh_high) + tn(a_low, dh_high) + tn(a_high, dh_low)
                w_high, w_low = split(decay * d_att * factor)
                term = mm(w_high, k[at, :]) + mm(w_low, k[at, :])
                total = term if total is None else total + term
                dk_o[at, :] += tn(w_high, q[...]) + tn(w_low, q[...])
            dq_o[...] += total

    rs[pl.ds(pl.multiple_of(i * chunk, chunk), chunk), :] = jnp.broadcast_to(
        jnp.sum(dq_o[...] * q[...].astype(F32), axis=1, keepdims=True), (chunk, 128)
    )

    @pl.when(i == 3)
    def _():
        col_sum = jnp.sum(dk_o[...] * k[...].astype(F32), axis=1, keepdims=True)
        both = jnp.where(iota((span, 128), 1) == 0, col_sum, rs[...] - col_sum)
        across = jnp.transpose(both)
        d_ig = across[0:1, :]
        d_cum = across[8:16, :]
        running = running_sum(d_cum)
        whole = jnp.where(s == 0, 0.0, running[:, span - 1 : span])
        later = (whole - running + d_cum)[0:1, :]
        d_fg = rows[3:4, :] * later
        r = iota((8, span), 0)
        dg_o[...] = jnp.where(r == 2 * h, d_ig, jnp.where(r == 2 * h + 1, d_fg, 0.0))


def front_back_kernel(
    seqs, sc, dq, dk, dv, d0, d1, d2, d3, q, k, v, act, cs, inner, halo, skip_d, small_i,
    gq, gk, gv, wq, wk, wv, dcs_o, div_o, small_o, ext, fq, fk, fv,
):
    i = pl.program_id(0)
    chunk, width = dq.shape
    span = chunk * 4

    @pl.when(i == 0)
    def _():
        small_o[...] = jnp.zeros_like(small_o)
        small_o[41:43, :] = small_i[0:2, :]
        fq[...] = jnp.zeros_like(fq)
        fk[...] = jnp.zeros_like(fk)
        fv[...] = jnp.zeros_like(fv)
        ext[0:EDGE, :] = halo[...]

    @pl.when(i > 0)
    def _():
        ext[0:EDGE, :] = ext[chunk : chunk + EDGE, :]

    ext[EDGE : EDGE + chunk, :] = inner[...].astype(F32)
    dg = d0[...] + d1[...] + d2[...] + d3[...]
    g_high, g_low = split(dg)
    small_o[0:8, :] += mm(g_high, q[...]) + mm(g_low, q[...])
    small_o[8:16, :] += mm(g_high, k[...]) + mm(g_low, k[...])
    small_o[16:24, :] += mm(g_high, v[...]) + mm(g_low, v[...])
    small_o[48:56, :] += jnp.broadcast_to(jnp.sum(dg, axis=1, keepdims=True), (8, width))
    dq_h, dq_l = split(dq[...] + tn(g_high, gq[...]) + tn(g_low, gq[...]))
    dk_h, dk_l = split(dk[...] + tn(g_high, gk[...]) + tn(g_low, gk[...]))
    dv_h, dv_l = split(dv[...] + tn(g_high, gv[...]) + tn(g_low, gv[...]))
    fq[...] += tn(act[...], dq_h)
    fk[...] += tn(act[...], dk_h)
    fv[...] += tn(inner[...], dv_h)
    d_act = skip_d[...] + nt(dq_h, wq[...]) + nt(dq_l, wq[...]) + nt(dk_h, wk[...]) + nt(dk_l, wk[...])
    div_o[...] = nt(dv_h, wv[...]) + nt(dv_l, wv[...])
    conv_sum = cs[...]
    sig = 1.0 / (1.0 + jnp.exp(-conv_sum))
    d_cs = d_act * (sig * (1.0 + conv_sum * (1.0 - sig)))
    dcs_o[...] = d_cs
    pos = sc[1] * span + i * chunk + iota((chunk, 1), 0)
    seg = seg_of(pos, sc, seqs)
    small_o[40:41, :] += jnp.sum(d_cs, axis=0, keepdims=True)
    small_o[39:40, :] += jnp.sum(d_cs * ext[EDGE : EDGE + chunk, :], axis=0, keepdims=True)
    for lag in range(1, 4):
        same = ((seg_of(pos - lag, sc, seqs) == seg) & (pos >= lag)).astype(F32)
        small_o[39 - lag : 40 - lag, :] += jnp.sum(
            d_cs * same * ext[EDGE - lag : EDGE - lag + chunk, :], axis=0, keepdims=True
        )

    @pl.when(i == 3)
    def _():
        on = iota((width, width), 0) // 4 == iota((width, width), 1) // 4
        ones = (iota((16, width), 1) % 4 == iota((16, width), 0) % 4).astype(BF)
        for at, full in enumerate((fq, fk, fv)):
            kept = jnp.where(on, full[...], 0.0)
            a, b = split(kept)
            compact = nt(ones, a) + nt(ones, b)
            small_o[24 + 4 * at : 28 + 4 * at, :] = compact[0:4, :]


def inner_back_kernel(
    seqs, first, last, sc, dcs, nxt, nxt_halo, div, normed, cw, gain, *rest
):
    if not first:
        gi_i = rest[0]
        rest = rest[1:]
    if last:
        w_in, w_gt, gg = rest[:3]
        rest = rest[3:]
    i0, i1, i2, i3, gi_o, ln_o, ext = rest
    i = pl.program_id(0)
    chunk = dcs.shape[0]
    span = chunk * 4

    @pl.when(i == 0)
    def _():
        gi_o[...] = jnp.zeros_like(gi_o) if first else gi_i[...]

    ext[0:chunk, :] = dcs[...]

    @pl.when(i < 3)
    def _():
        ext[chunk : chunk + EDGE, :] = nxt[...]

    @pl.when(i == 3)
    def _():
        ext[chunk : chunk + EDGE, :] = nxt_halo[...]

    pos = sc[1] * span + i * chunk + iota((chunk, 1), 0)
    seg = seg_of(pos, sc, seqs)
    d_inner = div[...] + cw[3:4, :] * ext[0:chunk, :]
    for lag in range(1, 4):
        same = (seg_of(pos + lag, sc, seqs) == seg).astype(F32)
        d_inner = d_inner + cw[3 - lag : 4 - lag, :] * ext[lag : lag + chunk, :] * same
    rounded = d_inner.astype(BF)
    put((i0, i1, i2, i3), i ^ sc[0], rounded)
    gi_o[...] += tn(rounded, normed[...])

    @pl.when(i == 3)
    def _():
        if last:
            both = gi_o[...] * w_in[...].astype(F32) + gg[...] * w_gt[...].astype(F32)
            ln_o[...] = jnp.sum(both, axis=0, keepdims=True) / gain[...]
        else:
            ln_o[...] = jnp.zeros_like(ln_o)


def out_kernel(seqs, micros, sc, tokens, *rest):
    blocks, (w_dn, out_o) = rest[: 4 * micros], rest[4 * micros :]
    h = sc[0]
    rows, width = blocks[0].shape
    pos = (sc[1] * 4 + h) * rows + iota((rows, 1), 0)
    for m in range(micros):
        ends = [sc[2 + m * seqs + e] for e in range(seqs)]
        seg = sum((pos >= e).astype(jnp.int32) for e in ends)
        valid = (seg < seqs).astype(F32)
        mixed = None
        for rel in range(4):
            at = pl.ds(pl.multiple_of((h ^ rel) * width, width), width)
            term = mm(blocks[4 * m + rel][...], w_dn[at, :])
            mixed = term if mixed is None else mixed + term
        out_o[m] = (tokens[m].astype(F32) + valid * mixed).astype(BF)


def tokens_back_kernel(first, sc, x, c, i0, i1, i2, i3, z0, z1, z2, z3, w_t, gain, *rest):
    out_o = rest[-1]
    h = sc[0]
    width = i0.shape[1]
    inner = w_t.shape[0] // 2
    d_normed = None
    for rel, (low, up) in enumerate(((i0, z0), (i1, z1), (i2, z2), (i3, z3))):
        start = pl.multiple_of((h ^ rel) * width, width)
        term = mm(low[...], w_t[pl.ds(start, width), :])
        term = term + mm(up[...], w_t[pl.ds(pl.multiple_of(inner + start, width), width), :])
        d_normed = term if d_normed is None else d_normed + term
    stream = x[...].astype(F32)
    centred = stream - jnp.mean(stream, axis=-1, keepdims=True)
    rstd = lax.rsqrt(jnp.mean(centred * centred, axis=-1, keepdims=True) + EPS)
    exact = centred * rstd
    d_n = d_normed * gain[...]
    d_cent = rstd * (d_n - exact * jnp.mean(d_n * exact, axis=-1, keepdims=True))
    d_x = d_cent - jnp.mean(d_cent, axis=-1, keepdims=True)
    out_o[...] = (c[...].astype(F32) + d_x).astype(BF)


def whole(shape):
    return pl.BlockSpec(shape, lambda i, sc: (0,) * len(shape))


def by_chunk(rows, width):
    return pl.BlockSpec((rows, width), lambda i, sc: (i, 0))


def head_cols(rows, width, skip=0):
    return pl.BlockSpec((rows, width), lambda i, sc: (0, sc[0] + skip))


def head_rows(rows, width, skip=0):
    return pl.BlockSpec((rows, width), lambda i, sc: (sc[0] + skip, 0))


def micro_block(m, rows, width):
    return pl.BlockSpec((None, rows, width), lambda i, sc: (m, 0, 0))


def call(body, grid, in_specs, out_specs, out_shape, scratch, flops, sent, args, aliases=None):
    return pl.pallas_call(
        body,
        grid_spec=pltpu.PrefetchScalarGridSpec(
            num_scalar_prefetch=1,
            grid=grid,
            in_specs=in_specs,
            out_specs=out_specs,
            scratch_shapes=scratch,
        ),
        out_shape=[jax.ShapeDtypeStruct(shape, dtype) for shape, dtype in out_shape],
        compiler_params=pltpu.CompilerParams(vmem_limit_bytes=VMEM_BYTES),
        cost_estimate=pl.CostEstimate(flops=flops, bytes_accessed=sent, transcendentals=0),
        input_output_aliases=aliases or {},
    )(*args)


def per_device(
    tokens, lengths, ln_gain, w_up, conv_w, conv_b, w_q, w_k, w_v, gate_w, i_bias, f_bias,
    gn_gain, skip, w_down, cotangent,
):
    micros, rows, dim = tokens.shape
    inner = w_down.shape[0]
    heads = i_bias.shape[0]
    width = inner // heads
    seqs = lengths.shape[2]
    dp, sq, hd = lax.axis_size("dp"), lax.axis_size("seq"), lax.axis_size("head")
    assert hd == heads == 4 and sq == 2 and conv_w.shape[0] == 4
    ranks = dp * sq
    every = ranks * hd
    span = rows * hd
    h, s = lax.axis_index("head"), lax.axis_index("seq")
    place = jnp.stack([h, s]).astype(jnp.int32)
    ends = jnp.cumsum(lengths[:, 0], axis=1).astype(jnp.int32)
    scal = [jnp.concatenate([place, ends[m]]) for m in range(micros)]
    scal_all = jnp.concatenate([place, ends.reshape(-1)])

    def across(value, rel):
        return lax.ppermute(value, "head", [(at, at ^ rel) for at in range(hd)])

    def exchange(parts):
        return [parts[0]] + [across(parts[rel], rel) for rel in range(1, hd)]

    def gather(value):
        return exchange([value] * hd)

    gain = ln_gain.reshape(1, dim)
    cb, gn, sk = conv_b.reshape(1, inner), gn_gain.reshape(1, inner), skip.reshape(1, inner)
    w_upt = w_up.T
    gate_t = gate_w.T

    def spread(weight):
        mine = lax.dynamic_slice_in_dim(weight, h * (width // 4), width // 4, 0).reshape(width, 4)
        on = (jnp.arange(width)[:, None] // 4) == (jnp.arange(width)[None, :] // 4)
        return jnp.where(on, jnp.tile(mine, (1, width // 4)), 0).astype(BF)

    wq, wk, wv = spread(w_q), spread(w_k), spread(w_v)
    sq_spec = whole((width, width))
    gate_specs = [head_cols(8, width, part * heads) for part in range(3)]

    x_parts = [gather(tokens[m]) for m in range(micros)]
    tails = [
        lax.ppermute(x_parts[m][0][rows - EDGE :], "seq", [(0, 1)]) for m in range(micros)
    ]
    x_halo = []
    for m in range(micros):
        own = jnp.where(h == hd - 1, tails[m], jnp.zeros_like(tails[m]))
        spread_out = [
            lax.ppermute(own, "head", [(hd - 1, at)]) for at in range(hd - 1)
        ]
        x_halo.append(sum(spread_out, own))
    c_parts = [gather(cotangent[m]) for m in range(micros)]

    bf_span, f_span = ((span, width), BF), ((span, width), F32)
    chunk_spec = by_chunk(rows, width)
    block = whole((rows, width))
    fronts, gates, states = [], [], []
    for m in range(micros):
        fronts.append(
            call(
                partial(front_kernel, seqs),
                (hd,),
                [whole((rows, dim))] * 4
                + [
                    whole((EDGE, dim)), whole((1, dim)), head_cols(dim, width),
                    head_cols(dim, width, heads), head_cols(4, width), head_cols(1, width),
                    sq_spec, sq_spec, sq_spec,
                ]
                + gate_specs,
                [
                    by_chunk(rows, dim), chunk_spec, chunk_spec, whole((EDGE, width)), chunk_spec,
                    chunk_spec, chunk_spec, chunk_spec, chunk_spec,
                    pl.BlockSpec((8, rows), lambda i, sc: (0, i)),
                ],
                [
                    ((span, dim), BF), f_span, bf_span, ((EDGE, width), F32), bf_span, f_span,
                    bf_span, bf_span, bf_span, ((8, span), F32),
                ],
                [pltpu.VMEM((rows, dim), BF), pltpu.VMEM((rows + EDGE, width), F32)],
                2_100_000_000,
                14_000_000,
                [scal[m], *x_parts[m], x_halo[m], gain, w_up, w_up, conv_w, cb, wq, wk, wv]
                + [gate_t] * 3,
            )
        )
    for m in range(micros):
        gates.append(gather(fronts[m][9]))
    for m in range(micros):
        k, v = fronts[m][7:9]
        states.append(
            call(
                partial(gates_kernel, seqs),
                (1,),
                [pl.BlockSpec(memory_space=pltpu.SMEM)] * 2
                + [whole((8, span))] * 4
                + [whole((span, width))] * 2,
                [whole((8, span)), whole((span, 8)), sq_spec],
                [((8, span), F32), ((span, 8), F32), ((width, width), F32)],
                [],
                600_000_000,
                4_000_000,
                [scal[m], i_bias, f_bias, *gates[m], k, v],
            )
        )
    states_in = [lax.ppermute(states[m][2], "seq", [(0, 1)]) for m in range(micros)]
    mixed, branches = [], []
    for m in range(micros):
        normed, gz, inner_b, halo, act, cs, q, k, v, _ = fronts[m]
        rows_t, cols_t, _ = states[m]
        got = call(
            mix_kernel,
            (hd,),
            [
                chunk_spec, whole((span, width)), whole((span, width)), by_chunk(rows, 8),
                whole((8, span)), sq_spec, chunk_spec, chunk_spec, head_cols(1, width),
                head_cols(1, width),
            ],
            [chunk_spec] + [block] * 4,
            [f_span] + [((rows, width), BF)] * 4,
            [pltpu.VMEM((rows, width), F32)],
            2_200_000_000,
            9_000_000,
            [scal[m], q, k, v, cols_t, rows_t, states_in[m], act, gz, gn, sk],
        )
        mixed.append(got)
        branches.append(exchange(list(got[1:])))
    downs = []
    for m in range(micros):
        normed, gz, inner_b, halo, act, cs, q, k, v, _ = fronts[m]
        rows_t, cols_t, _ = states[m]
        big = whole((width, dim))
        downs.append(
            call(
                partial(down_back_kernel, m == 0),
                (hd,),
                [whole((rows, dim))] * 4
                + [block] * 4
                + [
                    head_rows(width, dim), chunk_spec, chunk_spec, chunk_spec,
                    by_chunk(rows, dim), chunk_spec, by_chunk(rows, 8), head_cols(1, width),
                    head_cols(1, width),
                ]
                + ([] if m == 0 else [big, big]),
                [chunk_spec] + [block] * 4 + [chunk_spec, big, big, whole((8, width)), sq_spec],
                [f_span]
                + [((rows, width), BF)] * 4
                + [
                    f_span, ((width, dim), F32), ((width, dim), F32), ((8, width), F32),
                    ((width, width), F32),
                ],
                [pltpu.VMEM((rows, dim), BF), pltpu.VMEM((rows, width), BF)],
                2_400_000_000,
                14_000_000,
                [
                    scal[m], *c_parts[m], *mixed[m][1:], w_down, gz, act, mixed[m][0], normed, q,
                    cols_t, gn, sk,
                ]
                + ([] if m == 0 else [downs[m - 1][6], downs[m - 1][7]]),
            )
        )
    states_out = [lax.ppermute(downs[m][9], "seq", [(1, 0)]) for m in range(micros)]
    d_gates_z = [exchange(list(downs[m][1:5])) for m in range(micros)]
    mix_backs = []
    for m in range(micros):
        normed, gz, inner_b, halo, act, cs, q, k, v, _ = fronts[m]
        rows_t, cols_t, _ = states[m]
        all_spec = whole((span, width))
        mix_backs.append(
            call(
                mix_back_kernel,
                (hd,),
                [
                    chunk_spec, all_spec, all_spec, all_spec, chunk_spec, by_chunk(rows, 8),
                    whole((span, 8)), whole((8, span)), sq_spec, sq_spec,
                ],
                [chunk_spec, all_spec, all_spec, whole((8, span))],
                [f_span, f_span, f_span, ((8, span), F32)],
                [pltpu.VMEM((span, 128), F32)],
                7_000_000_000,
                12_000_000,
                [
                    scal[m], q, q, k, v, downs[m][0], cols_t, cols_t, rows_t, states_in[m],
                    states_out[m],
                ],
            )
        )
    d_gates = [gather(mix_backs[m][3]) for m in range(micros)]
    front_backs = []
    for m in range(micros):
        normed, gz, inner_b, halo, act, cs, q, k, v, _ = fronts[m]
        dq, dk, dv, _ = mix_backs[m]
        lane_spec = pl.BlockSpec((8, rows), lambda i, sc: (0, i))
        front_backs.append(
            call(
                partial(front_back_kernel, seqs),
                (hd,),
                [chunk_spec] * 3
                + [lane_spec] * 4
                + [chunk_spec] * 6
                + [whole((EDGE, width)), chunk_spec, whole((8, width))]
                + gate_specs
                + [sq_spec] * 3,
                [chunk_spec, chunk_spec, whole((SMALL, width))],
                [f_span, f_span, ((SMALL, width), F32)],
                [pltpu.VMEM((rows + EDGE, width), F32)] + [pltpu.VMEM((width, width), F32)] * 3,
                3_000_000_000,
                16_000_000,
                [
                    scal[m], dq, dk, dv, *d_gates[m], q, k, v, act, cs, inner_b, halo,
                    downs[m][5], downs[m][8], gate_t, gate_t, gate_t, wq, wk, wv,
                ],
            )
        )
    edges = [lax.ppermute(front_backs[m][0][:EDGE], "seq", [(1, 0)]) for m in range(micros)]
    inner_backs, d_inners = [], []
    for m in range(micros):
        first, last = m == 0, m == micros - 1
        big = whole((width, dim))
        per = rows // EDGE
        got = call(
            partial(inner_back_kernel, seqs, first, last),
            (hd,),
            [
                chunk_spec,
                pl.BlockSpec((EDGE, width), lambda i, sc: (jnp.minimum(i + 1, hd - 1) * per, 0)),
                whole((EDGE, width)), chunk_spec, by_chunk(rows, dim), head_cols(4, width),
                whole((1, dim)),
            ]
            + ([] if first else [big])
            + ([head_rows(width, dim), head_rows(width, dim, heads), big] if last else []),
            [block] * 4 + [big, whole((1, dim))],
            [((rows, width), BF)] * 4 + [((width, dim), F32), ((1, dim), F32)],
            [pltpu.VMEM((rows + EDGE, width), F32)],
            700_000_000,
            8_000_000,
            [
                scal[m], front_backs[m][0], front_backs[m][0], edges[m], front_backs[m][1],
                fronts[m][0], conv_w, gain,
            ]
            + ([] if first else [inner_backs[m - 1][4]])
            + ([w_upt, w_upt, downs[m][7]] if last else []),
        )
        inner_backs.append(got)
        d_inners.append(exchange(list(got[:4])))

    block_out = call(
        partial(out_kernel, seqs, micros),
        (1,),
        [whole(tokens.shape)] + [block] * (4 * micros) + [whole((inner, dim))],
        [whole(tokens.shape)],
        [(tokens.shape, BF)],
        [],
        1_200_000_000,
        6_000_000,
        [scal_all, tokens, *[part for m in range(micros) for part in branches[m]], w_down],
    )[0]
    d_tokens = None
    for m in range(micros):
        args = [
            scal[m], tokens, cotangent, *d_inners[m], *d_gates_z[m], w_upt, gain,
        ] + ([] if m == 0 else [d_tokens])
        d_tokens = call(
            partial(tokens_back_kernel, m == 0),
            (1,),
            [micro_block(m, rows, dim)] * 2
            + [block] * 8
            + [whole((2 * inner, dim)), whole((1, dim))]
            + ([] if m == 0 else [pl.BlockSpec(memory_space=pl.ANY)]),
            [micro_block(m, rows, dim)],
            [(tokens.shape, BF)],
            [],
            1_200_000_000,
            7_000_000,
            args,
            None if m == 0 else {len(args) - 1: 0},
        )[0]

    last = micros - 1
    gi, gg, gd = inner_backs[last][4], downs[last][7], downs[last][6]
    up_w, down_w = 2 * inner // every, inner // every
    up_terms = jnp.stack([gg.reshape(dp, up_w, dim), gi.reshape(dp, up_w, dim)], axis=1)
    terms = jnp.concatenate(
        [up_terms.reshape(ranks, up_w, dim), gd.reshape(ranks, down_w, dim)], axis=1
    ).astype(BF)
    terms = lax.all_to_all(terms, ("dp", "seq"), split_axis=0, concat_axis=0, tiled=True)
    terms = jnp.sum(terms.astype(F32), axis=0)
    axes = ("dp", "seq", "head")
    up_pairs, down_pairs = [], []
    for rank in range(ranks):
        for at in range(hd):
            up_first = at * dp + rank // 2 + (0 if rank % 2 else every // 2)
            up_pairs.append((rank * hd + at, up_first))
            down_pairs.append((rank * hd + at, at * ranks + rank))
    g_up = lax.ppermute(terms[:up_w], axes, up_pairs).T
    g_down = lax.ppermute(terms[up_w:], axes, down_pairs)

    small = sum(front_backs[m][2] for m in range(micros))
    ln_rows = inner_backs[last][5].reshape(2, width)
    small = jnp.concatenate([small[:44], ln_rows, small[46:]], axis=0)
    small = small + lax.ppermute(small, "seq", [(0, 1), (1, 0)])
    small = lax.all_to_all(
        jnp.broadcast_to(small[None], (dp, SMALL, width)), "dp", split_axis=0, concat_axis=0, tiled=True
    ).sum(axis=0)
    small = lax.all_to_all(
        jnp.broadcast_to(small[None], (hd, SMALL, width)), "head", split_axis=0, concat_axis=0, tiled=True
    )
    g_gate = small[:, 0:24].reshape(hd, 3, 8, width).transpose(1, 0, 3, 2).reshape(3 * inner, 8)
    maps = [
        small[:, at : at + 4].transpose(0, 2, 1).reshape(inner // 4, 4, 4) for at in (24, 28, 32)
    ]
    g_conv_w = small[:, 36:40].transpose(1, 0, 2).reshape(4, inner)
    g_ln = jnp.sum(small[:, 44:46], axis=0).reshape(dim)
    bias = small[0, 48:56, 0].reshape(heads, 2)
    return (
        block_out,
        d_tokens,
        g_ln,
        g_up,
        g_conv_w,
        small[:, 40].reshape(inner),
        *maps,
        g_gate,
        bias[:, 0],
        bias[:, 1],
        small[:, 41].reshape(inner),
        small[:, 42].reshape(inner),
        g_down,
    )


def solution(mesh):
    rows = P(None, ("dp", "seq", "head"), None)
    placed = (rows, P(None, "dp", None), *[P()] * 13, rows)
    outs = (rows, rows, P(), P(None, ("dp", "seq", "head")), *[P()] * 10, P(("dp", "seq", "head"), None))
    return jax.shard_map(per_device, mesh=mesh, in_specs=placed, out_specs=outs, check_vma=False)
```

```python
from functools import partial

import jax
import jax.numpy as jnp
from jax import lax
from jax.experimental import pallas as pl
from jax.experimental.pallas import tpu as pltpu
from jax.sharding import PartitionSpec as P

EPS = 1e-05
HIGH = lax.Precision.HIGHEST
BF = jnp.bfloat16
F32 = jnp.float32
EDGE = 16
SMALL = 48
NEVER = -1e30
VMEM_BYTES = 60 * 1024 * 1024


def mm(a, b):
    return lax.dot_general(a, b, (((1,), (0,)), ((), ())), preferred_element_type=F32)


def nt(a, b):
    return lax.dot_general(a, b, (((1,), (1,)), ((), ())), preferred_element_type=F32)


def tn(a, b):
    return lax.dot_general(a, b, (((0,), (0,)), ((), ())), preferred_element_type=F32)


def split(v):
    high = v.astype(BF)
    return high, (v - high.astype(F32)).astype(BF)


def iota(shape, dim):
    return lax.broadcasted_iota(jnp.int32, shape, dim)


def seg_of(pos, sc, seqs, m):
    total = (pos >= sc[2 + m * seqs]).astype(jnp.int32)
    for e in range(1, seqs):
        total = total + (pos >= sc[2 + m * seqs + e]).astype(jnp.int32)
    return total


def pick(refs, which, dest, rows):
    for at, ref in enumerate(refs):

        @pl.when(which == at)
        def _(ref=ref):
            dest[...] = ref[rows, :]


def put(refs, which, value):
    for at, ref in enumerate(refs):

        @pl.when(which == at)
        def _(ref=ref):
            ref[...] = value


def lane_sums(v):
    ones = jnp.ones((8, v.shape[1]), BF)
    high, low = split(v)
    return nt(ones, high) + nt(ones, low)


def running_sum(v):
    width = v.shape[1] // 8
    tri = (iota((width, width), 0) <= iota((width, width), 1)).astype(BF)
    chunks = jnp.concatenate([v[:, c * width : (c + 1) * width] for c in range(8)], axis=0)
    high, rest = split(chunks)
    rest = chunks - high.astype(F32)
    mid, low = split(rest)
    within = mm(high, tri) + (mm(mid, tri) + mm(low, tri))
    carry, parts = jnp.zeros((1, 1), F32), []
    for c in range(8):
        parts.append(within[c : c + 1, :] + carry)
        carry = carry + within[c : c + 1, width - 1 : width]
    return jnp.concatenate(parts, axis=1)


LANES = 128


def to_tiles(ext, start, value):
    rows, width = value.shape
    for t in range(width // LANES):
        ext[t, start : start + rows, :] = value[:, t * LANES : (t + 1) * LANES]


def conv_blocks(ext, rows, ages, cw, cb, step):
    for r in range(0, rows, step):
        age = jnp.broadcast_to(ages[r : r + step], (step, LANES))
        for t in range(ext.shape[0]):
            lanes = slice(t * LANES, (t + 1) * LANES)
            lags = [ext[t, EDGE + r : EDGE + r + step, :]]
            for lag in range(1, 4):
                earlier = ext[t, EDGE + r - lag : EDGE + r - lag + step, :]
                lags.append(jnp.where(age >= lag, earlier, 0.0))
            total = cb[:, lanes] + cw[3:4, lanes] * lags[0]
            for lag in range(1, 4):
                total = total + cw[3 - lag : 4 - lag, lanes] * lags[lag]
            yield slice(r, r + step), lanes, total, lags


def folded(v):
    return sum(v[e : e + 8] for e in range(8, v.shape[0], 8)) + v[0:8]


def front_kernel(
    sc, x0, x1, x2, x3, xh, marks, gain, w_in, w_gt, cw, cb, wq, wk, wv, gq, gk, gv, *rest
):
    normed_o, gz_o, five_o, halo_o, gt_o, xs, ext = rest[-7:]
    i = pl.program_id(0)
    chunk = xs.shape[0]
    pick((x0, x1, x2, x3), i ^ sc[0], xs, slice(0, chunk))

    def norm(rows):
        stream = rows.astype(F32)
        centred = stream - jnp.mean(stream, axis=-1, keepdims=True)
        variance = jnp.mean(centred * centred, axis=-1, keepdims=True)
        return (centred * lax.rsqrt(variance + EPS) * gain[...]).astype(BF)

    @pl.when(i == 0)
    def _():
        edge = mm(norm(xh[...]), w_in[...]).astype(BF)
        to_tiles(ext, 0, edge.astype(F32))
        halo_o[...] = edge

    @pl.when(i > 0)
    def _():
        ext[:, 0:EDGE, :] = ext[:, chunk : chunk + EDGE, :]

    for r in range(0, chunk, 32):
        normed_o[r : r + 32, :] = norm(xs[r : r + 32, :])
    inner = mm(normed_o[...], w_in[...]).astype(BF)
    five_o[4] = inner
    to_tiles(ext, EDGE, inner.astype(F32))
    gz_o[...] = mm(normed_o[...], w_gt[...])
    ages = jnp.transpose(marks[...])[:, 0:1]
    for rows, lanes, total, _ in conv_blocks(ext, chunk, ages, cw, cb, 64):
        five_o[3, rows, lanes] = (total / (1.0 + jnp.exp(-total))).astype(BF)
    q = mm(five_o[3], wq[...]).astype(BF)
    k = mm(five_o[3], wk[...]).astype(BF)
    v = mm(five_o[4], wv[...]).astype(BF)
    five_o[0] = q
    five_o[1] = k
    five_o[2] = v
    gt_o[...] = nt(gq[...], q) + nt(gk[...], k) + nt(gv[...], v)


def gates_kernel(seqs, sc, ib, fb, g0, g1, g2, g3, k, v, rows_o, s_o):
    m = pl.program_id(0)
    h, s = sc[0], sc[1]
    span, width = k.shape
    factor = width ** (-0.5)
    lin = (g0[...] + g1[...] + g2[...] + g3[...]).astype(BF).astype(F32)
    r = iota(lin.shape, 0)
    ig = jnp.sum(jnp.where(r == 2 * h, lin, 0.0), axis=0, keepdims=True) + ib[h]
    fg = jnp.sum(jnp.where(r == 2 * h + 1, lin, 0.0), axis=0, keepdims=True) + fb[h]
    pos = s * span + iota((1, span), 1)
    seg = seg_of(pos, sc, seqs, m)
    valid = (seg < seqs).astype(F32)
    log_keep = valid * (jnp.minimum(fg, 0.0) - jnp.log1p(jnp.exp(-jnp.abs(fg))))
    cum = running_sum(log_keep)
    prev = jnp.where(s == 0, -1, seg_of(s * span - 1, sc, seqs, m))
    last = seg_of(s * span + span - 1, sc, seqs, m)
    carried = jnp.where(seg == prev, jnp.exp(cum), 0.0)
    offset = jnp.where(seg < seqs, ig - cum, NEVER)
    tail = jnp.exp(jnp.where(seg == last, cum[:, span - 1 : span] + offset, NEVER)) * factor
    slope = valid / (1.0 + jnp.exp(fg))
    rows = jnp.zeros((8, span), F32)
    for at, row in enumerate((cum, offset, seg.astype(F32), slope, carried, tail, valid)):
        rows = jnp.where(r == at, row, rows)
    rows_o[...] = rows
    cols = jnp.transpose(rows)
    high, low = split(k[...].astype(F32) * cols[:, 5:6])
    s_o[...] = tn(high, v[...]) + tn(low, v[...])


def mix_kernel(
    sc, rows, s_in, gn, sk, five, gz, normed, c0, c1, c2, c3a, c3b, w_dn, *rest
):
    p0, p1, p2, p3, gd_o, gg_o, four_o, ds_o, small_o, sums_o = rest[:10]
    fb, zb, nb, cb, wb, pb, four, gd, gg, go, acc, a_high, decays = rest[10:23]
    q2, v2, dh2, dbr, brs, dgs, in_sems, out_sems = rest[23:]
    h = sc[0]
    micros, _, span, width = fb.shape
    chunk = acc.shape[0]
    two = 2 * chunk
    factor = width ** (-0.5)

    def rows_of(i, size=chunk):
        return pl.ds(pl.multiple_of(i * size, size), size)

    def qkv_in(m, j):
        at, three = rows_of(j, two), pl.ds(0, 3)
        to = fb.at[m, three, at]
        return pltpu.make_async_copy(five.at[m, three, at], to, in_sems.at[m, 0, j])

    def chunk_in(m, i):
        at = rows_of(i)
        return [
            pltpu.make_async_copy(five.at[m, 3, at], fb.at[m, 3, at], in_sems.at[m, 1, i]),
            pltpu.make_async_copy(gz.at[m, at], zb.at[m, at], in_sems.at[m, 2, i]),
            pltpu.make_async_copy(normed.at[m, at], nb.at[m, at], in_sems.at[m, 3, i]),
        ]

    def cot_in(m, rel, i, last=False):
        ref = (c0.at[m], c1.at[m], c2.at[m], c3b if last else c3a)[rel]
        return pltpu.make_async_copy(ref, cb.at[m, i], in_sems.at[m, 4, i])

    weight_in = pltpu.make_async_copy(w_dn.at[rows_of(h, width)], wb, in_sems.at[0, 5, 0])

    def others_in(m, last):
        for rel in range(4):
            cot_in(m, rel, rel ^ h, last).start()
        for copy in (*chunk_in(m, 1), qkv_in(m, 1), *chunk_in(m, 2), *chunk_in(m, 3)):
            copy.start()

    for copy in (qkv_in(0, 0), weight_in, *chunk_in(0, 0)):
        copy.start()
    others_in(0, False)
    small_o[...] = jnp.zeros_like(small_o)
    gd[...] = jnp.zeros_like(gd)
    gg[...] = jnp.zeros_like(gg)

    def pair_out(m, rel, i):
        at = pl.ds(2 * m, 2)
        to = (p0, p1, p2, p3)[rel].at[at]
        return pltpu.make_async_copy(pb.at[i, at], to, out_sems.at[m, 0, rel])

    def rows_out(m, i):
        at = rows_of(i)
        return [
            pltpu.make_async_copy(four.at[m, 0, at], four_o.at[m, 0, at], out_sems.at[m, 1, i]),
            pltpu.make_async_copy(four.at[m, 3, at], four_o.at[m, 3, at], out_sems.at[m, 2, i]),
        ]

    def key_out(m, j):
        at, pair = rows_of(j, two), pl.ds(1, 2)
        to = four_o.at[m, pair, at]
        return pltpu.make_async_copy(four.at[m, pair, at], to, out_sems.at[m, 3, j])

    grads_out = [
        pltpu.make_async_copy(go.at[0], gd_o, out_sems.at[0, 4, 0]),
        pltpu.make_async_copy(go.at[1], gg_o, out_sems.at[0, 4, 1]),
    ]

    def one(at_step, none):
        m, i = at_step // 4, at_step % 4

        @pl.when(i == 0)
        def _():
            four[m, 1] = jnp.zeros((span, width), F32)
            four[m, 2] = jnp.zeros((span, width), F32)
            ds_o[m] = jnp.zeros((width, width), F32)

        @pl.when(at_step == 1)
        def _():
            for copy in (qkv_in(1, 0), *chunk_in(1, 0)):
                copy.start()
            others_in(1, True)

        start = pl.multiple_of(i * chunk, chunk)
        own = pl.ds(start, chunk)

        @pl.when(i % 2 == 0)
        def _():
            at = rows_of(i // 2, two)
            qkv_in(m, i // 2).wait()
            v2[at, 0:width] = fb[m, 2, at, :]
            v2[at, width:] = fb[m, 2, at, :]

        acc[...] = jnp.zeros_like(acc)
        here = start + iota((chunk, 1), 0)
        cols = jnp.transpose(rows[m, :, own])
        cum, seg, carried, valid = cols[:, 0:1], cols[:, 2:3], cols[:, 4:5], cols[:, 6:7]

        def attend(j, none):
            at = rows_of(j, two)
            scores = nt(fb[m, 0, own, :], fb[m, 1, at, :]) * factor
            allowed = (seg == rows[m, 2:3, at]) & (j * two + iota((1, two), 1) <= here)
            decay = jnp.exp(jnp.where(allowed, cum + rows[m, 1:2, at], NEVER))
            decays[j] = decay
            high, low = split(scores * decay)
            a_high[j] = high
            acc[...] += mm(high, fb[m, 2, at, :]) + mm(low, fb[m, 2, at, :])
            return none

        lax.fori_loop(0, i // 2 + 1, attend, 0)
        q2[:, 0:width] = fb[m, 0, own, :]
        q2[:, width:] = fb[m, 0, own, :]
        acc[...] += carried * mm(q2[...], jnp.concatenate(split(s_in[m]), axis=0))

        @pl.when(at_step == 0)
        def _():
            weight_in.wait()

        for copy in chunk_in(m, i):
            copy.wait()
        cot_in(m, 0, i).wait()
        cb[m, i] = (cb[m, i].astype(F32) * valid).astype(BF)
        dbr[...] = nt(cb[m, i], wb[...])
        step = 32
        sum_gn, sum_sk = jnp.zeros((8, width), F32), jnp.zeros((8, width), F32)
        for r in range(0, chunk, step):
            part, at = slice(r, r + step), pl.ds(start + r, step)
            hidden = acc[part, :]
            centred = hidden - jnp.mean(hidden, axis=-1, keepdims=True)
            rstd = lax.rsqrt(jnp.mean(centred * centred, axis=-1, keepdims=True) + EPS)
            exact = centred * rstd
            normed_h = exact.astype(BF).astype(F32)
            gate = zb[m, at, :]
            sig = 1.0 / (1.0 + jnp.exp(-gate))
            gate_act = gate * sig
            act_f = fb[m, 3, at, :].astype(F32)
            mid = normed_h * gn[...] + sk[...] * act_f
            brs[part, :] = (mid * gate_act).astype(BF)
            d_branch = dbr[part, :]
            d_mid = d_branch * gate_act
            dgs[part, :] = (d_branch * mid * (sig + gate_act * (1.0 - sig))).astype(BF)
            sum_gn, sum_sk = sum_gn + folded(d_mid * normed_h), sum_sk + folded(d_mid * act_f)
            four[m, 3, at, :] = d_mid * sk[...]
            d_norm = (d_mid * gn[...]).astype(BF).astype(F32)
            along = jnp.mean(d_norm * exact, axis=-1, keepdims=True)
            d_hid = rstd * (d_norm - jnp.mean(d_norm, axis=-1, keepdims=True) - exact * along)
            dh_high, dh_low = split(d_hid)
            dh2[part, 0:width] = dh_high
            dh2[part, width:] = dh_low
            q2[part, width:] = (d_hid * carried[part]).astype(BF)
        small_o[0:1, :] += jnp.sum(sum_gn, axis=0, keepdims=True)
        small_o[1:2, :] += jnp.sum(sum_sk, axis=0, keepdims=True)
        pb[i, 2 * m] = brs[...]
        pb[i, 2 * m + 1] = dgs[...]
        gd[...] += tn(brs[...], cb[m, i])
        gg[...] += tn(dgs[...], nb[m, own, :])
        ds_o[m] += tn(fb[m, 0, own, :], q2[:, width:])
        acc[...] = carried * nt(dh2[:, 0:width], s_in[m].astype(BF))
        for rel in range(4):

            @pl.when((i ^ h) == rel)
            def _(rel=rel):
                pair_out(m, rel, i).start()

        @pl.when(at_step == 4 * micros - 1)
        def _():
            go[0] = gd[...].astype(BF)
            go[1] = gg[...].astype(BF)
            for copy in grads_out:
                copy.start()

        def attend_back(j, none):
            at = rows_of(j, two)
            d_att = nt(dh2[...], v2[at, :])
            four[m, 2, at, :] += tn(a_high[j], dh2[:, 0:width])
            w_high, w_low = split(decays[j] * d_att * factor)
            acc[...] += mm(w_high, fb[m, 1, at, :]) + mm(w_low, fb[m, 1, at, :])
            four[m, 1, at, :] += tn(w_high, fb[m, 0, own, :]) + tn(w_low, fb[m, 0, own, :])

            @pl.when(i == 3)
            def _():
                key_out(m, j).start()

            return none

        lax.fori_loop(0, i // 2 + 1, attend_back, 0)
        four[m, 0, own, :] = acc[...]
        for copy in rows_out(m, i):
            copy.start()
        sums_o[m, :, own] = lane_sums(acc[...] * fb[m, 0, own, :].astype(F32))
        return none

    lax.fori_loop(0, 4 * micros, one, 0)

    def finish(at_step, none):
        m, at = at_step // 4, rows_of(at_step % 4)
        col_sum = lane_sums(four[m, 1, at, :] * fb[m, 1, at, :].astype(F32))
        held = sums_o[m, :, at]
        sums_o[m, :, at] = jnp.where(iota((8, chunk), 0) == 0, col_sum, held - col_sum)
        return none

    lax.fori_loop(0, 4 * micros, finish, 0)
    for m in range(micros):
        for rel in range(4):
            pair_out(m, rel, rel ^ h).wait()
        for i in range(4):
            for copy in rows_out(m, i):
                copy.wait()
        for copy in (key_out(m, 0), key_out(m, 1)):
            copy.wait()
    for copy in grads_out:
        copy.wait()


def gates_back_kernel(sc, k, v, rows, sums, ds_out, dg_o):
    h, s = sc[0], sc[1]
    span = k.shape[0]
    turned = nt(twice(v[...], 1), jnp.concatenate(split(ds_out[...]), axis=1))
    cross = rows[5:6, :] * lane_sums(turned * k[...].astype(F32))
    r = iota((8, span), 0)
    d_ig = sums[0:1, :] + cross[0:1, :]
    d_cum = sums[1:2, :] - cross[0:1, :]
    running = running_sum(d_cum)
    total = jnp.where(s == 0, 0.0, running[:, span - 1 : span])
    d_fg = rows[3:4, :] * (total - running + d_cum)
    dg_o[...] = jnp.where(r == 2 * h, d_ig, jnp.where(r == 2 * h + 1, d_fg, 0.0))


def twice(v, axis=0):
    return jnp.concatenate([v, v], axis=axis)


def silu_slope(v):
    sig = 1.0 / (1.0 + jnp.exp(-v))
    return sig * (1.0 + v * (1.0 - sig))


def edge_kernel(
    sc, dq, dk, d0, d1, d2, d3, inner, halo, marks, skip_d, gq, gk, wq, wk, cw, cb, dcs_o, ext
):
    to_tiles(ext, 0, halo[...].astype(F32))
    to_tiles(ext, EDGE, inner[...].astype(F32))
    g_all = jnp.concatenate(split(d0[...] + d1[...] + d2[...] + d3[...]), axis=0)
    dq_h, dq_l = split(dq[...] + tn(g_all, twice(gq[...]))[0:EDGE, :])
    dk_h, dk_l = split(dk[...] + tn(g_all, twice(gk[...]))[0:EDGE, :])
    d_act = skip_d[...] + nt(dq_h, wq[...]) + nt(dq_l, wq[...]) + nt(dk_h, wk[...]) + nt(dk_l, wk[...])
    for _, lanes, total, _ in conv_blocks(ext, EDGE, jnp.transpose(marks[...])[0:EDGE, 0:1], cw, cb, EDGE):
        dcs_o[:, lanes] = d_act[:, lanes] * silu_slope(total)


def front_back_kernel(
    sc, d0, d1, d2, d3, rows_t, marks, ds_out, halo, small_i, edge, gq, gk, gv, wq, wk, wv,
    cw, cb, gain, on_map_i, to_lanes_i, four, five, normed, gg_i, w_up, *rest,
):
    i0, i1, i2, i3, late_o = rest[:5]
    fb, qb, nb, bb, wb, ib, ext, nxt, wide, fq, fk, fv, d_act, gi = rest[5:19]
    on_map, to_lanes, gg, small_o, in_sems, out_sems = rest[19:]
    h = sc[0]
    micros, _, span, width = fb.shape
    chunk = d_act.shape[0]

    def inward(m, i):
        at = pl.ds(pl.multiple_of(i * chunk, chunk), chunk)
        return [
            pltpu.make_async_copy(four.at[m, :, at], fb.at[m, :, at], in_sems.at[m, 0, i]),
            pltpu.make_async_copy(five.at[m, :, at], qb.at[m, :, at], in_sems.at[m, 1, i]),
            pltpu.make_async_copy(normed.at[m, at], nb.at[m, at], in_sems.at[m, 2, i]),
        ]

    def before(m, i):
        at = pl.ds(i * chunk - EDGE, EDGE)
        return pltpu.make_async_copy(five.at[m, 4, at], bb.at[m, i], in_sems.at[m, 3, i])

    befores = [before(m, i) for m in range(micros) for i in range(1, 4)]
    consts = [
        pltpu.make_async_copy(on_map_i, on_map, in_sems.at[0, 4, 0]),
        pltpu.make_async_copy(to_lanes_i, to_lanes, in_sems.at[0, 4, 1]),
        pltpu.make_async_copy(gg_i, gg, in_sems.at[0, 4, 2]),
    ]
    for at in range(2):
        columns = pl.ds(pl.multiple_of(at * (w_up.shape[1] // 2) + h * width, width), width)
        to = wb.at[:, pl.ds(at * width, width)]
        consts.append(pltpu.make_async_copy(w_up.at[:, columns], to, in_sems.at[1, 4, at]))
    for copy in (*inward(0, 3), *befores, *inward(0, 2), *inward(0, 1), *inward(0, 0)):
        copy.start()
    small_o[...] = jnp.zeros_like(small_o)
    small_o[41:43, :] += small_i[0:2, :]
    fq[...] = jnp.zeros_like(fq)
    fk[...] = jnp.zeros_like(fk)
    fv[...] = jnp.zeros_like(fv)
    gi[...] = jnp.zeros_like(gi)
    for m in range(micros):
        bb[m, 0] = halo[m]
    for copy in befores:
        copy.wait()

    def inner_out(m, rel, i):
        to = (i0, i1, i2, i3)[rel].at[m]
        return pltpu.make_async_copy(ib.at[m, i], to, out_sems.at[m, rel])

    def one(step, none):
        m, i = step // 4, 3 - step % 4

        @pl.when(i == 3)
        def _():
            to_tiles(nxt, chunk, edge[m])

        @pl.when(step == 1)
        def _():
            for at in (3, 2, 1, 0):
                for copy in inward(1, at):
                    copy.start()
            for copy in consts:
                copy.start()

        start = pl.multiple_of(i * chunk, chunk)
        own = pl.ds(start, chunk)
        for copy in inward(m, i):
            copy.wait()
        to_tiles(ext, 0, bb[m, i].astype(F32))
        to_tiles(ext, EDGE, qb[m, 4, own, :].astype(F32))
        dg = (d0[m, :, own] + d1[m, :, own]) + (d2[m, :, own] + d3[m, :, own])
        g_all = jnp.concatenate(split(dg), axis=0)
        for at in range(3):
            part = mm(g_all, qb[m, at, own, :])
            small_o[8 * at : 8 * at + 8, :] += part[0:8, :] + part[8:16, :]
        order = [dg[r : r + 1, :] for r in (0, 2, 4, 6, 1, 3, 5, 7)]
        small_o[45:46, 0:8] += lane_sums(jnp.concatenate(order, axis=0))[0:1, :]
        state = ds_out[m].astype(BF)
        tail = jnp.transpose(rows_t[m, :, own])[:, 5:6]
        both = jnp.transpose(marks[m, :, own])
        for at, gate in enumerate((gq, gk, gv)):
            total = fb[m, at, own, :] + tn(g_all, twice(gate[...]))
            if at == 1:
                total = total + tail * nt(qb[m, 2, own, :], state)
            if at == 2:
                total = total + tail * mm(qb[m, 1, own, :], state)
            high, low = split(total)
            wide[:, 2 * at * width : (2 * at + 1) * width] = high
            wide[:, (2 * at + 1) * width : (2 * at + 2) * width] = low
        maps = jnp.concatenate([wq[...], wq[...], wk[...], wk[...]], axis=1)
        d_act[...] = fb[m, 3, own, :] + nt(wide[:, 0 : 4 * width], maps)
        sums = [[0.0] * 5 for _ in range(width // LANES)]
        for at, lanes, total, lags in conv_blocks(ext, chunk, both[:, 0:1], cw, cb, 64):
            d_cs = d_act[at, lanes] * silu_slope(total)
            t = lanes.start // LANES
            nxt[t, at, :] = d_cs
            for lag in range(4):
                sums[t][3 - lag] = sums[t][3 - lag] + folded(d_cs * lags[lag])
            sums[t][4] = sums[t][4] + folded(d_cs)
        for t, group in enumerate(sums):
            for at, total in enumerate(group):
                lanes = slice(t * LANES, (t + 1) * LANES)
                small_o[36 + at : 37 + at, lanes] += jnp.sum(total, axis=0, keepdims=True)
        maps = jnp.concatenate([wv[...], wv[...]], axis=1)
        d_act[...] = nt(wide[:, 4 * width :], maps)
        fq[...] += tn(qb[m, 3, own, :], wide[:, 0:width])
        fk[...] += tn(qb[m, 3, own, :], wide[:, 2 * width : 3 * width])
        fv[...] += tn(qb[m, 4, own, :], wide[:, 4 * width : 5 * width])
        for r in range(0, chunk, 64):
            left = jnp.broadcast_to(both[r : r + 64, 1:2], (64, LANES))
            for t in range(width // LANES):
                lanes = slice(t * LANES, (t + 1) * LANES)
                total = d_act[r : r + 64, lanes] + cw[3:4, lanes] * nxt[t, r : r + 64, :]
                for lag in range(1, 4):
                    later = jnp.where(left >= lag, nxt[t, r + lag : r + lag + 64, :], 0.0)
                    total = total + cw[3 - lag : 4 - lag, lanes] * later
                ib[m, i, r : r + 64, lanes] = total.astype(BF)
        for rel in range(4):

            @pl.when((i ^ h) == rel)
            def _(rel=rel):
                inner_out(m, rel, i).start()

        gi[...] += tn(ib[m, i], nb[m, own, :])
        nxt[:, chunk : chunk + EDGE, :] = nxt[:, 0:EDGE, :]
        return none

    lax.fori_loop(0, 4 * micros, one, 0)
    late_o[0:width, :] = gi[...]
    for copy in consts:
        copy.wait()
    ones = (iota((16, width), 1) % 4 == iota((16, width), 0) % 4).astype(BF)
    for at, full in enumerate((fq, fk, fv)):
        high, low = split(full[...] * on_map[...])
        high, low = split(nt(ones, high) + nt(ones, low))
        compact = mm(high, to_lanes[...]) + mm(low, to_lanes[...])
        small_o[24 + 4 * at : 28 + 4 * at, :] += compact[0:4, :]
    both = gi[...] * jnp.transpose(wb[:, 0:width].astype(F32))
    both = both + gg[...].astype(F32) * jnp.transpose(wb[:, width:].astype(F32))
    total = jnp.sum(both, axis=0, keepdims=True) / gain[...]
    small_o[43:44, :] = total[:, 0:width]
    small_o[44:45, :] = total[:, width:]
    late_o[width:, 0:width] = small_o[0 : SMALL // 2, :]
    late_o[width:, width:] = small_o[SMALL // 2 :, :]
    for m in range(micros):
        for rel in range(4):
            inner_out(m, rel, rel ^ h).wait()


def tokens_kernel(seqs, sc, gain, *rest):
    (x_i, c_i), pairs, inners, (w_up, w_dn, out_o, back_o) = rest[:2], rest[2:6], rest[6:10], rest[10:14]
    x, c, ups, downs, acc, mix, dup, brs, sems = rest[14:]
    h = sc[0]
    micros, rows, dim = x.shape
    width = downs.shape[0] // 4
    inner = w_up.shape[1] // 2

    def place(rel, half=0, count=1):
        return pl.ds(pl.multiple_of((count * rel + half) * width, width), width)

    def columns_in(rel, half):
        at = pl.ds(pl.multiple_of(half * inner + (h ^ rel) * width, width), width)
        return pltpu.make_async_copy(w_up.at[:, at], ups.at[:, place(rel, half, 2)], sems.at[half, rel])

    def rows_in(rel):
        return pltpu.make_async_copy(w_dn.at[place(h ^ rel)], downs.at[place(rel)], sems.at[2, rel])

    def inner_in(m, rel, ref):
        to = dup.at[pl.ds(m * rows, rows), place(rel, 0, 2)]
        return pltpu.make_async_copy(ref.at[m], to, sems.at[3 + m, rel])

    def gate_in(m, rel, ref):
        to = dup.at[pl.ds(m * rows, rows), place(rel, 1, 2)]
        return pltpu.make_async_copy(ref.at[2 * m + 1], to, sems.at[5 + m, rel])

    def branch_in(m, rel, ref):
        to = brs.at[pl.ds(m * rows, rows), place(rel)]
        return pltpu.make_async_copy(ref.at[2 * m], to, sems.at[7 + m, rel])

    def first_in(rel, pair):
        return [rows_in(rel)] + [branch_in(m, rel, pair) for m in range(micros)]

    def second_in(rel, pair, ref):
        group = [columns_in(rel, 0), columns_in(rel, 1)]
        for m in range(micros):
            group = group + [inner_in(m, rel, ref), gate_in(m, rel, pair)]
        return group

    tokens_in = [
        pltpu.make_async_copy(x_i, x, sems.at[9, 0]),
        pltpu.make_async_copy(c_i, c, sems.at[9, 1]),
    ]
    for rel in range(4):
        for copy in first_in(rel, pairs[rel]):
            copy.start()
    for rel in range(4):
        for copy in second_in(rel, pairs[rel], inners[rel]):
            copy.start()
    for copy in tokens_in:
        copy.start()
    acc[...] = jnp.zeros_like(acc)
    for rel in range(4):
        for copy in first_in(rel, pairs[0]):
            copy.wait()
    mix[...] = mm(brs[...], downs[...])

    def one(rel, none):
        at = pl.ds(pl.multiple_of(2 * rel * width, 2 * width), 2 * width)
        for copy in second_in(rel, pairs[0], inners[0]):
            copy.wait()
        acc[...] += nt(dup[:, at], ups[:, at])
        return none

    lax.fori_loop(0, 4, one, 0)
    for copy in tokens_in:
        copy.wait()
    step = 128

    def finish(at, none):
        m, r = at // (rows // step), pl.multiple_of(at % (rows // step) * step, step)
        here, both = pl.ds(r, step), pl.ds(pl.multiple_of(at * step, step), step)
        stream = x[m, here, :].astype(F32)
        pos = (sc[1] * 4 + h) * rows + r + iota((step, 1), 0)
        valid = (seg_of(pos, sc, seqs, m) < seqs).astype(F32)
        out_o[m, here, :] = (stream + valid * mix[both, :]).astype(BF)
        centred = stream - jnp.mean(stream, axis=-1, keepdims=True)
        rstd = lax.rsqrt(jnp.mean(centred * centred, axis=-1, keepdims=True) + EPS)
        exact = centred * rstd
        d_n = acc[both, :] * gain[...]
        along = jnp.mean(d_n * exact, axis=-1, keepdims=True)
        d_x = rstd * (d_n - jnp.mean(d_n, axis=-1, keepdims=True) - exact * along)
        back_o[m, here, :] = (c[m, here, :].astype(F32) + d_x).astype(BF)
        return none

    lax.fori_loop(0, micros * rows // step, finish, 0)


def table_kernel(
    sc, t0, t1, t2, t3, gate_o, wq_o, wk_o, wv_o, cw_o, cb_o, gn_o, sk_o, ln_o, ib_o, fb_o, small
):
    heads, _, width = small.shape
    blocks = width // 4
    for rel, ref in enumerate((t0, t1, t2, t3)):
        small[sc[0] ^ rel, 0 : SMALL // 2, :] = ref[:, 0:width]
        small[sc[0] ^ rel, SMALL // 2 :, :] = ref[:, width:]
    for h in range(heads):
        at = slice(h * width, (h + 1) * width)
        for part in range(3):
            start = (part * heads + h) * width
            gate_o[:, start : start + width] = small[h, 8 * part : 8 * part + 8, :]
        cw_o[:, at] = small[h, 36:40, :]
        for row, ref in ((40, cb_o), (41, gn_o), (42, sk_o)):
            ref[at] = small[h, row, :]
    for at, ref in enumerate((wq_o, wk_o, wv_o)):
        rows = slice(24 + 4 * at, 28 + 4 * at)
        for i in range(4):
            lanes = slice(i * blocks, (i + 1) * blocks)
            ref[i] = jnp.concatenate([small[h, rows, lanes] for h in range(heads)], axis=1)
    for half in range(2):
        ln_o[half * width : (half + 1) * width] = sum(small[h, 43 + half, :] for h in range(heads))
    ib_o[...] = small[0, 45, 0:4]
    fb_o[...] = small[0, 45, 4:8]


def whole(shape):
    return pl.BlockSpec(shape, lambda i, sc: (0,) * len(shape))


def by_chunk(rows, width):
    return pl.BlockSpec((rows, width), lambda i, sc: (i, 0))


def head_cols(rows, width, skip=0):
    return pl.BlockSpec((rows, width), lambda i, sc: (0, sc[0] + skip))


def head_rows(rows, width, skip=0):
    return pl.BlockSpec((rows, width), lambda i, sc: (sc[0] + skip, 0))


def of_micro(m, *shape):
    rest = (0,) * len(shape)
    return pl.BlockSpec((None,) + shape, lambda i, sc: (i if m is None else m,) + rest)


def micro_chunk(m, rows, width):
    return pl.BlockSpec((None, rows, width), lambda i, sc: (m, i, 0))


def micro_lanes(m, rows):
    return pl.BlockSpec((None, 8, rows), lambda i, sc: (m, 0, i))


def call(body, grid, in_specs, out_specs, out_shape, scratch, micros_us, args, aliases=None):
    return pl.pallas_call(
        body,
        grid_spec=pltpu.PrefetchScalarGridSpec(
            num_scalar_prefetch=1,
            grid=grid,
            in_specs=in_specs,
            out_specs=out_specs,
            scratch_shapes=scratch,
        ),
        out_shape=[jax.ShapeDtypeStruct(shape, dtype) for shape, dtype in out_shape],
        compiler_params=pltpu.CompilerParams(vmem_limit_bytes=VMEM_BYTES),
        cost_estimate=pl.CostEstimate(
            flops=int(micros_us * 0.05 * 1.15e9), bytes_accessed=1_000_000, transcendentals=0
        ),
        input_output_aliases=aliases or {},
    )(*args)


def together(*groups):
    flat = iter(lax.optimization_barrier([part for group in groups for part in group]))
    return [[next(flat) for _ in group] for group in groups]


def after(value, *others):
    return lax.optimization_barrier((value, *others))[0]


def per_device(
    tokens, lengths, ln_gain, w_up, conv_w, conv_b, w_q, w_k, w_v, gate_w, i_bias, f_bias,
    gn_gain, skip, w_down, cotangent,
):
    micros, rows, dim = tokens.shape
    inner = w_down.shape[0]
    heads = i_bias.shape[0]
    width = inner // heads
    seqs = lengths.shape[2]
    dp, sq, hd = lax.axis_size("dp"), lax.axis_size("seq"), lax.axis_size("head")
    assert hd == heads == 4 and sq == 2 and micros == 2 and conv_w.shape[0] == 4
    ranks = dp * sq
    every = ranks * hd
    span = rows * hd
    h, s = lax.axis_index("head"), lax.axis_index("seq")
    ends = jnp.cumsum(lengths[:, 0], axis=1).astype(jnp.int32)
    sc = jnp.concatenate([jnp.stack([h, s]).astype(jnp.int32), ends.reshape(-1)])

    def across(value, rel):
        return lax.ppermute(value, "head", [(at, at ^ rel) for at in range(hd)])

    def exchange(parts):
        return [parts[0]] + [across(parts[rel], rel) for rel in range(1, hd)]

    def gather(value):
        return exchange([value] * hd)

    def halo_of(parts):
        ends_of = [part[rows - EDGE :] for part in parts]
        last_rows = ends_of[0]
        for rel in range(1, hd):
            last_rows = jnp.where(h == (hd - 1) ^ rel, ends_of[rel], last_rows)
        return lax.ppermute(last_rows, "seq", [(0, 1)])

    xs = [gather(tokens[0])]

    place = s * span + jnp.arange(span, dtype=jnp.int32)[None, :, None]
    past = place >= ends[:, None, :]
    age = place[..., 0] - jnp.max(jnp.where(past, ends[:, None, :], 0), axis=2)
    left = jnp.min(jnp.where(past, 1 << 20, ends[:, None, :]), axis=2) - 1 - place[..., 0]
    marks = jnp.stack([age, left] + [jnp.zeros_like(age)] * 6, axis=1).astype(F32)
    gain = ln_gain.reshape(1, dim)
    cb, gn, sk = conv_b.reshape(1, inner), gn_gain.reshape(1, inner), skip.reshape(1, inner)
    gate_t = gate_w.T

    r, c = jnp.arange(width)[:, None], jnp.arange(width)[None, :]
    on = r // 4 == c // 4
    on_map = on.astype(F32)
    to_lanes = (c == r % 4 * (width // 4) + r // 4).astype(BF)

    def spread(weight):
        mine = lax.dynamic_slice_in_dim(weight, h * (width // 4), width // 4, 0).reshape(width, 4)
        return jnp.where(on, jnp.tile(mine, (1, width // 4)), 0).astype(BF)

    wq, wk, wv = spread(w_q), spread(w_k), spread(w_v)
    consts = [sc, marks, gain, cb, gn, sk, gate_t, wq, wk, wv, on_map, to_lanes]
    xs[0], consts = together(xs[0], consts)
    sc, marks, gain, cb, gn, sk, gate_t, wq, wk, wv, on_map, to_lanes = consts
    x_halo = [halo_of(xs[0])]
    xs.append(gather(after(tokens[1], *xs[0])))
    sq_spec = whole((width, width))
    tiles = pltpu.VMEM((width // LANES, rows + EDGE, LANES), F32)
    dma = pltpu.SemaphoreType.DMA
    gate_specs = [head_cols(8, width, part * heads) for part in range(3)]
    conv_specs = [head_cols(4, width), head_cols(1, width)]
    anywhere = pl.BlockSpec(memory_space=pl.ANY)

    bf_span, f_span = ((micros, span, width), BF), ((micros, span, width), F32)
    block = whole((rows, width))
    big = whole((width, dim))
    lanes = (micros, 8, span)
    front = None
    for m in range(micros):
        args = [sc, *xs[m], x_halo[m], marks, gain, w_up, w_up, conv_w, cb, wq, wk, wv]
        args = args + [gate_t] * 3 + (list(front) if m else [])
        front = call(
            front_kernel,
            (hd,),
            [whole((rows, dim))] * 4
            + [
                whole((EDGE, dim)), micro_lanes(m, rows), whole((1, dim)),
                head_cols(dim, width), head_cols(dim, width, heads), *conv_specs,
            ]
            + [sq_spec] * 3
            + gate_specs
            + [anywhere] * (5 if m else 0),
            [
                micro_chunk(m, rows, dim), micro_chunk(m, rows, width),
                pl.BlockSpec((None, 5, rows, width), partial(lambda m, i, sc: (m, 0, i, 0), m)),
                of_micro(m, EDGE, width),
                micro_lanes(m, rows),
            ],
            [
                ((micros, span, dim), BF), f_span, ((micros, 5, span, width), BF),
                ((micros, EDGE, width), BF), (lanes, F32),
            ],
            [pltpu.VMEM((rows, dim), BF), tiles],
            11,
            args,
            {len(args) - 5 + at: at for at in range(5)} if m else None,
        )
        if m == 0:
            front, xs[1] = together(front, xs[1])
            x_halo.append(halo_of(xs[1]))
            cot = after(cotangent, *xs[1])
            c_parts = [cot, across(cot, 1), across(cot, 2)]
        else:
            front, c_parts = together(front, c_parts)
    normed, gz, five, halo, gate_terms = front
    gates = exchange([gate_terms] * hd)
    def of_five(at, count):
        return pl.BlockSpec((None, None, count, width), lambda i, sc: (i, at, 0, 0))

    lane_spec = of_micro(None, 8, span)
    state_spec = of_micro(None, width, width)
    gates, (c_x, c_y) = together(gates, c_parts[1:])
    c_parts = c_parts + [across(c_x[0], 2), across(c_y[1], 1)]
    state = call(
        partial(gates_kernel, seqs),
        (micros,),
        [pl.BlockSpec(memory_space=pltpu.SMEM)] * 2 + [lane_spec] * 4 + [of_five(1, span), of_five(2, span)],
        [lane_spec, state_spec],
        [(lanes, F32), ((micros, width, width), F32)],
        [],
        7,
        [sc, i_bias, f_bias, *gates, five, five],
    )
    state, c_parts = together(state, c_parts)
    rows_t, states = state
    states_in = lax.ppermute(states, "seq", [(0, 1)])

    *pairs, gd, gg, four, d_states, small_mix, sums = call(
        mix_kernel,
        (1,),
        [whole(lanes), whole((micros, width, width)), head_cols(1, width), head_cols(1, width)]
        + [anywhere] * 9,
        [anywhere] * 7 + [whole((micros, width, width)), whole((8, width)), whole(lanes)],
        [((2 * micros, rows, width), BF)] * 4
        + [((width, dim), BF)] * 2
        + [
            ((micros, 4, span, width), F32), ((micros, width, width), F32), ((8, width), F32),
            (lanes, F32),
        ],
        [
            pltpu.VMEM((micros, 4, span, width), BF),
            pltpu.VMEM((micros, span, width), F32),
            pltpu.VMEM((micros, span, dim), BF),
            pltpu.VMEM((micros, hd, rows, dim), BF),
            pltpu.VMEM((width, dim), BF),
            pltpu.VMEM((hd, 2 * micros, rows, width), BF),
            pltpu.VMEM((micros, 4, span, width), F32),
            pltpu.VMEM((width, dim), F32),
            pltpu.VMEM((width, dim), F32),
            pltpu.VMEM((2, width, dim), BF),
            pltpu.VMEM((rows, width), F32),
            pltpu.VMEM((hd // 2, rows, 2 * rows), BF),
            pltpu.VMEM((hd // 2, rows, 2 * rows), F32),
            pltpu.VMEM((rows, 2 * width), BF),
            pltpu.VMEM((span, 2 * width), BF),
            pltpu.VMEM((rows, 2 * width), BF),
            pltpu.VMEM((rows, width), F32),
            pltpu.VMEM((rows, width), BF),
            pltpu.VMEM((rows, width), BF),
            dma((micros, 6, 4)),
            dma((micros, 5, 4)),
        ],
        45,
        [sc, rows_t, states_in, gn, sk, five, gz, normed, *c_parts, w_down],
    )
    d_states = lax.ppermute(d_states, "seq", [(1, 0)])
    d_gates = call(
        gates_back_kernel,
        (micros,),
        [of_five(1, span), of_five(2, span), lane_spec, lane_spec, state_spec],
        [lane_spec],
        [(lanes, F32)],
        [],
        8,
        [sc, five, five, rows_t, sums, d_states],
    )[0]
    d_gates = exchange([d_gates] * hd)

    half_w, down_w = inner // every, inner // every
    early = [gg.reshape(ranks, half_w, dim), gd.reshape(ranks, down_w, dim)]
    early = lax.all_to_all(
        jnp.concatenate(early, axis=1), ("dp", "seq"), split_axis=0, concat_axis=0, tiled=True
    )
    pairs = exchange([after(part, *d_gates) for part in pairs])

    top = of_micro(None, EDGE, width)

    def of_four(at):
        return pl.BlockSpec((None, None, EDGE, width), lambda i, sc: (i, at, 0, 0))

    edges = call(
        edge_kernel,
        (micros,),
        [of_four(0), of_four(1)]
        + [of_micro(None, 8, 128)] * 4
        + [of_five(4, EDGE), top, of_micro(None, 8, 128), of_four(3)]
        + gate_specs[:2]
        + [sq_spec, sq_spec, *conv_specs],
        [top],
        [((micros, EDGE, width), F32)],
        [pltpu.VMEM((width // LANES, 2 * EDGE, LANES), F32)],
        4,
        [sc, four, four, *d_gates, five, halo, marks, four, gate_t, gate_t, wq, wk, conv_w, cb],
    )[0]
    edges = lax.ppermute(edges, "seq", [(1, 0)])
    axes = ("dp", "seq", "head")
    *d_inners, late = call(
        front_back_kernel,
        (1,),
        [whole(lanes)] * 6
        + [
            whole((micros, width, width)), whole((micros, EDGE, width)), whole((8, width)),
            whole((micros, EDGE, width)),
        ]
        + gate_specs
        + [sq_spec] * 3
        + conv_specs
        + [whole((1, dim))]
        + [anywhere] * 7,
        [anywhere] * 4 + [whole((width + SMALL // 2, dim))],
        [((micros, rows, width), BF)] * 4 + [((width + SMALL // 2, dim), F32)],
        [
            pltpu.VMEM((micros, 4, span, width), F32),
            pltpu.VMEM((micros, 5, span, width), BF),
            pltpu.VMEM((micros, span, dim), BF),
            pltpu.VMEM((micros, hd, EDGE, width), BF),
            pltpu.VMEM((dim, 2 * width), BF),
            pltpu.VMEM((micros, hd, rows, width), BF),
            tiles,
            tiles,
            pltpu.VMEM((rows, 6 * width), BF),
            *[pltpu.VMEM((width, width), F32)] * 3,
            pltpu.VMEM((rows, width), F32),
            pltpu.VMEM((width, dim), F32),
            pltpu.VMEM((width, width), F32),
            pltpu.VMEM((width, width), BF),
            pltpu.VMEM((width, dim), BF),
            pltpu.VMEM((SMALL, width), F32),
            dma((micros, 5, 4)),
            dma((micros, 4)),
        ],
        28,
        [
            sc, *d_gates, rows_t, marks, d_states, halo, small_mix, edges, gate_t, gate_t, gate_t,
            wq, wk, wv, conv_w, cb, gain, on_map, to_lanes, four, five, normed, gg, w_up,
        ],
    )
    (late, *d_inners), pairs = together([late, *d_inners], pairs)
    d_inners = exchange(d_inners)

    late = late + lax.ppermute(late, "seq", [(0, 1), (1, 0)])
    small = late[width:]
    blocks = late[:width].reshape(dp, 2 * half_w, dim)
    d = lax.axis_index("dp")
    if dp == 4:
        high = lax.reduce_precision(small, 8, 7)
        table = jnp.concatenate([high.astype(BF), (small - high).astype(BF)], axis=0)

        def to_plane(rel):
            block = lax.dynamic_index_in_dim(blocks, d ^ rel, 0, keepdims=False).astype(BF)
            block = jnp.concatenate([block, table], axis=0)
            if rel == 0:
                return block
            pairs_of = [(a * sq + 1, (a ^ rel) * sq + 1) for a in range(dp)]
            return lax.ppermute(block, ("dp", "seq"), pairs_of)

        terms = [to_plane(rel).astype(F32) for rel in range(dp)]
        terms = (terms[0] + terms[1]) + (terms[2] + terms[3])
        g_inner, small = terms[: 2 * half_w], terms[2 * half_w :]
        small = small[: SMALL // 2] + small[SMALL // 2 :]
        small = jnp.where(s == 1, small, lax.ppermute(small, "seq", [(1, 0)]))
    else:
        small = lax.psum(small, "dp")
        terms = lax.all_to_all(blocks.astype(BF), "dp", split_axis=0, concat_axis=0, tiled=True)
        g_inner = jnp.sum(terms.astype(F32), axis=0)
    early = jnp.sum(early.astype(F32), axis=0)
    g_gate, g_down = early[:half_w], early[half_w:]
    g_gate = jnp.concatenate([g_gate, lax.ppermute(g_gate, "seq", [(1, 0)])], axis=0)
    up_pairs, down_pairs = [], []
    for rank in range(ranks):
        for at in range(hd):
            block_at = at * dp + rank // 2 + (0 if rank % 2 else every // 2)
            up_pairs.append((rank * hd + at, block_at))
            down_pairs.append((rank * hd + at, at * ranks + rank))
    g_down = lax.ppermute(g_down, axes, down_pairs)
    g_up = jnp.where(s == 0, g_gate, g_inner)
    d_inners, (small, g_up) = together(d_inners, [small, g_up])
    g_up = lax.ppermute(g_up, axes, up_pairs).T

    token_spec = whole(tokens.shape)
    block_out, d_tokens = call(
        partial(tokens_kernel, seqs),
        (1,),
        [whole((1, dim))] + [anywhere] * 12,
        [token_spec] * 2,
        [(tokens.shape, BF)] * 2,
        [
            pltpu.VMEM(tokens.shape, BF),
            pltpu.VMEM(tokens.shape, BF),
            pltpu.VMEM((dim, 2 * inner), BF),
            pltpu.VMEM((inner, dim), BF),
            pltpu.VMEM((micros * rows, dim), F32),
            pltpu.VMEM((micros * rows, dim), F32),
            pltpu.VMEM((micros * rows, 2 * inner), BF),
            pltpu.VMEM((micros * rows, inner), BF),
            dma((10, hd)),
        ],
        10,
        [sc, gain, tokens, cotangent, *pairs, *d_inners, w_up, w_down],
    )

    (block_out, d_tokens), (small,) = together([block_out, d_tokens], [small])
    table = gather(small)
    flat = [((8, 3 * inner), F32), *[((4, 4, inner // 4), F32)] * 3, ((4, inner), F32)]
    flat = flat + [((inner,), F32)] * 3 + [((dim,), F32)] + [((heads,), F32)] * 2
    g_gate, g_wq, g_wk, g_wv, g_cw, g_cb, g_gn, g_sk, g_ln, g_ib, g_fb = call(
        table_kernel,
        (1,),
        [whole(small.shape)] * 4,
        [whole(shape) for shape, _ in flat],
        flat,
        [pltpu.VMEM((hd, SMALL, width), F32)],
        3,
        [sc, *table],
    )
    maps = [part.transpose(2, 0, 1) for part in (g_wq, g_wk, g_wv)]
    return (
        block_out, d_tokens, g_ln, g_up, g_cw, g_cb, *maps, g_gate.T, g_ib, g_fb, g_gn, g_sk, g_down,
    )


def solution(mesh):
    rows = P(None, ("dp", "seq", "head"), None)
    placed = (rows, P(None, "dp", None), *[P()] * 13, rows)
    outs = (rows, rows, P(), P(None, ("dp", "seq", "head")), *[P()] * 10, P(("dp", "seq", "head"), None))
    return jax.shard_map(per_device, mesh=mesh, in_specs=placed, out_specs=outs, check_vma=False)
```

```python
from functools import partial

import jax
import jax.numpy as jnp
from jax import lax
from jax.experimental import pallas as pl
from jax.experimental.pallas import tpu as pltpu
from jax.sharding import PartitionSpec as P

EPS = 1e-05
HIGH = lax.Precision.HIGHEST
BF = jnp.bfloat16
F32 = jnp.float32
EDGE = 16
SMALL = 48
NEVER = -1e30
VMEM_BYTES = 52 * 1024 * 1024


def mm(a, b):
    return lax.dot_general(a, b, (((1,), (0,)), ((), ())), preferred_element_type=F32)


def nt(a, b):
    return lax.dot_general(a, b, (((1,), (1,)), ((), ())), preferred_element_type=F32)


def tn(a, b):
    return lax.dot_general(a, b, (((0,), (0,)), ((), ())), preferred_element_type=F32)


def split(v):
    high = v.astype(BF)
    return high, (v - high.astype(F32)).astype(BF)


def iota(shape, dim):
    return lax.broadcasted_iota(jnp.int32, shape, dim)


def seg_of(pos, sc, seqs, m):
    total = (pos >= sc[2 + m * seqs]).astype(jnp.int32)
    for e in range(1, seqs):
        total = total + (pos >= sc[2 + m * seqs + e]).astype(jnp.int32)
    return total


def pick(refs, which, dest, rows):
    for at, ref in enumerate(refs):

        @pl.when(which == at)
        def _(ref=ref):
            dest[...] = ref[rows, :]


def put(refs, which, value):
    for at, ref in enumerate(refs):

        @pl.when(which == at)
        def _(ref=ref):
            ref[...] = value


def lane_sums(v):
    ones = jnp.ones((8, v.shape[1]), BF)
    high, low = split(v)
    return nt(ones, high) + nt(ones, low)


def running_sum(v):
    width = v.shape[1] // 8
    tri = (iota((width, width), 0) <= iota((width, width), 1)).astype(BF)
    chunks = jnp.concatenate([v[:, c * width : (c + 1) * width] for c in range(8)], axis=0)
    high, rest = split(chunks)
    rest = chunks - high.astype(F32)
    mid, low = split(rest)
    within = mm(high, tri) + (mm(mid, tri) + mm(low, tri))
    carry, parts = jnp.zeros((1, 1), F32), []
    for c in range(8):
        parts.append(within[c : c + 1, :] + carry)
        carry = carry + within[c : c + 1, width - 1 : width]
    return jnp.concatenate(parts, axis=1)


LANES = 128


def to_tiles(ext, start, value):
    rows, width = value.shape
    for t in range(width // LANES):
        ext[t, start : start + rows, :] = value[:, t * LANES : (t + 1) * LANES]


def conv_blocks(ext, rows, ages, cw, cb, step):
    for r in range(0, rows, step):
        age = jnp.broadcast_to(ages[r : r + step], (step, LANES))
        for t in range(ext.shape[0]):
            lanes = slice(t * LANES, (t + 1) * LANES)
            lags = [ext[t, EDGE + r : EDGE + r + step, :]]
            for lag in range(1, 4):
                earlier = ext[t, EDGE + r - lag : EDGE + r - lag + step, :]
                lags.append(jnp.where(age >= lag, earlier, 0.0))
            total = cb[:, lanes] + cw[3:4, lanes] * lags[0]
            for lag in range(1, 4):
                total = total + cw[3 - lag : 4 - lag, lanes] * lags[lag]
            yield slice(r, r + step), lanes, total, lags


def folded(v):
    return sum(v[e : e + 8] for e in range(8, v.shape[0], 8)) + v[0:8]


def front_kernel(
    sc, x0, x1, x2, x3a, x3b, xh, marks, gain, w_in, w_gt, cw, cb, wq, wk, wv, gq, gk, gv, *rest
):
    normed_o, gz_o, five_o, halo_o, gt_o, xs, ext = rest[-7:]
    m, i = pl.program_id(0) // 4, pl.program_id(0) % 4
    chunk = xs.shape[0]
    rel = i ^ sc[0]
    pick((x0, x1, x2, x3a, x3b), jnp.where((rel == 3) & (m == 1), 4, rel), xs, slice(0, chunk))

    def norm(rows):
        stream = rows.astype(F32)
        centred = stream - jnp.mean(stream, axis=-1, keepdims=True)
        variance = jnp.mean(centred * centred, axis=-1, keepdims=True)
        return (centred * lax.rsqrt(variance + EPS) * gain[...]).astype(BF)

    @pl.when(i == 0)
    def _():
        edge = mm(norm(xh[...]), w_in[...]).astype(BF)
        to_tiles(ext, 0, edge.astype(F32))
        halo_o[...] = edge

    @pl.when(i > 0)
    def _():
        ext[:, 0:EDGE, :] = ext[:, chunk : chunk + EDGE, :]

    for r in range(0, chunk, 32):
        normed_o[r : r + 32, :] = norm(xs[r : r + 32, :])
    inner = mm(normed_o[...], w_in[...]).astype(BF)
    five_o[4] = inner
    to_tiles(ext, EDGE, inner.astype(F32))
    gz_o[...] = mm(normed_o[...], w_gt[...])
    ages = jnp.transpose(marks[...])[:, 0:1]
    for rows, lanes, total, _ in conv_blocks(ext, chunk, ages, cw, cb, 64):
        five_o[3, rows, lanes] = (total / (1.0 + jnp.exp(-total))).astype(BF)
    q = mm(five_o[3], wq[...]).astype(BF)
    k = mm(five_o[3], wk[...]).astype(BF)
    v = mm(five_o[4], wv[...]).astype(BF)
    five_o[0] = q
    five_o[1] = k
    five_o[2] = v
    gt_o[...] = nt(gq[...], q) + nt(gk[...], k) + nt(gv[...], v)


def gates_kernel(seqs, sc, ib, fb, g0, g1, g2, g3, k, v, rows_o, s_o):
    m = pl.program_id(0)
    h, s = sc[0], sc[1]
    span, width = k.shape
    factor = width ** (-0.5)
    lin = ((g0[...] + g1[m]) + (g2[m] + g3[m])).astype(BF).astype(F32)
    r = iota(lin.shape, 0)
    ig = jnp.sum(jnp.where(r == 2 * h, lin, 0.0), axis=0, keepdims=True) + ib[h]
    fg = jnp.sum(jnp.where(r == 2 * h + 1, lin, 0.0), axis=0, keepdims=True) + fb[h]
    pos = s * span + iota((1, span), 1)
    seg = seg_of(pos, sc, seqs, m)
    valid = (seg < seqs).astype(F32)
    log_keep = valid * (jnp.minimum(fg, 0.0) - jnp.log1p(jnp.exp(-jnp.abs(fg))))
    cum = running_sum(log_keep)
    prev = jnp.where(s == 0, -1, seg_of(s * span - 1, sc, seqs, m))
    last = seg_of(s * span + span - 1, sc, seqs, m)
    carried = jnp.where(seg == prev, jnp.exp(cum), 0.0)
    offset = jnp.where(seg < seqs, ig - cum, NEVER)
    tail = jnp.exp(jnp.where(seg == last, cum[:, span - 1 : span] + offset, NEVER)) * factor
    slope = valid / (1.0 + jnp.exp(fg))
    rows = jnp.zeros((8, span), F32)
    for at, row in enumerate((cum, offset, seg.astype(F32), slope, carried, tail, valid)):
        rows = jnp.where(r == at, row, rows)
    rows_o[...] = rows
    cols = jnp.transpose(rows)
    high, low = split(k[...].astype(F32) * cols[:, 5:6])
    s_o[...] = tn(high, v[...]) + tn(low, v[...])


def mix_kernel(
    sc, rows, s_in, gn, sk, five, gz, normed, c0, c1, c2, c3a, c3b, w_dn, *rest
):
    p0, p1, p2, p3, gd_o, gg_o, both_o, four_o, ds_o, small_o, sums_o = rest[:11]
    fb, zb, nb, cb, wb, pb, four, gd, gg, go, acc, a_high, decays = rest[11:24]
    q2, v2, dh2, dbr, brs, dgs, in_sems, out_sems, pack_sems = rest[24:]
    h = sc[0]
    micros, _, span, width = fb.shape
    chunk = acc.shape[0]
    two = 2 * chunk
    factor = width ** (-0.5)

    def rows_of(i, size=chunk):
        return pl.ds(pl.multiple_of(i * size, size), size)

    def qkv_in(m, j):
        at, three = rows_of(j, two), pl.ds(0, 3)
        to = fb.at[m, three, at]
        return pltpu.make_async_copy(five.at[m, three, at], to, in_sems.at[m, 0, j])

    def chunk_in(m, i):
        at = rows_of(i)
        return [
            pltpu.make_async_copy(five.at[m, 3, at], fb.at[m, 3, at], in_sems.at[m, 1, i]),
            pltpu.make_async_copy(gz.at[m, at], zb.at[m, at], in_sems.at[m, 2, i]),
            pltpu.make_async_copy(normed.at[m, at], nb.at[m, at], in_sems.at[m, 3, i]),
        ]

    def cot_in(m, rel, i, last=False):
        ref = (c0.at[m], c1.at[m], c2.at[m], c3b if last else c3a)[rel]
        return pltpu.make_async_copy(ref, cb.at[m, i], in_sems.at[m, 4, i])

    weight_in = pltpu.make_async_copy(w_dn.at[rows_of(h, width)], wb, in_sems.at[0, 5, 0])

    def others_in(m, last):
        for rel in range(4):
            cot_in(m, rel, rel ^ h, last).start()
        for copy in (*chunk_in(m, 1), qkv_in(m, 1), *chunk_in(m, 2), *chunk_in(m, 3)):
            copy.start()

    for copy in (qkv_in(0, 0), weight_in, *chunk_in(0, 0)):
        copy.start()
    others_in(0, False)
    small_o[...] = jnp.zeros_like(small_o)
    gd[...] = jnp.zeros_like(gd)
    gg[...] = jnp.zeros_like(gg)

    def pair_out(m, rel, i):
        at = pl.ds(2 * m, 2)
        to = (p0, p1, p2, p3)[rel].at[at]
        return pltpu.make_async_copy(pb.at[i, at], to, out_sems.at[m, 0, rel])

    def rows_out(m, i):
        at = rows_of(i)
        return [
            pltpu.make_async_copy(four.at[m, 0, at], four_o.at[m, 0, at], out_sems.at[m, 1, i]),
            pltpu.make_async_copy(four.at[m, 3, at], four_o.at[m, 3, at], out_sems.at[m, 2, i]),
        ]

    def key_out(m, j):
        at, pair = rows_of(j, two), pl.ds(1, 2)
        to = four_o.at[m, pair, at]
        return pltpu.make_async_copy(four.at[m, pair, at], to, out_sems.at[m, 3, j])

    grads_out = [
        pltpu.make_async_copy(go.at[0], gd_o, out_sems.at[0, 4, 0]),
        pltpu.make_async_copy(go.at[1], gg_o, out_sems.at[0, 4, 1]),
    ]
    ranks, piece = both_o.shape[0], both_o.shape[1] // 2
    if piece % EDGE == 0:
        grads_out = grads_out[1:]
        for r in range(ranks):
            for at, which in enumerate((1, 0)):
                to = both_o.at[r, pl.ds(at * piece, piece)]
                rows_r = go.at[which, pl.ds(r * piece, piece)]
                grads_out.append(pltpu.make_async_copy(rows_r, to, pack_sems.at[at, r]))

    def one(at_step, none):
        m, i = at_step // 4, at_step % 4

        @pl.when(i == 0)
        def _():
            four[m, 1] = jnp.zeros((span, width), F32)
            four[m, 2] = jnp.zeros((span, width), F32)
            ds_o[m] = jnp.zeros((width, width), F32)

        @pl.when(at_step == 1)
        def _():
            for copy in (qkv_in(1, 0), *chunk_in(1, 0)):
                copy.start()
            others_in(1, True)

        start = pl.multiple_of(i * chunk, chunk)
        own = pl.ds(start, chunk)

        @pl.when(i % 2 == 0)
        def _():
            at = rows_of(i // 2, two)
            qkv_in(m, i // 2).wait()
            v2[at, 0:width] = fb[m, 2, at, :]
            v2[at, width:] = fb[m, 2, at, :]

        @pl.when(at_step == 0)
        def _():
            weight_in.wait()

        for copy in chunk_in(m, i):
            copy.wait()
        cot_in(m, 0, i).wait()
        here = start + iota((chunk, 1), 0)
        cols = jnp.transpose(rows[m, :, own])
        cum, seg, carried, valid = cols[:, 0:1], cols[:, 2:3], cols[:, 4:5], cols[:, 6:7]

        def attend(j):
            at = slice(j * two, (j + 1) * two)
            scores = nt(fb[m, 0, own, :], fb[m, 1, at, :]) * factor
            allowed = (seg == rows[m, 2:3, at]) & (j * two + iota((1, two), 1) <= here)
            decay = jnp.exp(jnp.where(allowed, cum + rows[m, 1:2, at], NEVER))
            decays[j] = decay
            high, low = split(scores * decay)
            a_high[j] = high
            return mm(high, fb[m, 2, at, :]) + mm(low, fb[m, 2, at, :])

        q2[:, 0:width] = fb[m, 0, own, :]
        q2[:, width:] = fb[m, 0, own, :]
        state = jnp.concatenate(split(s_in[m]), axis=0)
        acc[...] = attend(0) + carried * mm(q2[...], state)

        cb[m, i] = (cb[m, i].astype(F32) * valid).astype(BF)
        dbr[...] = nt(cb[m, i], wb[...])

        @pl.when(i >= 2)
        def _():
            acc[...] += attend(1)

        step = 32
        sum_gn, sum_sk = jnp.zeros((8, width), F32), jnp.zeros((8, width), F32)
        for r in range(0, chunk, step):
            part, at = slice(r, r + step), pl.ds(start + r, step)
            hidden = acc[part, :]
            centred = hidden - jnp.mean(hidden, axis=-1, keepdims=True)
            rstd = lax.rsqrt(jnp.mean(centred * centred, axis=-1, keepdims=True) + EPS)
            exact = centred * rstd
            normed_h = exact.astype(BF).astype(F32)
            gate = zb[m, at, :]
            sig = 1.0 / (1.0 + jnp.exp(-gate))
            gate_act = gate * sig
            act_f = fb[m, 3, at, :].astype(F32)
            mid = normed_h * gn[...] + sk[...] * act_f
            brs[part, :] = (mid * gate_act).astype(BF)
            d_branch = dbr[part, :]
            d_mid = d_branch * gate_act
            dgs[part, :] = (d_branch * mid * (sig + gate_act * (1.0 - sig))).astype(BF)
            sum_gn, sum_sk = sum_gn + folded(d_mid * normed_h), sum_sk + folded(d_mid * act_f)
            four[m, 3, at, :] = d_mid * sk[...]
            d_norm = (d_mid * gn[...]).astype(BF).astype(F32)
            along = jnp.mean(d_norm * exact, axis=-1, keepdims=True)
            d_hid = rstd * (d_norm - jnp.mean(d_norm, axis=-1, keepdims=True) - exact * along)
            dh_high, dh_low = split(d_hid)
            dh2[part, 0:width] = dh_high
            dh2[part, width:] = dh_low
            q2[part, width:] = (d_hid * carried[part]).astype(BF)
        small_o[0:1, :] += jnp.sum(sum_gn, axis=0, keepdims=True)
        small_o[1:2, :] += jnp.sum(sum_sk, axis=0, keepdims=True)
        pb[i, 2 * m] = brs[...]
        pb[i, 2 * m + 1] = dgs[...]
        gd[...] += tn(brs[...], cb[m, i])
        gg[...] += tn(dgs[...], nb[m, own, :])
        ds_o[m] += tn(fb[m, 0, own, :], q2[:, width:])
        acc[...] = carried * nt(dh2[:, 0:width], s_in[m].astype(BF))
        def attend_back(j):
            at = slice(j * two, (j + 1) * two)
            d_att = nt(dh2[...], v2[at, :])
            four[m, 2, at, :] += tn(a_high[j], dh2[:, 0:width])
            w_high, w_low = split(decays[j] * d_att * factor)
            four[m, 1, at, :] += tn(w_high, fb[m, 0, own, :]) + tn(w_low, fb[m, 0, own, :])
            return mm(w_high, fb[m, 1, at, :]) + mm(w_low, fb[m, 1, at, :])

        acc[...] += attend_back(0)
        for rel in range(4):

            @pl.when((i ^ h) == rel)
            def _(rel=rel):
                pair_out(m, rel, i).start()

        @pl.when(at_step == 4 * micros - 1)
        def _():
            go[0] = gd[...].astype(BF)
            go[1] = gg[...].astype(BF)
            for copy in grads_out:
                copy.start()

        @pl.when(i == 3)
        def _():
            key_out(m, 0).start()

        @pl.when(i >= 2)
        def _():
            acc[...] += attend_back(1)

        @pl.when(i == 3)
        def _():
            key_out(m, 1).start()

        four[m, 0, own, :] = acc[...]
        for copy in rows_out(m, i):
            copy.start()
        sums_o[m, :, own] = lane_sums(acc[...] * fb[m, 0, own, :].astype(F32))
        return none

    lax.fori_loop(0, 4 * micros, one, 0)

    def finish(at_step, none):
        m, at = at_step // 4, rows_of(at_step % 4)
        col_sum = lane_sums(four[m, 1, at, :] * fb[m, 1, at, :].astype(F32))
        held = sums_o[m, :, at]
        sums_o[m, :, at] = jnp.where(iota((8, chunk), 0) == 0, col_sum, held - col_sum)
        return none

    lax.fori_loop(0, 4 * micros, finish, 0)
    for m in range(micros):
        for rel in range(4):
            pair_out(m, rel, rel ^ h).wait()
        for i in range(4):
            for copy in rows_out(m, i):
                copy.wait()
        for copy in (key_out(m, 0), key_out(m, 1)):
            copy.wait()
    for copy in grads_out:
        copy.wait()


def gates_back_kernel(sc, k, v, rows, sums, ds_out, dg_o):
    h, s = sc[0], sc[1]
    span = k.shape[0]
    turned = nt(twice(v[...], 1), jnp.concatenate(split(ds_out[pl.program_id(0)]), axis=1))
    cross = rows[5:6, :] * lane_sums(turned * k[...].astype(F32))
    r = iota((8, span), 0)
    d_ig = sums[0:1, :] + cross[0:1, :]
    d_cum = sums[1:2, :] - cross[0:1, :]
    running = running_sum(d_cum)
    total = jnp.where(s == 0, 0.0, running[:, span - 1 : span])
    d_fg = rows[3:4, :] * (total - running + d_cum)
    dg_o[...] = jnp.where(r == 2 * h, d_ig, jnp.where(r == 2 * h + 1, d_fg, 0.0))


def twice(v, axis=0):
    return jnp.concatenate([v, v], axis=axis)


def silu_slope(v):
    sig = 1.0 / (1.0 + jnp.exp(-v))
    return sig * (1.0 + v * (1.0 - sig))


def edge_kernel(
    sc, dq, dk, d0, d1, d2, d3, inner, halo, marks, skip_d, gq, gk, wq, wk, cw, cb, dcs_o, ext
):
    to_tiles(ext, 0, halo[...].astype(F32))
    to_tiles(ext, EDGE, inner[...].astype(F32))
    m, at = pl.program_id(0), slice(0, 128)
    total = (d0[m, :, at] + d1[m, :, at]) + (d2[m, :, at] + d3[m, :, at])
    g_all = jnp.concatenate(split(total), axis=0)
    dq_h, dq_l = split(dq[...] + tn(g_all, twice(gq[...]))[0:EDGE, :])
    dk_h, dk_l = split(dk[...] + tn(g_all, twice(gk[...]))[0:EDGE, :])
    d_act = skip_d[...] + nt(dq_h, wq[...]) + nt(dq_l, wq[...]) + nt(dk_h, wk[...]) + nt(dk_l, wk[...])
    for _, lanes, total, _ in conv_blocks(ext, EDGE, jnp.transpose(marks[...])[0:EDGE, 0:1], cw, cb, EDGE):
        dcs_o[:, lanes] = d_act[:, lanes] * silu_slope(total)


def front_back_kernel(
    sc, d0, d1, d2, d3, rows_t, marks, ds_out, halo, small_i, edge, gq, gk, gv, wq, wk, wv,
    cw, cb, gain, on_map_i, to_lanes_i, four, five, normed, gg_i, w_up, *rest,
):
    i0, i1, i2, i3, late_o = rest[:5]
    fb, qb, nb, bb, wb, ib, ext, nxt, wide, fq, fk, fv, d_act, gi = rest[5:19]
    on_map, to_lanes, gg, small_o, in_sems, out_sems = rest[19:]
    h = sc[0]
    micros, _, span, width = fb.shape
    chunk = d_act.shape[0]

    def inward(m, i):
        at = pl.ds(pl.multiple_of(i * chunk, chunk), chunk)
        return [
            pltpu.make_async_copy(four.at[m, :, at], fb.at[m, :, at], in_sems.at[m, 0, i]),
            pltpu.make_async_copy(five.at[m, :, at], qb.at[m, :, at], in_sems.at[m, 1, i]),
            pltpu.make_async_copy(normed.at[m, at], nb.at[m, at], in_sems.at[m, 2, i]),
        ]

    def before(m, i):
        at = pl.ds(i * chunk - EDGE, EDGE)
        return pltpu.make_async_copy(five.at[m, 4, at], bb.at[m, i], in_sems.at[m, 3, i])

    befores = [before(m, i) for m in range(micros) for i in range(1, 4)]
    consts = [
        pltpu.make_async_copy(on_map_i, on_map, in_sems.at[0, 4, 0]),
        pltpu.make_async_copy(to_lanes_i, to_lanes, in_sems.at[0, 4, 1]),
        pltpu.make_async_copy(gg_i, gg, in_sems.at[0, 4, 2]),
    ]
    for at in range(2):
        columns = pl.ds(pl.multiple_of(at * (w_up.shape[1] // 2) + h * width, width), width)
        to = wb.at[:, pl.ds(at * width, width)]
        consts.append(pltpu.make_async_copy(w_up.at[:, columns], to, in_sems.at[1, 4, at]))
    for copy in (*inward(0, 3), *befores, *inward(0, 2), *inward(0, 1), *inward(0, 0)):
        copy.start()
    small_o[...] = jnp.zeros_like(small_o)
    small_o[41:43, :] += small_i[0:2, :]
    fq[...] = jnp.zeros_like(fq)
    fk[...] = jnp.zeros_like(fk)
    fv[...] = jnp.zeros_like(fv)
    gi[...] = jnp.zeros_like(gi)
    for m in range(micros):
        bb[m, 0] = halo[m]
    for copy in befores:
        copy.wait()

    def inner_out(m, rel, i):
        to = (i0, i1, i2, i3)[rel].at[m]
        return pltpu.make_async_copy(ib.at[m, i], to, out_sems.at[m, rel])

    def one(step, none):
        m, i = step // 4, 3 - step % 4

        @pl.when(i == 3)
        def _():
            to_tiles(nxt, chunk, edge[m])

        @pl.when(step == 1)
        def _():
            for at in (3, 2, 1, 0):
                for copy in inward(1, at):
                    copy.start()
            for copy in consts:
                copy.start()

        start = pl.multiple_of(i * chunk, chunk)
        own = pl.ds(start, chunk)
        for copy in inward(m, i):
            copy.wait()
        to_tiles(ext, 0, bb[m, i].astype(F32))
        to_tiles(ext, EDGE, qb[m, 4, own, :].astype(F32))
        dg = (d0[m, :, own] + d1[m, :, own]) + (d2[m, :, own] + d3[m, :, own])
        g_all = jnp.concatenate(split(dg), axis=0)
        for at in range(3):
            part = mm(g_all, qb[m, at, own, :])
            small_o[8 * at : 8 * at + 8, :] += part[0:8, :] + part[8:16, :]
        order = [dg[r : r + 1, :] for r in (0, 2, 4, 6, 1, 3, 5, 7)]
        small_o[45:46, 0:8] += lane_sums(jnp.concatenate(order, axis=0))[0:1, :]
        state = ds_out[m].astype(BF)
        tail = jnp.transpose(rows_t[m, :, own])[:, 5:6]
        both = jnp.transpose(marks[m, :, own])
        for at, gate in enumerate((gq, gk, gv)):
            total = fb[m, at, own, :] + tn(g_all, twice(gate[...]))
            if at == 1:
                total = total + tail * nt(qb[m, 2, own, :], state)
            if at == 2:
                total = total + tail * mm(qb[m, 1, own, :], state)
            high, low = split(total)
            wide[:, 2 * at * width : (2 * at + 1) * width] = high
            wide[:, (2 * at + 1) * width : (2 * at + 2) * width] = low
        maps = jnp.concatenate([wq[...], wq[...], wk[...], wk[...]], axis=1)
        d_act[...] = fb[m, 3, own, :] + nt(wide[:, 0 : 4 * width], maps)
        sums = [[0.0] * 5 for _ in range(width // LANES)]
        for at, lanes, total, lags in conv_blocks(ext, chunk, both[:, 0:1], cw, cb, 64):
            d_cs = d_act[at, lanes] * silu_slope(total)
            t = lanes.start // LANES
            nxt[t, at, :] = d_cs
            for lag in range(4):
                sums[t][3 - lag] = sums[t][3 - lag] + folded(d_cs * lags[lag])
            sums[t][4] = sums[t][4] + folded(d_cs)
        for t, group in enumerate(sums):
            for at, total in enumerate(group):
                lanes = slice(t * LANES, (t + 1) * LANES)
                small_o[36 + at : 37 + at, lanes] += jnp.sum(total, axis=0, keepdims=True)
        maps = jnp.concatenate([wv[...], wv[...]], axis=1)
        d_act[...] = nt(wide[:, 4 * width :], maps)
        fq[...] += tn(qb[m, 3, own, :], wide[:, 0:width])
        fk[...] += tn(qb[m, 3, own, :], wide[:, 2 * width : 3 * width])
        fv[...] += tn(qb[m, 4, own, :], wide[:, 4 * width : 5 * width])
        for r in range(0, chunk, 64):
            left = jnp.broadcast_to(both[r : r + 64, 1:2], (64, LANES))
            for t in range(width // LANES):
                lanes = slice(t * LANES, (t + 1) * LANES)
                total = d_act[r : r + 64, lanes] + cw[3:4, lanes] * nxt[t, r : r + 64, :]
                for lag in range(1, 4):
                    later = jnp.where(left >= lag, nxt[t, r + lag : r + lag + 64, :], 0.0)
                    total = total + cw[3 - lag : 4 - lag, lanes] * later
                ib[m, i, r : r + 64, lanes] = total.astype(BF)
        gi[...] += tn(ib[m, i], nb[m, own, :])
        nxt[:, chunk : chunk + EDGE, :] = nxt[:, 0:EDGE, :]
        for rel in range(4):

            @pl.when((i ^ h) == rel)
            def _(rel=rel):
                inner_out(m, rel, i).start()

        return none

    lax.fori_loop(0, 4 * micros, one, 0)
    late_o[0:width, :] = gi[...]
    for copy in consts:
        copy.wait()
    ones = (iota((16, width), 1) % 4 == iota((16, width), 0) % 4).astype(BF)
    for at, full in enumerate((fq, fk, fv)):
        high, low = split(full[...] * on_map[...])
        high, low = split(nt(ones, high) + nt(ones, low))
        compact = mm(high, to_lanes[...]) + mm(low, to_lanes[...])
        small_o[24 + 4 * at : 28 + 4 * at, :] += compact[0:4, :]
    both = gi[...] * jnp.transpose(wb[:, 0:width].astype(F32))
    both = both + gg[...].astype(F32) * jnp.transpose(wb[:, width:].astype(F32))
    total = jnp.sum(both, axis=0, keepdims=True) / gain[...]
    small_o[43:44, :] = total[:, 0:width]
    small_o[44:45, :] = total[:, width:]
    late_o[width:, 0:width] = small_o[0 : SMALL // 2, :]
    late_o[width:, width:] = small_o[SMALL // 2 :, :]
    for m in range(micros):
        for rel in range(4):
            inner_out(m, rel, rel ^ h).wait()


def tokens_kernel(seqs, sc, gain, *rest):
    (x_i, c_i), pairs, inners, (w_up, w_dn, out_o, back_o) = rest[:2], rest[2:6], rest[6:10], rest[10:14]
    x, c, ups, downs, acc, mix, dup, brs, sems = rest[14:]
    h = sc[0]
    micros, rows, dim = x.shape
    width = downs.shape[0] // 4
    inner = w_up.shape[1] // 2

    def place(rel, half=0, count=1):
        return pl.ds(pl.multiple_of((count * rel + half) * width, width), width)

    def columns_in(rel, half):
        at = pl.ds(pl.multiple_of(half * inner + (h ^ rel) * width, width), width)
        return pltpu.make_async_copy(w_up.at[:, at], ups.at[:, place(rel, half, 2)], sems.at[half, rel])

    def rows_in(rel):
        return pltpu.make_async_copy(w_dn.at[place(h ^ rel)], downs.at[place(rel)], sems.at[2, rel])

    def inner_in(m, rel, ref):
        to = dup.at[pl.ds(m * rows, rows), place(rel, 0, 2)]
        return pltpu.make_async_copy(ref.at[m], to, sems.at[3 + m, rel])

    def gate_in(m, rel, ref):
        to = dup.at[pl.ds(m * rows, rows), place(rel, 1, 2)]
        return pltpu.make_async_copy(ref.at[2 * m + 1], to, sems.at[5 + m, rel])

    def branch_in(m, rel, ref):
        to = brs.at[pl.ds(m * rows, rows), place(rel)]
        return pltpu.make_async_copy(ref.at[2 * m], to, sems.at[7 + m, rel])

    def first_in(rel, pair):
        return [rows_in(rel)] + [branch_in(m, rel, pair) for m in range(micros)]

    def second_in(rel, pair, ref):
        group = [columns_in(rel, 0), columns_in(rel, 1)]
        for m in range(micros):
            group = group + [inner_in(m, rel, ref), gate_in(m, rel, pair)]
        return group

    tokens_in = [
        pltpu.make_async_copy(x_i, x, sems.at[9, 0]),
        pltpu.make_async_copy(c_i, c, sems.at[9, 1]),
    ]
    for rel in range(4):
        for copy in first_in(rel, pairs[rel]):
            copy.start()
    for rel in range(4):
        for copy in second_in(rel, pairs[rel], inners[rel]):
            copy.start()
    for copy in tokens_in:
        copy.start()
    acc[...] = jnp.zeros_like(acc)
    for rel in range(4):
        for copy in first_in(rel, pairs[0]):
            copy.wait()
    mix[...] = mm(brs[...], downs[...])

    def one(rel, none):
        at = pl.ds(pl.multiple_of(2 * rel * width, 2 * width), 2 * width)
        for copy in second_in(rel, pairs[0], inners[0]):
            copy.wait()
        acc[...] += nt(dup[:, at], ups[:, at])
        return none

    lax.fori_loop(0, 4, one, 0)
    for copy in tokens_in:
        copy.wait()
    step = 128

    def finish(at, none):
        m, r = at // (rows // step), pl.multiple_of(at % (rows // step) * step, step)
        here, both = pl.ds(r, step), pl.ds(pl.multiple_of(at * step, step), step)
        stream = x[m, here, :].astype(F32)
        pos = (sc[1] * 4 + h) * rows + r + iota((step, 1), 0)
        valid = (seg_of(pos, sc, seqs, m) < seqs).astype(F32)
        out_o[m, here, :] = (stream + valid * mix[both, :]).astype(BF)
        centred = stream - jnp.mean(stream, axis=-1, keepdims=True)
        rstd = lax.rsqrt(jnp.mean(centred * centred, axis=-1, keepdims=True) + EPS)
        exact = centred * rstd
        d_n = acc[both, :] * gain[...]
        along = jnp.mean(d_n * exact, axis=-1, keepdims=True)
        d_x = rstd * (d_n - jnp.mean(d_n, axis=-1, keepdims=True) - exact * along)
        back_o[m, here, :] = (c[m, here, :].astype(F32) + d_x).astype(BF)
        return none

    lax.fori_loop(0, micros * rows // step, finish, 0)


def table_kernel(
    sc, t0, t1, t2, t3, gate_o, wq_o, wk_o, wv_o, cw_o, cb_o, gn_o, sk_o, ln_o, ib_o, fb_o, small
):
    heads, _, width = small.shape
    blocks = width // 4
    for rel, ref in enumerate((t0, t1, t2, t3)):
        small[sc[0] ^ rel, 0 : SMALL // 2, :] = ref[:, 0:width]
        small[sc[0] ^ rel, SMALL // 2 :, :] = ref[:, width:]
    for h in range(heads):
        at = slice(h * width, (h + 1) * width)
        for part in range(3):
            start = (part * heads + h) * width
            gate_o[:, start : start + width] = small[h, 8 * part : 8 * part + 8, :]
        cw_o[:, at] = small[h, 36:40, :]
        for row, ref in ((40, cb_o), (41, gn_o), (42, sk_o)):
            ref[at] = small[h, row, :]
    for at, ref in enumerate((wq_o, wk_o, wv_o)):
        rows = slice(24 + 4 * at, 28 + 4 * at)
        for i in range(4):
            lanes = slice(i * blocks, (i + 1) * blocks)
            ref[i] = jnp.concatenate([small[h, rows, lanes] for h in range(heads)], axis=1)
    for half in range(2):
        ln_o[half * width : (half + 1) * width] = sum(small[h, 43 + half, :] for h in range(heads))
    ib_o[...] = small[0, 45, 0:4]
    fb_o[...] = small[0, 45, 4:8]


def whole(shape):
    return pl.BlockSpec(shape, lambda i, sc: (0,) * len(shape))


def by_chunk(rows, width):
    return pl.BlockSpec((rows, width), lambda i, sc: (i, 0))


def head_cols(rows, width, skip=0):
    return pl.BlockSpec((rows, width), lambda i, sc: (0, sc[0] + skip))


def head_rows(rows, width, skip=0):
    return pl.BlockSpec((rows, width), lambda i, sc: (sc[0] + skip, 0))


def of_micro(m, *shape):
    rest = (0,) * len(shape)
    return pl.BlockSpec((None,) + shape, lambda i, sc: (i if m is None else m,) + rest)


def micro_chunk(m, rows, width):
    return pl.BlockSpec((None, rows, width), lambda i, sc: (m, i, 0))


def micro_lanes(m, rows):
    return pl.BlockSpec((None, 8, rows), lambda i, sc: (m, 0, i))


def call(body, grid, in_specs, out_specs, out_shape, scratch, micros_us, args, aliases=None):
    return pl.pallas_call(
        body,
        grid_spec=pltpu.PrefetchScalarGridSpec(
            num_scalar_prefetch=1,
            grid=grid,
            in_specs=in_specs,
            out_specs=out_specs,
            scratch_shapes=scratch,
        ),
        out_shape=[jax.ShapeDtypeStruct(shape, dtype) for shape, dtype in out_shape],
        compiler_params=pltpu.CompilerParams(vmem_limit_bytes=VMEM_BYTES),
        cost_estimate=pl.CostEstimate(
            flops=int(micros_us * 0.05 * 1.15e9), bytes_accessed=1_000_000, transcendentals=0
        ),
        input_output_aliases=aliases or {},
    )(*args)


def together(*groups):
    flat = iter(lax.optimization_barrier([part for group in groups for part in group]))
    return [[next(flat) for _ in group] for group in groups]


def after(value, *others):
    return lax.optimization_barrier((value, *others))[0]


def per_device(
    tokens, lengths, ln_gain, w_up, conv_w, conv_b, w_q, w_k, w_v, gate_w, i_bias, f_bias,
    gn_gain, skip, w_down, cotangent,
):
    micros, rows, dim = tokens.shape
    inner = w_down.shape[0]
    heads = i_bias.shape[0]
    width = inner // heads
    seqs = lengths.shape[2]
    dp, sq, hd = lax.axis_size("dp"), lax.axis_size("seq"), lax.axis_size("head")
    assert hd == heads == 4 and sq == 2 and micros == 2 and conv_w.shape[0] == 4
    ranks = dp * sq
    every = ranks * hd
    span = rows * hd
    h, s = lax.axis_index("head"), lax.axis_index("seq")
    ends = jnp.cumsum(lengths[:, 0], axis=1).astype(jnp.int32)
    sc = jnp.concatenate([jnp.stack([h, s]).astype(jnp.int32), ends.reshape(-1)])

    def across(value, rel):
        return lax.ppermute(value, "head", [(at, at ^ rel) for at in range(hd)])

    def exchange(parts):
        return [parts[0]] + [across(parts[rel], rel) for rel in range(1, hd)]

    def gather(value):
        return exchange([value] * hd)

    x_near = [across(tokens, 1), across(tokens, 2)]

    place = s * span + jnp.arange(span, dtype=jnp.int32)[None, :, None]
    past = place >= ends[:, None, :]
    age = place[..., 0] - jnp.max(jnp.where(past, ends[:, None, :], 0), axis=2)
    left = jnp.min(jnp.where(past, 1 << 20, ends[:, None, :]), axis=2) - 1 - place[..., 0]
    marks = jnp.stack([age, left] + [jnp.zeros_like(age)] * 6, axis=1).astype(F32)
    gain = ln_gain.reshape(1, dim)
    cb, gn, sk = conv_b.reshape(1, inner), gn_gain.reshape(1, inner), skip.reshape(1, inner)
    gate_t = gate_w.T

    r, c = jnp.arange(width)[:, None], jnp.arange(width)[None, :]
    on = r // 4 == c // 4
    on_map = on.astype(F32)
    to_lanes = (c == r % 4 * (width // 4) + r // 4).astype(BF)

    def spread(weight):
        mine = lax.dynamic_slice_in_dim(weight, h * (width // 4), width // 4, 0).reshape(width, 4)
        return jnp.where(on, jnp.tile(mine, (1, width // 4)), 0).astype(BF)

    wq, wk, wv = spread(w_q), spread(w_k), spread(w_v)
    consts = [sc, marks, gain, cb, gn, sk, gate_t, wq, wk, wv, on_map, to_lanes]
    x_near, consts = together(x_near, consts)
    sc, marks, gain, cb, gn, sk, gate_t, wq, wk, wv, on_map, to_lanes = consts
    x_far = [across(x_near[0][0], 2), across(x_near[1][1], 1)]
    x_parts, x_far = together([tokens, *x_near], x_far)
    tails = [part[:, rows - EDGE :] for part in x_parts]
    tails.append(jnp.stack([part[rows - EDGE :] for part in x_far]))
    tail = tails[0]
    for rel in range(1, hd):
        tail = jnp.where(h == (hd - 1) ^ rel, tails[rel], tail)
    x_halo = lax.ppermute(tail, "seq", [(0, 1)])
    cot = after(cotangent, *x_far)
    c_parts = [cot, across(cot, 1), across(cot, 2)]

    sq_spec = whole((width, width))
    tiles = pltpu.VMEM((width // LANES, rows + EDGE, LANES), F32)
    dma = pltpu.SemaphoreType.DMA
    gate_specs = [head_cols(8, width, part * heads) for part in range(3)]
    conv_specs = [head_cols(4, width), head_cols(1, width)]
    anywhere = pl.BlockSpec(memory_space=pl.ANY)
    held = pl.BlockSpec(memory_space=pltpu.VMEM)

    bf_span, f_span = ((micros, span, width), BF), ((micros, span, width), F32)
    block = whole((rows, width))
    big = whole((width, dim))
    lanes = (micros, 8, span)
    def chunked(rows, width):
        return pl.BlockSpec((None, rows, width), lambda i, sc: (i // hd, i % hd, 0))

    def of_step(*shape):
        rest = (0,) * len(shape)
        return pl.BlockSpec((None,) + shape, lambda i, sc: (i // hd,) + rest)

    chunk_lanes = pl.BlockSpec((None, 8, rows), lambda i, sc: (i // hd, 0, i % hd))
    front = call(
        front_kernel,
        (micros * hd,),
        [of_step(rows, dim)] * 3
        + [whole((rows, dim))] * 2
        + [
            of_step(EDGE, dim), chunk_lanes, whole((1, dim)), head_cols(dim, width),
            head_cols(dim, width, heads), *conv_specs,
        ]
        + [sq_spec] * 3
        + gate_specs,
        [
            chunked(rows, dim), chunked(rows, width),
            pl.BlockSpec((None, 5, rows, width), lambda i, sc: (i // hd, 0, i % hd, 0)),
            of_step(EDGE, width), chunk_lanes,
        ],
        [
            ((micros, span, dim), BF), f_span, ((micros, 5, span, width), BF),
            ((micros, EDGE, width), BF), (lanes, F32),
        ],
        [pltpu.VMEM((rows, dim), BF), tiles],
        20,
        [
            sc, *x_parts, *x_far, x_halo, marks, gain, w_up, w_up, conv_w, cb, wq, wk, wv, gate_t,
            gate_t, gate_t,
        ],
    )
    front, c_parts = together(front, c_parts)
    normed, gz, five, halo, gate_terms = front
    gates = exchange([gate_terms] * hd)
    def of_five(at, count):
        return pl.BlockSpec((None, None, count, width), lambda i, sc: (i, at, 0, 0))

    lane_spec = of_micro(None, 8, span)
    state_spec = of_micro(None, width, width)
    gates, onward = together(gates, [c_parts[1][0], c_parts[2][1]])
    c_parts = c_parts + [across(onward[0], 2), across(onward[1], 1)]
    state = call(
        partial(gates_kernel, seqs),
        (micros,),
        [pl.BlockSpec(memory_space=pltpu.SMEM)] * 2 + [lane_spec] + [held] * 3 + [of_five(1, span), of_five(2, span)],
        [lane_spec, state_spec],
        [(lanes, F32), ((micros, width, width), F32)],
        [],
        7,
        [sc, i_bias, f_bias, *gates, five, five],
    )
    state, c_parts = together(state, c_parts)
    rows_t, states = state
    states_in = lax.ppermute(states, "seq", [(0, 1)])

    half_w = inner // every
    *pairs, gd, gg, both, four, d_states, small_mix, sums = call(
        mix_kernel,
        (1,),
        [whole(lanes), held, head_cols(1, width), head_cols(1, width)]
        + [anywhere] * 9,
        [anywhere] * 8 + [whole((micros, width, width)), whole((8, width)), whole(lanes)],
        [((2 * micros, rows, width), BF)] * 4
        + [((width, dim), BF)] * 2
        + [
            ((ranks, 2 * half_w, dim), BF), ((micros, 4, span, width), F32), ((micros, width, width), F32), ((8, width), F32),
            (lanes, F32),
        ],
        [
            pltpu.VMEM((micros, 4, span, width), BF),
            pltpu.VMEM((micros, span, width), F32),
            pltpu.VMEM((micros, span, dim), BF),
            pltpu.VMEM((micros, hd, rows, dim), BF),
            pltpu.VMEM((width, dim), BF),
            pltpu.VMEM((hd, 2 * micros, rows, width), BF),
            pltpu.VMEM((micros, 4, span, width), F32),
            pltpu.VMEM((width, dim), F32),
            pltpu.VMEM((width, dim), F32),
            pltpu.VMEM((2, width, dim), BF),
            pltpu.VMEM((rows, width), F32),
            pltpu.VMEM((hd // 2, rows, 2 * rows), BF),
            pltpu.VMEM((hd // 2, rows, 2 * rows), F32),
            pltpu.VMEM((rows, 2 * width), BF),
            pltpu.VMEM((span, 2 * width), BF),
            pltpu.VMEM((rows, 2 * width), BF),
            pltpu.VMEM((rows, width), F32),
            pltpu.VMEM((rows, width), BF),
            pltpu.VMEM((rows, width), BF),
            dma((micros, 6, 4)),
            dma((micros, 5, 4)),
            dma((2, ranks)),
        ],
        45,
        [sc, rows_t, states_in, gn, sk, five, gz, normed, *c_parts, w_down],
    )
    d_states = lax.ppermute(d_states, "seq", [(1, 0)])
    d_gates = call(
        gates_back_kernel,
        (micros,),
        [of_five(1, span), of_five(2, span), lane_spec, lane_spec, held],
        [lane_spec],
        [(lanes, F32)],
        [],
        8,
        [sc, five, five, rows_t, sums, d_states],
    )[0]
    d_gates = exchange([d_gates] * hd)

    if half_w % EDGE:
        both = [gg.reshape(ranks, half_w, dim), gd.reshape(ranks, half_w, dim)]
        both = jnp.concatenate(both, axis=1)
    early = lax.all_to_all(both, ("dp", "seq"), split_axis=0, concat_axis=0, tiled=True)
    pairs = exchange([after(part, *d_gates) for part in pairs])

    top = of_micro(None, EDGE, width)

    def of_four(at):
        return pl.BlockSpec((None, None, EDGE, width), lambda i, sc: (i, at, 0, 0))

    edges = call(
        edge_kernel,
        (micros,),
        [of_four(0), of_four(1)]
        + [whole(lanes)]
        + [held] * 3
        + [of_five(4, EDGE), top, of_micro(None, 8, 128), of_four(3)]
        + gate_specs[:2]
        + [sq_spec, sq_spec, *conv_specs],
        [top],
        [((micros, EDGE, width), F32)],
        [pltpu.VMEM((width // LANES, 2 * EDGE, LANES), F32)],
        4,
        [sc, four, four, *d_gates, five, halo, marks, four, gate_t, gate_t, wq, wk, conv_w, cb],
    )[0]
    edges = lax.ppermute(edges, "seq", [(1, 0)])
    axes = ("dp", "seq", "head")
    *d_inners, late = call(
        front_back_kernel,
        (1,),
        [whole(lanes)]
        + [held] * 3
        + [whole(lanes)] * 2
        + [held, whole((micros, EDGE, width)), whole((8, width)), held]
        + gate_specs
        + [sq_spec] * 3
        + conv_specs
        + [whole((1, dim))]
        + [anywhere] * 7,
        [anywhere] * 4 + [whole((width + SMALL // 2, dim))],
        [((micros, rows, width), BF)] * 4 + [((width + SMALL // 2, dim), F32)],
        [
            pltpu.VMEM((micros, 4, span, width), F32),
            pltpu.VMEM((micros, 5, span, width), BF),
            pltpu.VMEM((micros, span, dim), BF),
            pltpu.VMEM((micros, hd, EDGE, width), BF),
            pltpu.VMEM((dim, 2 * width), BF),
            pltpu.VMEM((micros, hd, rows, width), BF),
            tiles,
            tiles,
            pltpu.VMEM((rows, 6 * width), BF),
            *[pltpu.VMEM((width, width), F32)] * 3,
            pltpu.VMEM((rows, width), F32),
            pltpu.VMEM((width, dim), F32),
            pltpu.VMEM((width, width), F32),
            pltpu.VMEM((width, width), BF),
            pltpu.VMEM((width, dim), BF),
            pltpu.VMEM((SMALL, width), F32),
            dma((micros, 5, 4)),
            dma((micros, 4)),
        ],
        28,
        [
            sc, *d_gates, rows_t, marks, d_states, halo, small_mix, edges, gate_t, gate_t, gate_t,
            wq, wk, wv, conv_w, cb, gain, on_map, to_lanes, four, five, normed, gg, w_up,
        ],
    )
    (late, *d_inners), pairs = together([late, *d_inners], pairs)
    d_inners = exchange(d_inners)

    late = late + lax.ppermute(late, "seq", [(0, 1), (1, 0)])
    small = late[width:]
    blocks = late[:width].reshape(dp, 2 * half_w, dim)
    d = lax.axis_index("dp")
    if dp == 4:
        high = lax.reduce_precision(small, 8, 7)
        table = jnp.concatenate([high.astype(BF), (small - high).astype(BF)], axis=0)

        def to_plane(rel):
            block = lax.dynamic_index_in_dim(blocks, d ^ rel, 0, keepdims=False).astype(BF)
            block = jnp.concatenate([block, table], axis=0)
            if rel == 0:
                return block
            pairs_of = [(a * sq + 1, (a ^ rel) * sq + 1) for a in range(dp)]
            return lax.ppermute(block, ("dp", "seq"), pairs_of)

        terms = [to_plane(rel).astype(F32) for rel in range(dp)]
        terms = (terms[0] + terms[1]) + (terms[2] + terms[3])
        g_inner, small = terms[: 2 * half_w], terms[2 * half_w :]
        small = small[: SMALL // 2] + small[SMALL // 2 :]
        small = jnp.where(s == 1, small, lax.ppermute(small, "seq", [(1, 0)]))
    else:
        small = lax.psum(small, "dp")
        terms = lax.all_to_all(blocks.astype(BF), "dp", split_axis=0, concat_axis=0, tiled=True)
        g_inner = jnp.sum(terms.astype(F32), axis=0)
    early = jnp.sum(early.astype(F32), axis=0)
    g_gate, g_down = early[:half_w], early[half_w:]
    g_gate = jnp.concatenate([g_gate, lax.ppermute(g_gate, "seq", [(1, 0)])], axis=0)
    up_pairs, down_pairs = [], []
    for rank in range(ranks):
        for at in range(hd):
            block_at = at * dp + rank // 2 + (0 if rank % 2 else every // 2)
            up_pairs.append((rank * hd + at, block_at))
            down_pairs.append((rank * hd + at, at * ranks + rank))
    g_down = lax.ppermute(g_down, axes, down_pairs)
    g_up = jnp.where(s == 0, g_gate, g_inner)
    d_inners, (small, g_up) = together(d_inners, [small, g_up])
    g_up = lax.ppermute(g_up, axes, up_pairs).T

    token_spec = whole(tokens.shape)
    block_out, d_tokens = call(
        partial(tokens_kernel, seqs),
        (1,),
        [whole((1, dim))] + [anywhere] * 12,
        [token_spec] * 2,
        [(tokens.shape, BF)] * 2,
        [
            pltpu.VMEM(tokens.shape, BF),
            pltpu.VMEM(tokens.shape, BF),
            pltpu.VMEM((dim, 2 * inner), BF),
            pltpu.VMEM((inner, dim), BF),
            pltpu.VMEM((micros * rows, dim), F32),
            pltpu.VMEM((micros * rows, dim), F32),
            pltpu.VMEM((micros * rows, 2 * inner), BF),
            pltpu.VMEM((micros * rows, inner), BF),
            dma((10, hd)),
        ],
        10,
        [sc, gain, tokens, cotangent, *pairs, *d_inners, w_up, w_down],
    )

    (block_out, d_tokens), (small,) = together([block_out, d_tokens], [small])
    table = gather(small)
    flat = [((8, 3 * inner), F32), *[((4, 4, inner // 4), F32)] * 3, ((4, inner), F32)]
    flat = flat + [((inner,), F32)] * 3 + [((dim,), F32)] + [((heads,), F32)] * 2
    g_gate, g_wq, g_wk, g_wv, g_cw, g_cb, g_gn, g_sk, g_ln, g_ib, g_fb = call(
        table_kernel,
        (1,),
        [whole(small.shape)] + [held] * 3,
        [whole(shape) for shape, _ in flat],
        flat,
        [pltpu.VMEM((hd, SMALL, width), F32)],
        3,
        [sc, *table],
    )
    maps = [part.transpose(2, 0, 1) for part in (g_wq, g_wk, g_wv)]
    return (
        block_out, d_tokens, g_ln, g_up, g_cw, g_cb, *maps, g_gate.T, g_ib, g_fb, g_gn, g_sk, g_down,
    )


def solution(mesh):
    rows = P(None, ("dp", "seq", "head"), None)
    placed = (rows, P(None, "dp", None), *[P()] * 13, rows)
    outs = (rows, rows, P(), P(None, ("dp", "seq", "head")), *[P()] * 10, P(("dp", "seq", "head"), None))
    return jax.shard_map(per_device, mesh=mesh, in_specs=placed, out_specs=outs, check_vma=False)
```

```python
from functools import partial

import jax
import jax.numpy as jnp
from jax import lax
from jax.experimental import pallas as pl
from jax.experimental.pallas import tpu as pltpu
from jax.sharding import PartitionSpec as P

EPS = 1e-05
HIGH = lax.Precision.HIGHEST
BF = jnp.bfloat16
F32 = jnp.float32
EDGE = 16
SMALL = 48
NEVER = -1e30
VMEM_BYTES = 52 * 1024 * 1024


def mm(a, b):
    return lax.dot_general(a, b, (((1,), (0,)), ((), ())), preferred_element_type=F32)


def nt(a, b):
    return lax.dot_general(a, b, (((1,), (1,)), ((), ())), preferred_element_type=F32)


def tn(a, b):
    return lax.dot_general(a, b, (((0,), (0,)), ((), ())), preferred_element_type=F32)


def split(v):
    high = v.astype(BF)
    return high, (v - high.astype(F32)).astype(BF)


def iota(shape, dim):
    return lax.broadcasted_iota(jnp.int32, shape, dim)


def seg_of(pos, sc, seqs, m):
    total = (pos >= sc[2 + m * seqs]).astype(jnp.int32)
    for e in range(1, seqs):
        total = total + (pos >= sc[2 + m * seqs + e]).astype(jnp.int32)
    return total


def pick(refs, which, dest, rows):
    for at, ref in enumerate(refs):

        @pl.when(which == at)
        def _(ref=ref):
            dest[...] = ref[rows, :]


def put(refs, which, value):
    for at, ref in enumerate(refs):

        @pl.when(which == at)
        def _(ref=ref):
            ref[...] = value


def lane_sums(v):
    ones = jnp.ones((8, v.shape[1]), BF)
    high, low = split(v)
    return nt(ones, high) + nt(ones, low)


def running_sum(v):
    width = v.shape[1] // 8
    tri = (iota((width, width), 0) <= iota((width, width), 1)).astype(BF)
    chunks = jnp.concatenate([v[:, c * width : (c + 1) * width] for c in range(8)], axis=0)
    high, rest = split(chunks)
    rest = chunks - high.astype(F32)
    mid, low = split(rest)
    within = mm(high, tri) + (mm(mid, tri) + mm(low, tri))
    carry, parts = jnp.zeros((1, 1), F32), []
    for c in range(8):
        parts.append(within[c : c + 1, :] + carry)
        carry = carry + within[c : c + 1, width - 1 : width]
    return jnp.concatenate(parts, axis=1)


LANES = 128


def to_tiles(ext, start, value):
    rows, width = value.shape
    for t in range(width // LANES):
        ext[t, start : start + rows, :] = value[:, t * LANES : (t + 1) * LANES]


def conv_blocks(ext, rows, ages, cw, cb, step):
    for r in range(0, rows, step):
        age = jnp.broadcast_to(ages[r : r + step], (step, LANES))
        for t in range(ext.shape[0]):
            lanes = slice(t * LANES, (t + 1) * LANES)
            lags = [ext[t, EDGE + r : EDGE + r + step, :]]
            for lag in range(1, 4):
                earlier = ext[t, EDGE + r - lag : EDGE + r - lag + step, :]
                lags.append(jnp.where(age >= lag, earlier, 0.0))
            total = cb[:, lanes] + cw[3:4, lanes] * lags[0]
            for lag in range(1, 4):
                total = total + cw[3 - lag : 4 - lag, lanes] * lags[lag]
            yield slice(r, r + step), lanes, total, lags


def folded(v):
    return sum(v[e : e + 8] for e in range(8, v.shape[0], 8)) + v[0:8]


def front_kernel(
    sc, x0, x1, x2, x3a, x3b, xh, marks, gain, w_in, w_gt, cw, cb, wq, wk, wv, gq, gk, gv, *rest
):
    normed_o, gz_o, five_o, halo_o, gt_o, xs, ext = rest[-7:]
    m, i = pl.program_id(0) // 4, pl.program_id(0) % 4
    chunk = xs.shape[0]
    rel = i ^ sc[0]
    pick((x0, x1, x2, x3a, x3b), jnp.where((rel == 3) & (m == 1), 4, rel), xs, slice(0, chunk))

    def norm(rows):
        stream = rows.astype(F32)
        centred = stream - jnp.mean(stream, axis=-1, keepdims=True)
        variance = jnp.mean(centred * centred, axis=-1, keepdims=True)
        return (centred * lax.rsqrt(variance + EPS) * gain[...]).astype(BF)

    @pl.when(i == 0)
    def _():
        edge = mm(norm(xh[...]), w_in[...]).astype(BF)
        to_tiles(ext, 0, edge.astype(F32))
        halo_o[...] = edge

    @pl.when(i > 0)
    def _():
        ext[:, 0:EDGE, :] = ext[:, chunk : chunk + EDGE, :]

    for r in range(0, chunk, 32):
        normed_o[r : r + 32, :] = norm(xs[r : r + 32, :])
    inner = mm(normed_o[...], w_in[...]).astype(BF)
    five_o[4] = inner
    to_tiles(ext, EDGE, inner.astype(F32))
    gz_o[...] = mm(normed_o[...], w_gt[...])
    ages = jnp.transpose(marks[...])[:, 0:1]
    for rows, lanes, total, _ in conv_blocks(ext, chunk, ages, cw, cb, 64):
        five_o[3, rows, lanes] = (total / (1.0 + jnp.exp(-total))).astype(BF)
    q = mm(five_o[3], wq[...]).astype(BF)
    k = mm(five_o[3], wk[...]).astype(BF)
    v = mm(five_o[4], wv[...]).astype(BF)
    five_o[0] = q
    five_o[1] = k
    five_o[2] = v
    gt_o[...] = nt(gq[...], q) + nt(gk[...], k) + nt(gv[...], v)


def gates_kernel(seqs, sc, ib, fb, g0, g1, g2, g3, k, v, rows_o, s_o):
    m = pl.program_id(0)
    h, s = sc[0], sc[1]
    span, width = k.shape
    factor = width ** (-0.5)
    lin = ((g0[...] + g1[m]) + (g2[m] + g3[m])).astype(BF).astype(F32)
    r = iota(lin.shape, 0)
    ig = jnp.sum(jnp.where(r == 2 * h, lin, 0.0), axis=0, keepdims=True) + ib[h]
    fg = jnp.sum(jnp.where(r == 2 * h + 1, lin, 0.0), axis=0, keepdims=True) + fb[h]
    pos = s * span + iota((1, span), 1)
    seg = seg_of(pos, sc, seqs, m)
    valid = (seg < seqs).astype(F32)
    log_keep = valid * (jnp.minimum(fg, 0.0) - jnp.log1p(jnp.exp(-jnp.abs(fg))))
    cum = running_sum(log_keep)
    prev = jnp.where(s == 0, -1, seg_of(s * span - 1, sc, seqs, m))
    last = seg_of(s * span + span - 1, sc, seqs, m)
    carried = jnp.where(seg == prev, jnp.exp(cum), 0.0)
    offset = jnp.where(seg < seqs, ig - cum, NEVER)
    tail = jnp.exp(jnp.where(seg == last, cum[:, span - 1 : span] + offset, NEVER)) * factor
    slope = valid / (1.0 + jnp.exp(fg))
    rows = jnp.zeros((8, span), F32)
    for at, row in enumerate((cum, offset, seg.astype(F32), slope, carried, tail, valid)):
        rows = jnp.where(r == at, row, rows)
    rows_o[...] = rows
    cols = jnp.transpose(rows)
    high, low = split(k[...].astype(F32) * cols[:, 5:6])
    s_o[...] = tn(high, v[...]) + tn(low, v[...])


def mix_kernel(
    sc, rows, s_in, gn, sk, five, gz, normed, c0, c1, c2, c3a, c3b, w_dn, *rest
):
    p0, p1, p2, p3, gd_o, gg_o, both_o, four_o, ds_o, small_o, sums_o = rest[:11]
    fb, zb, nb, cb, wb, pb, four, gd, gg, go, acc, a_high, decays = rest[11:24]
    q2, v2, dh2, dbr, in_sems, out_sems, pack_sems = rest[24:]
    h = sc[0]
    micros, _, span, width = fb.shape
    chunk = acc.shape[0]
    two = 2 * chunk
    factor = width ** (-0.5)

    def rows_of(i, size=chunk):
        return pl.ds(pl.multiple_of(i * size, size), size)

    def qkv_in(m, j):
        at, three = rows_of(j, two), pl.ds(0, 3)
        to = fb.at[m, three, at]
        return pltpu.make_async_copy(five.at[m, three, at], to, in_sems.at[m, 0, j])

    def chunk_in(m, i):
        at = rows_of(i)
        return [
            pltpu.make_async_copy(five.at[m, 3, at], fb.at[m, 3, at], in_sems.at[m, 1, i]),
            pltpu.make_async_copy(gz.at[m, at], zb.at[m, at], in_sems.at[m, 2, i]),
            pltpu.make_async_copy(normed.at[m, at], nb.at[m, at], in_sems.at[m, 3, i]),
        ]

    def cot_in(m, rel, i, last=False):
        ref = (c0.at[m], c1.at[m], c2.at[m], c3b if last else c3a)[rel]
        return pltpu.make_async_copy(ref, cb.at[m, i], in_sems.at[m, 4, i])

    weight_in = pltpu.make_async_copy(w_dn.at[rows_of(h, width)], wb, in_sems.at[0, 5, 0])

    def others_in(m, last):
        for rel in range(4):
            cot_in(m, rel, rel ^ h, last).start()
        for copy in (*chunk_in(m, 1), qkv_in(m, 1), *chunk_in(m, 2), *chunk_in(m, 3)):
            copy.start()

    for copy in (qkv_in(0, 0), weight_in, *chunk_in(0, 0)):
        copy.start()
    others_in(0, False)
    small_o[...] = jnp.zeros_like(small_o)
    gd[...] = jnp.zeros_like(gd)
    gg[...] = jnp.zeros_like(gg)

    def pair_out(m, rel, i):
        at = pl.ds(2 * m, 2)
        to = (p0, p1, p2, p3)[rel].at[at]
        return pltpu.make_async_copy(pb.at[i, at], to, out_sems.at[m, 0, rel])

    def rows_out(m, i):
        at = rows_of(i)
        return [
            pltpu.make_async_copy(four.at[m, 0, at], four_o.at[m, 0, at], out_sems.at[m, 1, i]),
            pltpu.make_async_copy(four.at[m, 3, at], four_o.at[m, 3, at], out_sems.at[m, 2, i]),
        ]

    def key_out(m, j):
        at, pair = rows_of(j, two), pl.ds(1, 2)
        to = four_o.at[m, pair, at]
        return pltpu.make_async_copy(four.at[m, pair, at], to, out_sems.at[m, 3, j])

    grads_out = [
        pltpu.make_async_copy(go.at[0], gd_o, out_sems.at[0, 4, 0]),
        pltpu.make_async_copy(go.at[1], gg_o, out_sems.at[0, 4, 1]),
    ]
    ranks, piece = both_o.shape[0], both_o.shape[1] // 2
    if piece % EDGE == 0:
        grads_out = grads_out[1:]
        for r in range(ranks):
            for at, which in enumerate((1, 0)):
                to = both_o.at[r, pl.ds(at * piece, piece)]
                rows_r = go.at[which, pl.ds(r * piece, piece)]
                grads_out.append(pltpu.make_async_copy(rows_r, to, pack_sems.at[at, r]))

    def one(at_step, none):
        m, i = at_step // 4, at_step % 4

        @pl.when(i == 0)
        def _():
            four[m, 1] = jnp.zeros((span, width), F32)
            four[m, 2] = jnp.zeros((span, width), F32)
            ds_o[m] = jnp.zeros((width, width), F32)

        @pl.when(at_step == 1)
        def _():
            for copy in (qkv_in(1, 0), *chunk_in(1, 0)):
                copy.start()
            others_in(1, True)

        start = pl.multiple_of(i * chunk, chunk)
        own = pl.ds(start, chunk)

        @pl.when(i % 2 == 0)
        def _():
            at = rows_of(i // 2, two)
            qkv_in(m, i // 2).wait()
            v2[at, 0:width] = fb[m, 2, at, :]
            v2[at, width:] = fb[m, 2, at, :]

        @pl.when(at_step == 0)
        def _():
            weight_in.wait()

        for copy in chunk_in(m, i):
            copy.wait()
        cot_in(m, 0, i).wait()
        here = start + iota((chunk, 1), 0)
        cols = jnp.transpose(rows[m, :, own])
        cum, seg, carried, valid = cols[:, 0:1], cols[:, 2:3], cols[:, 4:5], cols[:, 6:7]

        def attend(j, wide=two):
            at = slice(j * two, j * two + wide)
            scores = nt(fb[m, 0, own, :], fb[m, 1, at, :]) * factor
            allowed = (seg == rows[m, 2:3, at]) & (j * two + iota((1, wide), 1) <= here)
            decay = jnp.exp(jnp.where(allowed, cum + rows[m, 1:2, at], NEVER))
            decays[j, :, 0:wide] = decay
            high, low = split(scores * decay)
            a_high[j, :, 0:wide] = high
            return mm(high, fb[m, 2, at, :]) + mm(low, fb[m, 2, at, :])

        q2[:, 0:width] = fb[m, 0, own, :]
        q2[:, width:] = fb[m, 0, own, :]
        state = jnp.concatenate(split(s_in[m]), axis=0)
        acc[...] = attend(0) + carried * mm(q2[...], state)

        cb[m, i] = (cb[m, i].astype(F32) * valid).astype(BF)
        dbr[...] = nt(cb[m, i], wb[...])

        @pl.when(i == 2)
        def _():
            acc[...] += attend(1, chunk)

        @pl.when(i == 3)
        def _():
            acc[...] += attend(1)

        step = 32
        sum_gn, sum_sk = jnp.zeros((8, width), F32), jnp.zeros((8, width), F32)
        for r in range(0, chunk, step):
            part, at = slice(r, r + step), pl.ds(start + r, step)
            hidden = acc[part, :]
            centred = hidden - jnp.mean(hidden, axis=-1, keepdims=True)
            rstd = lax.rsqrt(jnp.mean(centred * centred, axis=-1, keepdims=True) + EPS)
            exact = centred * rstd
            normed_h = exact.astype(BF).astype(F32)
            gate = zb[m, at, :]
            sig = 1.0 / (1.0 + jnp.exp(-gate))
            gate_act = gate * sig
            act_f = fb[m, 3, at, :].astype(F32)
            mid = normed_h * gn[...] + sk[...] * act_f
            pb[i, 2 * m, part, :] = (mid * gate_act).astype(BF)
            d_branch = dbr[part, :]
            d_mid = d_branch * gate_act
            pb[i, 2 * m + 1, part, :] = (d_branch * mid * (sig + gate_act * (1.0 - sig))).astype(BF)
            sum_gn, sum_sk = sum_gn + folded(d_mid * normed_h), sum_sk + folded(d_mid * act_f)
            four[m, 3, at, :] = d_mid * sk[...]
            d_norm = (d_mid * gn[...]).astype(BF).astype(F32)
            along = jnp.mean(d_norm * exact, axis=-1, keepdims=True)
            d_hid = rstd * (d_norm - jnp.mean(d_norm, axis=-1, keepdims=True) - exact * along)
            dh_high, dh_low = split(d_hid)
            dh2[part, 0:width] = dh_high
            dh2[part, width:] = dh_low
            q2[part, width:] = (d_hid * carried[part]).astype(BF)
        small_o[0:1, :] += jnp.sum(sum_gn, axis=0, keepdims=True)
        small_o[1:2, :] += jnp.sum(sum_sk, axis=0, keepdims=True)
        gd[...] += tn(pb[i, 2 * m], cb[m, i])
        gg[...] += tn(pb[i, 2 * m + 1], nb[m, own, :])
        ds_o[m] += tn(fb[m, 0, own, :], q2[:, width:])
        acc[...] = carried * nt(dh2[:, 0:width], s_in[m].astype(BF))
        def attend_back(j, wide=two):
            at = slice(j * two, j * two + wide)
            d_att = nt(dh2[...], v2[at, :])
            four[m, 2, at, :] += tn(a_high[j, :, 0:wide], dh2[:, 0:width])
            w_high, w_low = split(decays[j, :, 0:wide] * d_att * factor)
            four[m, 1, at, :] += tn(w_high, fb[m, 0, own, :]) + tn(w_low, fb[m, 0, own, :])
            return mm(w_high, fb[m, 1, at, :]) + mm(w_low, fb[m, 1, at, :])

        acc[...] += attend_back(0)
        for rel in range(4):

            @pl.when((i ^ h) == rel)
            def _(rel=rel):
                pair_out(m, rel, i).start()

        @pl.when(at_step == 4 * micros - 1)
        def _():
            go[0] = gd[...].astype(BF)
            go[1] = gg[...].astype(BF)
            for copy in grads_out:
                copy.start()

        @pl.when(i == 3)
        def _():
            key_out(m, 0).start()

        @pl.when(i == 2)
        def _():
            acc[...] += attend_back(1, chunk)

        @pl.when(i == 3)
        def _():
            acc[...] += attend_back(1)

        @pl.when(i == 3)
        def _():
            key_out(m, 1).start()

        four[m, 0, own, :] = acc[...]
        for copy in rows_out(m, i):
            copy.start()
        return none

    lax.fori_loop(0, 4 * micros, one, 0)

    def finish(at_step, none):
        m, at = at_step // 2, rows_of(at_step % 2, two)
        row_sum = lane_sums(four[m, 0, at, :] * fb[m, 0, at, :].astype(F32))
        col_sum = lane_sums(four[m, 1, at, :] * fb[m, 1, at, :].astype(F32))
        sums_o[m, :, at] = jnp.where(iota((8, two), 0) == 0, col_sum, row_sum - col_sum)
        return none

    lax.fori_loop(0, 2 * micros, finish, 0)
    for m in range(micros):
        for rel in range(4):
            pair_out(m, rel, rel ^ h).wait()
        for i in range(4):
            for copy in rows_out(m, i):
                copy.wait()
        for copy in (key_out(m, 0), key_out(m, 1)):
            copy.wait()
    for copy in grads_out:
        copy.wait()


def gates_back_kernel(sc, k, v, rows, sums, ds_out, dg_o):
    h, s = sc[0], sc[1]
    span = k.shape[0]
    turned = nt(twice(v[...], 1), jnp.concatenate(split(ds_out[pl.program_id(0)]), axis=1))
    cross = rows[5:6, :] * lane_sums(turned * k[...].astype(F32))
    r = iota((8, span), 0)
    d_ig = sums[0:1, :] + cross[0:1, :]
    d_cum = sums[1:2, :] - cross[0:1, :]
    running = running_sum(d_cum)
    total = jnp.where(s == 0, 0.0, running[:, span - 1 : span])
    d_fg = rows[3:4, :] * (total - running + d_cum)
    dg_o[...] = jnp.where(r == 2 * h, d_ig, jnp.where(r == 2 * h + 1, d_fg, 0.0))


def twice(v, axis=0):
    return jnp.concatenate([v, v], axis=axis)


def silu_slope(v):
    sig = 1.0 / (1.0 + jnp.exp(-v))
    return sig * (1.0 + v * (1.0 - sig))


def edge_kernel(
    sc, dq, dk, d0, d1, d2, d3, inner, halo, marks, skip_d, gq, gk, wq, wk, cw, cb, dcs_o, ext
):
    to_tiles(ext, 0, halo[...].astype(F32))
    to_tiles(ext, EDGE, inner[...].astype(F32))
    m, at = pl.program_id(0), slice(0, 128)
    total = (d0[m, :, at] + d1[m, :, at]) + (d2[m, :, at] + d3[m, :, at])
    g_all = jnp.concatenate(split(total), axis=0)
    dq_h, dq_l = split(dq[...] + tn(g_all, twice(gq[...]))[0:EDGE, :])
    dk_h, dk_l = split(dk[...] + tn(g_all, twice(gk[...]))[0:EDGE, :])
    d_act = skip_d[...] + nt(dq_h, wq[...]) + nt(dq_l, wq[...]) + nt(dk_h, wk[...]) + nt(dk_l, wk[...])
    for _, lanes, total, _ in conv_blocks(ext, EDGE, jnp.transpose(marks[...])[0:EDGE, 0:1], cw, cb, EDGE):
        dcs_o[:, lanes] = d_act[:, lanes] * silu_slope(total)


def front_back_kernel(
    sc, d0, d1, d2, d3, rows_t, marks, ds_out, halo, small_i, edge, gq, gk, gv, wq, wk, wv,
    cw, cb, gain, on_map_i, to_lanes_i, four, five, normed, gg_i, w_up, *rest,
):
    i0, i1, i2, i3, late_o = rest[:5]
    fb, qb, nb, bb, wb, ib, ext, nxt, wide, fq, fk, fv, d_act, gi = rest[5:19]
    on_map, to_lanes, gg, small_o, in_sems, out_sems = rest[19:]
    h = sc[0]
    micros, _, span, width = fb.shape
    chunk = d_act.shape[0]

    def inward(m, i):
        at = pl.ds(pl.multiple_of(i * chunk, chunk), chunk)
        return [
            pltpu.make_async_copy(four.at[m, :, at], fb.at[m, :, at], in_sems.at[m, 0, i]),
            pltpu.make_async_copy(five.at[m, :, at], qb.at[m, :, at], in_sems.at[m, 1, i]),
            pltpu.make_async_copy(normed.at[m, at], nb.at[m, at], in_sems.at[m, 2, i]),
        ]

    def before(m, i):
        at = pl.ds(i * chunk - EDGE, EDGE)
        return pltpu.make_async_copy(five.at[m, 4, at], bb.at[m, i], in_sems.at[m, 3, i])

    befores = [before(m, i) for m in range(micros) for i in range(1, 4)]
    consts = [
        pltpu.make_async_copy(on_map_i, on_map, in_sems.at[0, 4, 0]),
        pltpu.make_async_copy(to_lanes_i, to_lanes, in_sems.at[0, 4, 1]),
        pltpu.make_async_copy(gg_i, gg, in_sems.at[0, 4, 2]),
    ]
    for at in range(2):
        columns = pl.ds(pl.multiple_of(at * (w_up.shape[1] // 2) + h * width, width), width)
        to = wb.at[:, pl.ds(at * width, width)]
        consts.append(pltpu.make_async_copy(w_up.at[:, columns], to, in_sems.at[1, 4, at]))
    for copy in (*inward(0, 3), *befores, *inward(0, 2), *inward(0, 1), *inward(0, 0)):
        copy.start()
    small_o[...] = jnp.zeros_like(small_o)
    small_o[41:43, :] += small_i[0:2, :]
    fq[...] = jnp.zeros_like(fq)
    fk[...] = jnp.zeros_like(fk)
    fv[...] = jnp.zeros_like(fv)
    gi[...] = jnp.zeros_like(gi)
    for m in range(micros):
        bb[m, 0] = halo[m]
    for copy in befores:
        copy.wait()

    def inner_out(m, rel, i):
        to = (i0, i1, i2, i3)[rel].at[m]
        return pltpu.make_async_copy(ib.at[m, i], to, out_sems.at[m, rel])

    def one(step, none):
        m, i = step // 4, 3 - step % 4

        @pl.when(i == 3)
        def _():
            to_tiles(nxt, chunk, edge[m])

        @pl.when(step == 1)
        def _():
            for at in (3, 2, 1, 0):
                for copy in inward(1, at):
                    copy.start()
            for copy in consts:
                copy.start()

        start = pl.multiple_of(i * chunk, chunk)
        own = pl.ds(start, chunk)
        for copy in inward(m, i):
            copy.wait()
        to_tiles(ext, 0, bb[m, i].astype(F32))
        to_tiles(ext, EDGE, qb[m, 4, own, :].astype(F32))
        dg = (d0[m, :, own] + d1[m, :, own]) + (d2[m, :, own] + d3[m, :, own])
        g_all = jnp.concatenate(split(dg), axis=0)
        for at in range(3):
            part = mm(g_all, qb[m, at, own, :])
            small_o[8 * at : 8 * at + 8, :] += part[0:8, :] + part[8:16, :]
        order = [dg[r : r + 1, :] for r in (0, 2, 4, 6, 1, 3, 5, 7)]
        small_o[45:46, 0:8] += lane_sums(jnp.concatenate(order, axis=0))[0:1, :]
        state = ds_out[m].astype(BF)
        tail = jnp.transpose(rows_t[m, :, own])[:, 5:6]
        both = jnp.transpose(marks[m, :, own])
        for at, gate in enumerate((gq, gk, gv)):
            total = fb[m, at, own, :] + tn(g_all, twice(gate[...]))
            if at == 1:
                total = total + tail * nt(qb[m, 2, own, :], state)
            if at == 2:
                total = total + tail * mm(qb[m, 1, own, :], state)
            high, low = split(total)
            wide[:, 2 * at * width : (2 * at + 1) * width] = high
            wide[:, (2 * at + 1) * width : (2 * at + 2) * width] = low
        maps = jnp.concatenate([wq[...], wq[...], wk[...], wk[...]], axis=1)
        d_act[...] = fb[m, 3, own, :] + nt(wide[:, 0 : 4 * width], maps)
        sums = [[0.0] * 5 for _ in range(width // LANES)]
        for at, lanes, total, lags in conv_blocks(ext, chunk, both[:, 0:1], cw, cb, 64):
            d_cs = d_act[at, lanes] * silu_slope(total)
            t = lanes.start // LANES
            nxt[t, at, :] = d_cs
            for lag in range(4):
                sums[t][3 - lag] = sums[t][3 - lag] + folded(d_cs * lags[lag])
            sums[t][4] = sums[t][4] + folded(d_cs)
        for t, group in enumerate(sums):
            for at, total in enumerate(group):
                lanes = slice(t * LANES, (t + 1) * LANES)
                small_o[36 + at : 37 + at, lanes] += jnp.sum(total, axis=0, keepdims=True)
        maps = jnp.concatenate([wv[...], wv[...]], axis=1)
        d_act[...] = nt(wide[:, 4 * width :], maps)
        fq[...] += tn(qb[m, 3, own, :], wide[:, 0:width])
        fk[...] += tn(qb[m, 3, own, :], wide[:, 2 * width : 3 * width])
        fv[...] += tn(qb[m, 4, own, :], wide[:, 4 * width : 5 * width])
        for r in range(0, chunk, 64):
            left = jnp.broadcast_to(both[r : r + 64, 1:2], (64, LANES))
            for t in range(width // LANES):
                lanes = slice(t * LANES, (t + 1) * LANES)
                total = d_act[r : r + 64, lanes] + cw[3:4, lanes] * nxt[t, r : r + 64, :]
                for lag in range(1, 4):
                    later = jnp.where(left >= lag, nxt[t, r + lag : r + lag + 64, :], 0.0)
                    total = total + cw[3 - lag : 4 - lag, lanes] * later
                ib[m, i, r : r + 64, lanes] = total.astype(BF)
        gi[...] += tn(ib[m, i], nb[m, own, :])
        nxt[:, chunk : chunk + EDGE, :] = nxt[:, 0:EDGE, :]
        for rel in range(4):

            @pl.when((i ^ h) == rel)
            def _(rel=rel):
                inner_out(m, rel, i).start()

        return none

    lax.fori_loop(0, 4 * micros, one, 0)
    late_o[0:width, :] = gi[...]
    for copy in consts:
        copy.wait()
    ones = (iota((16, width), 1) % 4 == iota((16, width), 0) % 4).astype(BF)
    for at, full in enumerate((fq, fk, fv)):
        high, low = split(full[...] * on_map[...])
        high, low = split(nt(ones, high) + nt(ones, low))
        compact = mm(high, to_lanes[...]) + mm(low, to_lanes[...])
        small_o[24 + 4 * at : 28 + 4 * at, :] += compact[0:4, :]
    both = gi[...] * jnp.transpose(wb[:, 0:width].astype(F32))
    both = both + gg[...].astype(F32) * jnp.transpose(wb[:, width:].astype(F32))
    total = jnp.sum(both, axis=0, keepdims=True) / gain[...]
    small_o[43:44, :] = total[:, 0:width]
    small_o[44:45, :] = total[:, width:]
    late_o[width:, 0:width] = small_o[0 : SMALL // 2, :]
    late_o[width:, width:] = small_o[SMALL // 2 :, :]
    for m in range(micros):
        for rel in range(4):
            inner_out(m, rel, rel ^ h).wait()


def tokens_kernel(seqs, sc, gain, *rest):
    (x_i, c_i), pairs, inners, (w_up, w_dn, out_o, back_o) = rest[:2], rest[2:6], rest[6:10], rest[10:14]
    x, c, ups, downs, acc, mix, dup, brs, sems = rest[14:]
    h = sc[0]
    micros, rows, dim = x.shape
    width = downs.shape[0] // 4
    inner = w_up.shape[1] // 2

    def place(rel, half=0, count=1):
        return pl.ds(pl.multiple_of((count * rel + half) * width, width), width)

    def columns_in(rel, half):
        at = pl.ds(pl.multiple_of(half * inner + (h ^ rel) * width, width), width)
        return pltpu.make_async_copy(w_up.at[:, at], ups.at[:, place(rel, half, 2)], sems.at[half, rel])

    def rows_in(rel):
        return pltpu.make_async_copy(w_dn.at[place(h ^ rel)], downs.at[place(rel)], sems.at[2, rel])

    def inner_in(m, rel, ref):
        to = dup.at[pl.ds(m * rows, rows), place(rel, 0, 2)]
        return pltpu.make_async_copy(ref.at[m], to, sems.at[3 + m, rel])

    def gate_in(m, rel, ref):
        to = dup.at[pl.ds(m * rows, rows), place(rel, 1, 2)]
        return pltpu.make_async_copy(ref.at[2 * m + 1], to, sems.at[5 + m, rel])

    def branch_in(m, rel, ref):
        to = brs.at[pl.ds(m * rows, rows), place(rel)]
        return pltpu.make_async_copy(ref.at[2 * m], to, sems.at[7 + m, rel])

    def first_in(rel, pair):
        return [rows_in(rel)] + [branch_in(m, rel, pair) for m in range(micros)]

    def second_in(rel, pair, ref):
        group = [columns_in(rel, 0), columns_in(rel, 1)]
        for m in range(micros):
            group = group + [inner_in(m, rel, ref), gate_in(m, rel, pair)]
        return group

    tokens_in = [
        pltpu.make_async_copy(x_i, x, sems.at[9, 0]),
        pltpu.make_async_copy(c_i, c, sems.at[9, 1]),
    ]
    for rel in range(4):
        for copy in first_in(rel, pairs[rel]):
            copy.start()
    for rel in range(4):
        for copy in second_in(rel, pairs[rel], inners[rel]):
            copy.start()
    for copy in tokens_in:
        copy.start()
    acc[...] = jnp.zeros_like(acc)
    for rel in range(4):
        for copy in first_in(rel, pairs[0]):
            copy.wait()
    mix[...] = mm(brs[...], downs[...])

    def one(rel, none):
        at = pl.ds(pl.multiple_of(2 * rel * width, 2 * width), 2 * width)
        for copy in second_in(rel, pairs[0], inners[0]):
            copy.wait()
        acc[...] += nt(dup[:, at], ups[:, at])
        return none

    lax.fori_loop(0, 4, one, 0)
    for copy in tokens_in:
        copy.wait()
    step = 128

    def finish(at, none):
        m, r = at // (rows // step), pl.multiple_of(at % (rows // step) * step, step)
        here, both = pl.ds(r, step), pl.ds(pl.multiple_of(at * step, step), step)
        stream = x[m, here, :].astype(F32)
        pos = (sc[1] * 4 + h) * rows + r + iota((step, 1), 0)
        valid = (seg_of(pos, sc, seqs, m) < seqs).astype(F32)
        out_o[m, here, :] = (stream + valid * mix[both, :]).astype(BF)
        centred = stream - jnp.mean(stream, axis=-1, keepdims=True)
        rstd = lax.rsqrt(jnp.mean(centred * centred, axis=-1, keepdims=True) + EPS)
        exact = centred * rstd
        d_n = acc[both, :] * gain[...]
        along = jnp.mean(d_n * exact, axis=-1, keepdims=True)
        d_x = rstd * (d_n - jnp.mean(d_n, axis=-1, keepdims=True) - exact * along)
        back_o[m, here, :] = (c[m, here, :].astype(F32) + d_x).astype(BF)
        return none

    lax.fori_loop(0, micros * rows // step, finish, 0)


def table_kernel(
    sc, t0, t1, t2, t3, gate_o, wq_o, wk_o, wv_o, cw_o, cb_o, gn_o, sk_o, ln_o, ib_o, fb_o, small
):
    heads, _, width = small.shape
    blocks = width // 4
    for rel, ref in enumerate((t0, t1, t2, t3)):
        small[sc[0] ^ rel, 0 : SMALL // 2, :] = ref[:, 0:width]
        small[sc[0] ^ rel, SMALL // 2 :, :] = ref[:, width:]
    for h in range(heads):
        at = slice(h * width, (h + 1) * width)
        for part in range(3):
            start = (part * heads + h) * width
            gate_o[:, start : start + width] = small[h, 8 * part : 8 * part + 8, :]
        cw_o[:, at] = small[h, 36:40, :]
        for row, ref in ((40, cb_o), (41, gn_o), (42, sk_o)):
            ref[at] = small[h, row, :]
    for at, ref in enumerate((wq_o, wk_o, wv_o)):
        rows = slice(24 + 4 * at, 28 + 4 * at)
        for i in range(4):
            lanes = slice(i * blocks, (i + 1) * blocks)
            ref[i] = jnp.concatenate([small[h, rows, lanes] for h in range(heads)], axis=1)
    for half in range(2):
        ln_o[half * width : (half + 1) * width] = sum(small[h, 43 + half, :] for h in range(heads))
    ib_o[...] = small[0, 45, 0:4]
    fb_o[...] = small[0, 45, 4:8]


def whole(shape):
    return pl.BlockSpec(shape, lambda i, sc: (0,) * len(shape))


def by_chunk(rows, width):
    return pl.BlockSpec((rows, width), lambda i, sc: (i, 0))


def head_cols(rows, width, skip=0):
    return pl.BlockSpec((rows, width), lambda i, sc: (0, sc[0] + skip))


def head_rows(rows, width, skip=0):
    return pl.BlockSpec((rows, width), lambda i, sc: (sc[0] + skip, 0))


def of_micro(m, *shape):
    rest = (0,) * len(shape)
    return pl.BlockSpec((None,) + shape, lambda i, sc: (i if m is None else m,) + rest)


def micro_chunk(m, rows, width):
    return pl.BlockSpec((None, rows, width), lambda i, sc: (m, i, 0))


def micro_lanes(m, rows):
    return pl.BlockSpec((None, 8, rows), lambda i, sc: (m, 0, i))


def call(body, grid, in_specs, out_specs, out_shape, scratch, micros_us, args, aliases=None):
    return pl.pallas_call(
        body,
        grid_spec=pltpu.PrefetchScalarGridSpec(
            num_scalar_prefetch=1,
            grid=grid,
            in_specs=in_specs,
            out_specs=out_specs,
            scratch_shapes=scratch,
        ),
        out_shape=[jax.ShapeDtypeStruct(shape, dtype) for shape, dtype in out_shape],
        compiler_params=pltpu.CompilerParams(vmem_limit_bytes=VMEM_BYTES),
        cost_estimate=pl.CostEstimate(
            flops=int(micros_us * 0.05 * 1.15e9), bytes_accessed=1_000_000, transcendentals=0
        ),
        input_output_aliases=aliases or {},
    )(*args)


def together(*groups):
    flat = iter(lax.optimization_barrier([part for group in groups for part in group]))
    return [[next(flat) for _ in group] for group in groups]


def after(value, *others):
    return lax.optimization_barrier((value, *others))[0]


def per_device(
    tokens, lengths, ln_gain, w_up, conv_w, conv_b, w_q, w_k, w_v, gate_w, i_bias, f_bias,
    gn_gain, skip, w_down, cotangent,
):
    micros, rows, dim = tokens.shape
    inner = w_down.shape[0]
    heads = i_bias.shape[0]
    width = inner // heads
    seqs = lengths.shape[2]
    dp, sq, hd = lax.axis_size("dp"), lax.axis_size("seq"), lax.axis_size("head")
    assert hd == heads == 4 and sq == 2 and micros == 2 and conv_w.shape[0] == 4
    ranks = dp * sq
    every = ranks * hd
    span = rows * hd
    h, s = lax.axis_index("head"), lax.axis_index("seq")
    ends = jnp.cumsum(lengths[:, 0], axis=1).astype(jnp.int32)
    sc = jnp.concatenate([jnp.stack([h, s]).astype(jnp.int32), ends.reshape(-1)])

    def across(value, rel):
        return lax.ppermute(value, "head", [(at, at ^ rel) for at in range(hd)])

    def exchange(parts):
        return [parts[0]] + [across(parts[rel], rel) for rel in range(1, hd)]

    def gather(value):
        return exchange([value] * hd)

    x_near = [across(tokens, 1), across(tokens, 2)]

    place = s * span + jnp.arange(span, dtype=jnp.int32)[None, :, None]
    past = place >= ends[:, None, :]
    age = place[..., 0] - jnp.max(jnp.where(past, ends[:, None, :], 0), axis=2)
    left = jnp.min(jnp.where(past, 1 << 20, ends[:, None, :]), axis=2) - 1 - place[..., 0]
    marks = jnp.stack([age, left] + [jnp.zeros_like(age)] * 6, axis=1).astype(F32)
    gain = ln_gain.reshape(1, dim)
    cb, gn, sk = conv_b.reshape(1, inner), gn_gain.reshape(1, inner), skip.reshape(1, inner)
    gate_t = gate_w.T

    r, c = jnp.arange(width)[:, None], jnp.arange(width)[None, :]
    on = r // 4 == c // 4
    on_map = on.astype(F32)
    to_lanes = (c == r % 4 * (width // 4) + r // 4).astype(BF)

    def spread(weight):
        mine = lax.dynamic_slice_in_dim(weight, h * (width // 4), width // 4, 0).reshape(width, 4)
        return jnp.where(on, jnp.tile(mine, (1, width // 4)), 0).astype(BF)

    wq, wk, wv = spread(w_q), spread(w_k), spread(w_v)
    consts = [sc, marks, gain, cb, gn, sk, gate_t, wq, wk, wv, on_map, to_lanes]
    x_near, consts = together(x_near, consts)
    sc, marks, gain, cb, gn, sk, gate_t, wq, wk, wv, on_map, to_lanes = consts
    x_far = [across(x_near[0][0], 2), across(x_near[1][1], 1)]
    x_parts, x_far = together([tokens, *x_near], x_far)
    tails = [part[:, rows - EDGE :] for part in x_parts]
    tails.append(jnp.stack([part[rows - EDGE :] for part in x_far]))
    tail = tails[0]
    for rel in range(1, hd):
        tail = jnp.where(h == (hd - 1) ^ rel, tails[rel], tail)
    x_halo = lax.ppermute(tail, "seq", [(0, 1)])
    cot = after(cotangent, *x_far)
    c_parts = [cot, across(cot, 1), across(cot, 2)]

    sq_spec = whole((width, width))
    tiles = pltpu.VMEM((width // LANES, rows + EDGE, LANES), F32)
    dma = pltpu.SemaphoreType.DMA
    gate_specs = [head_cols(8, width, part * heads) for part in range(3)]
    conv_specs = [head_cols(4, width), head_cols(1, width)]
    anywhere = pl.BlockSpec(memory_space=pl.ANY)
    held = pl.BlockSpec(memory_space=pltpu.VMEM)

    bf_span, f_span = ((micros, span, width), BF), ((micros, span, width), F32)
    block = whole((rows, width))
    big = whole((width, dim))
    lanes = (micros, 8, span)
    def chunked(rows, width):
        return pl.BlockSpec((None, rows, width), lambda i, sc: (i // hd, i % hd, 0))

    def of_step(*shape):
        rest = (0,) * len(shape)
        return pl.BlockSpec((None,) + shape, lambda i, sc: (i // hd,) + rest)

    chunk_lanes = pl.BlockSpec((None, 8, rows), lambda i, sc: (i // hd, 0, i % hd))
    front = call(
        front_kernel,
        (micros * hd,),
        [of_step(rows, dim)] * 3
        + [whole((rows, dim))] * 2
        + [
            of_step(EDGE, dim), chunk_lanes, whole((1, dim)), head_cols(dim, width),
            head_cols(dim, width, heads), *conv_specs,
        ]
        + [sq_spec] * 3
        + gate_specs,
        [
            chunked(rows, dim), chunked(rows, width),
            pl.BlockSpec((None, 5, rows, width), lambda i, sc: (i // hd, 0, i % hd, 0)),
            of_step(EDGE, width), chunk_lanes,
        ],
        [
            ((micros, span, dim), BF), f_span, ((micros, 5, span, width), BF),
            ((micros, EDGE, width), BF), (lanes, F32),
        ],
        [pltpu.VMEM((rows, dim), BF), tiles],
        20,
        [
            sc, *x_parts, *x_far, x_halo, marks, gain, w_up, w_up, conv_w, cb, wq, wk, wv, gate_t,
            gate_t, gate_t,
        ],
    )
    front, c_parts = together(front, c_parts)
    normed, gz, five, halo, gate_terms = front
    gates = exchange([gate_terms] * hd)
    def of_five(at, count):
        return pl.BlockSpec((None, None, count, width), lambda i, sc: (i, at, 0, 0))

    lane_spec = of_micro(None, 8, span)
    state_spec = of_micro(None, width, width)
    gates, onward = together(gates, [c_parts[1][0], c_parts[2][1]])
    c_parts = c_parts + [across(onward[0], 2), across(onward[1], 1)]
    state = call(
        partial(gates_kernel, seqs),
        (micros,),
        [pl.BlockSpec(memory_space=pltpu.SMEM)] * 2 + [lane_spec] + [held] * 3 + [of_five(1, span), of_five(2, span)],
        [lane_spec, state_spec],
        [(lanes, F32), ((micros, width, width), F32)],
        [],
        7,
        [sc, i_bias, f_bias, *gates, five, five],
    )
    state, c_parts = together(state, c_parts)
    rows_t, states = state
    states_in = lax.ppermute(states, "seq", [(0, 1)])

    half_w = inner // every
    *pairs, gd, gg, both, four, d_states, small_mix, sums = call(
        mix_kernel,
        (1,),
        [whole(lanes), held, head_cols(1, width), head_cols(1, width)]
        + [anywhere] * 9,
        [anywhere] * 8 + [whole((micros, width, width)), whole((8, width)), whole(lanes)],
        [((2 * micros, rows, width), BF)] * 4
        + [((width, dim), BF)] * 2
        + [
            ((ranks, 2 * half_w, dim), BF), ((micros, 4, span, width), F32), ((micros, width, width), F32), ((8, width), F32),
            (lanes, F32),
        ],
        [
            pltpu.VMEM((micros, 4, span, width), BF),
            pltpu.VMEM((micros, span, width), F32),
            pltpu.VMEM((micros, span, dim), BF),
            pltpu.VMEM((micros, hd, rows, dim), BF),
            pltpu.VMEM((width, dim), BF),
            pltpu.VMEM((hd, 2 * micros, rows, width), BF),
            pltpu.VMEM((micros, 4, span, width), F32),
            pltpu.VMEM((width, dim), F32),
            pltpu.VMEM((width, dim), F32),
            pltpu.VMEM((2, width, dim), BF),
            pltpu.VMEM((rows, width), F32),
            pltpu.VMEM((hd // 2, rows, 2 * rows), BF),
            pltpu.VMEM((hd // 2, rows, 2 * rows), F32),
            pltpu.VMEM((rows, 2 * width), BF),
            pltpu.VMEM((span, 2 * width), BF),
            pltpu.VMEM((rows, 2 * width), BF),
            pltpu.VMEM((rows, width), F32),
            dma((micros, 6, 4)),
            dma((micros, 5, 4)),
            dma((2, ranks)),
        ],
        45,
        [sc, rows_t, states_in, gn, sk, five, gz, normed, *c_parts, w_down],
    )
    d_states = lax.ppermute(d_states, "seq", [(1, 0)])
    d_gates = call(
        gates_back_kernel,
        (micros,),
        [of_five(1, span), of_five(2, span), lane_spec, lane_spec, held],
        [lane_spec],
        [(lanes, F32)],
        [],
        8,
        [sc, five, five, rows_t, sums, d_states],
    )[0]
    d_gates = exchange([d_gates] * hd)

    if half_w % EDGE:
        both = [gg.reshape(ranks, half_w, dim), gd.reshape(ranks, half_w, dim)]
        both = jnp.concatenate(both, axis=1)
    early = lax.all_to_all(both, ("dp", "seq"), split_axis=0, concat_axis=0, tiled=True)
    pairs = exchange([after(part, *d_gates) for part in pairs])

    top = of_micro(None, EDGE, width)

    def of_four(at):
        return pl.BlockSpec((None, None, EDGE, width), lambda i, sc: (i, at, 0, 0))

    edges = call(
        edge_kernel,
        (micros,),
        [of_four(0), of_four(1)]
        + [whole(lanes)]
        + [held] * 3
        + [of_five(4, EDGE), top, of_micro(None, 8, 128), of_four(3)]
        + gate_specs[:2]
        + [sq_spec, sq_spec, *conv_specs],
        [top],
        [((micros, EDGE, width), F32)],
        [pltpu.VMEM((width // LANES, 2 * EDGE, LANES), F32)],
        4,
        [sc, four, four, *d_gates, five, halo, marks, four, gate_t, gate_t, wq, wk, conv_w, cb],
    )[0]
    edges = lax.ppermute(edges, "seq", [(1, 0)])
    axes = ("dp", "seq", "head")
    *d_inners, late = call(
        front_back_kernel,
        (1,),
        [whole(lanes)]
        + [held] * 3
        + [whole(lanes)] * 2
        + [held, whole((micros, EDGE, width)), whole((8, width)), held]
        + gate_specs
        + [sq_spec] * 3
        + conv_specs
        + [whole((1, dim))]
        + [anywhere] * 7,
        [anywhere] * 4 + [whole((width + SMALL // 2, dim))],
        [((micros, rows, width), BF)] * 4 + [((width + SMALL // 2, dim), F32)],
        [
            pltpu.VMEM((micros, 4, span, width), F32),
            pltpu.VMEM((micros, 5, span, width), BF),
            pltpu.VMEM((micros, span, dim), BF),
            pltpu.VMEM((micros, hd, EDGE, width), BF),
            pltpu.VMEM((dim, 2 * width), BF),
            pltpu.VMEM((micros, hd, rows, width), BF),
            tiles,
            tiles,
            pltpu.VMEM((rows, 6 * width), BF),
            *[pltpu.VMEM((width, width), F32)] * 3,
            pltpu.VMEM((rows, width), F32),
            pltpu.VMEM((width, dim), F32),
            pltpu.VMEM((width, width), F32),
            pltpu.VMEM((width, width), BF),
            pltpu.VMEM((width, dim), BF),
            pltpu.VMEM((SMALL, width), F32),
            dma((micros, 5, 4)),
            dma((micros, 4)),
        ],
        28,
        [
            sc, *d_gates, rows_t, marks, d_states, halo, small_mix, edges, gate_t, gate_t, gate_t,
            wq, wk, wv, conv_w, cb, gain, on_map, to_lanes, four, five, normed, gg, w_up,
        ],
    )
    (late, *d_inners), pairs = together([late, *d_inners], pairs)
    d_inners = exchange(d_inners)

    late = late + lax.ppermute(late, "seq", [(0, 1), (1, 0)])
    small = late[width:]
    blocks = late[:width].reshape(dp, 2 * half_w, dim)
    d = lax.axis_index("dp")
    if dp == 4 and SMALL <= 2 * half_w:
        high = lax.reduce_precision(small, 8, 7)
        table = jnp.concatenate([high.astype(BF), (small - high).astype(BF)], axis=0)
        table = jnp.pad(table, ((0, 2 * half_w - SMALL), (0, 0)))

        def to_plane(rel):
            block = lax.dynamic_index_in_dim(blocks, d ^ rel, 0, keepdims=False).astype(BF)
            block = jnp.where(s == 1, block, table)
            return lax.ppermute(block, "dp", [(a, a ^ rel) for a in range(dp)]) if rel else block

        terms = [to_plane(rel).astype(F32) for rel in range(dp)]
        g_inner = (terms[0] + terms[1]) + (terms[2] + terms[3])
        small = g_inner[: SMALL // 2] + g_inner[SMALL // 2 : SMALL]
        small = jnp.where(s == 0, small, lax.ppermute(small, "seq", [(0, 1)]))
    else:
        small = lax.psum(small, "dp")
        terms = lax.all_to_all(blocks.astype(BF), "dp", split_axis=0, concat_axis=0, tiled=True)
        g_inner = jnp.sum(terms.astype(F32), axis=0)
    early = jnp.sum(early.astype(F32), axis=0)
    g_gate, g_down = early[:half_w], early[half_w:]
    g_gate = jnp.concatenate([g_gate, lax.ppermute(g_gate, "seq", [(1, 0)])], axis=0)
    up_pairs, down_pairs = [], []
    for rank in range(ranks):
        for at in range(hd):
            block_at = at * dp + rank // 2 + (0 if rank % 2 else every // 2)
            up_pairs.append((rank * hd + at, block_at))
            down_pairs.append((rank * hd + at, at * ranks + rank))
    g_down = lax.ppermute(g_down, axes, down_pairs)
    g_up = jnp.where(s == 0, g_gate, g_inner)
    d_inners, (small, g_up) = together(d_inners, [small, g_up])
    g_up = lax.ppermute(g_up, axes, up_pairs).T

    token_spec = whole(tokens.shape)
    block_out, d_tokens = call(
        partial(tokens_kernel, seqs),
        (1,),
        [whole((1, dim))] + [anywhere] * 12,
        [token_spec] * 2,
        [(tokens.shape, BF)] * 2,
        [
            pltpu.VMEM(tokens.shape, BF),
            pltpu.VMEM(tokens.shape, BF),
            pltpu.VMEM((dim, 2 * inner), BF),
            pltpu.VMEM((inner, dim), BF),
            pltpu.VMEM((micros * rows, dim), F32),
            pltpu.VMEM((micros * rows, dim), F32),
            pltpu.VMEM((micros * rows, 2 * inner), BF),
            pltpu.VMEM((micros * rows, inner), BF),
            dma((10, hd)),
        ],
        100,
        [sc, gain, tokens, cotangent, *pairs, *d_inners, w_up, w_down],
    )

    (block_out, d_tokens), (small,) = together([block_out, d_tokens], [small])
    table = gather(small)
    flat = [((8, 3 * inner), F32), *[((4, 4, inner // 4), F32)] * 3, ((4, inner), F32)]
    flat = flat + [((inner,), F32)] * 3 + [((dim,), F32)] + [((heads,), F32)] * 2
    g_gate, g_wq, g_wk, g_wv, g_cw, g_cb, g_gn, g_sk, g_ln, g_ib, g_fb = call(
        table_kernel,
        (1,),
        [whole(small.shape)] + [held] * 3,
        [whole(shape) for shape, _ in flat],
        flat,
        [pltpu.VMEM((hd, SMALL, width), F32)],
        3,
        [sc, *table],
    )
    maps = [part.transpose(2, 0, 1) for part in (g_wq, g_wk, g_wv)]
    return (
        block_out, d_tokens, g_ln, g_up, g_cw, g_cb, *maps, g_gate.T, g_ib, g_fb, g_gn, g_sk, g_down,
    )


def solution(mesh):
    rows = P(None, ("dp", "seq", "head"), None)
    placed = (rows, P(None, "dp", None), *[P()] * 13, rows)
    outs = (rows, rows, P(), P(None, ("dp", "seq", "head")), *[P()] * 10, P(("dp", "seq", "head"), None))
    return jax.shard_map(per_device, mesh=mesh, in_specs=placed, out_specs=outs, check_vma=False)
```
